128 devices in a mesh: pipe: 4 (over x), ctx: 32 (over z, y, core).
Axes of the slice: x: 4, y: 4, z: 4, core: 2. Of those that a mesh axis runs over, the one named last changes fastest.
Arguments:
- incoming: bfloat16 [4, 8192, 8192], P('pipe', 'ctx'), may hold values from -6 to 6
- norm_gain: float32 [4, 8192], P('pipe'), may hold values from 0.5 to 1.5
- proj_state: bfloat16 [4, 8192, 256], P('pipe'), may hold values from -0.015625 to 0.015625
- proj_step: bfloat16 [4, 8192, 128], P('pipe'), may hold values from -0.0625 to 0.0625
- conv_weight: float32 [4, 4, 8192], P('pipe'), may hold values from -3 to 3
- decay_rate: float32 [4, 128], P('pipe'), may hold values from 2.4414063e-05 to 0.05
- step_bias: float32 [4, 128], P('pipe'), may hold values from -2 to 1
- skip_gain: float32 [4, 128], P('pipe'), may hold values from 0.5 to 2
- out_gain: float32 [4, 8192], P('pipe'), may hold values from 0.5 to 1.5
Outputs:
- passed: bfloat16 [4, 8192, 8192], P('pipe', 'ctx')
The draws below stay inside these ranges and needn't reach their ends.
All inputs are finite; a program needn't handle non-finite values.
Results may differ from the reference program's by a relative error of at most 0.0071.
Values may be sent and summed in bfloat16 or wider, within the bound.
A program may use at most 320 MiB of HBM per device.

```python
import math
import jax
import jax.numpy as jnp
from jax import lax

D = 8192
H = 128
P_SIZE = 64
N = 128
GROUP = 256
CONV = 4
TOKENS = 8192
N_PIPE = 4


def level_of(own_key, extent, shards, smallest, largest):
    factor_of, own = 1.0, jax.random.fold_in(own_key, 6)
    for axis_at, parts in shards:
        heights = jnp.exp(jax.random.uniform(jax.random.fold_in(own, axis_at), (parts,), jnp.float32, smallest / len(shards), largest / len(shards)))
        factor_of = factor_of * jnp.repeat(heights, extent[axis_at] // parts).reshape([-1 if axis == axis_at else 1 for axis in range(len(extent))])
    return factor_of


def scatter_about(stream_key, extent, scale, most, shards=(), kind=jnp.bfloat16):
    drawn = jax.random.normal(stream_key, extent, jnp.float32) * scale
    if len(shards) > 0:
        drawn = level_of(stream_key, extent, shards, -0.22, 0.18) * drawn
    return jnp.clip(drawn, min=-most, max=most).astype(kind)


def setup_inputs(seed: int = 0) -> dict:
    key_list = jax.random.split(jax.random.key(seed), 10)
    incoming = scatter_about(key_list[0], (N_PIPE, TOKENS, D), 1.0, 6.0, ((0, 4), (1, 32)))
    norm_gain = jnp.clip(0.5 + 1.0 * jax.random.uniform(key_list[1], (N_PIPE, D), jnp.float32) ** level_of(key_list[1], (N_PIPE, D), ((0, 4),), -0.2, 0.2), 0.5, 1.5)
    proj_state = scatter_about(key_list[2], (N_PIPE, D, 2 * N), (16 * D) ** -0.5, 0.015625, ((0, 4),))
    proj_step = scatter_about(key_list[3], (N_PIPE, D, H), D ** -0.5, 0.0625, ((0, 4),))
    conv_weight = scatter_about(key_list[4], (N_PIPE, CONV, D), CONV ** -0.5, 3.0, ((0, 4),), jnp.float32)
    decay_rate = jnp.clip(jnp.exp(math.log(0.05) - 7.624619 * jax.random.uniform(key_list[5], (N_PIPE, H), jnp.float32) ** level_of(key_list[5], (N_PIPE, H), ((0, 4),), -0.2, 0.2)), 2.441406286379788e-05, 0.05)
    step_bias = jnp.clip(-2.0 + 3.0 * jax.random.uniform(key_list[6], (N_PIPE, H), jnp.float32) ** level_of(key_list[6], (N_PIPE, H), ((0, 4),), -0.2, 0.2), -2.0, 1.0)
    skip_gain = jnp.clip(0.5 + 1.5 * jax.random.uniform(key_list[7], (N_PIPE, H), jnp.float32) ** level_of(key_list[7], (N_PIPE, H), ((0, 4),), -0.2, 0.2), 0.5, 2.0)
    out_gain = jnp.clip(0.5 + 1.0 * jax.random.uniform(key_list[8], (N_PIPE, D), jnp.float32) ** level_of(key_list[8], (N_PIPE, D), ((0, 4),), -0.2, 0.2), 0.5, 1.5)
    return {"incoming": incoming, "norm_gain": norm_gain, "proj_state": proj_state, "proj_step": proj_step, "conv_weight": conv_weight, "decay_rate": decay_rate, "step_bias": step_bias, "skip_gain": skip_gain, "out_gain": out_gain}


epsilon = 1e-05
highest = lax.Precision.HIGHEST

def normalize(values_in, gain_row):
    values = values_in.astype(jnp.float32)
    meansq = lax.optimization_barrier(jnp.mean(values * values, axis=-1, keepdims=True))
    return (values * lax.rsqrt(meansq + epsilon) * gain_row).astype(jnp.bfloat16)

def run_layer(stream, norm_row, state_weight, step_weight, conv_taps, decay_rates, biases, skip_row, out_row):
    normed = normalize(stream, norm_row)
    projected = jnp.dot(normed, state_weight, preferred_element_type=jnp.float32)
    write_proj = projected[:, :N].astype(jnp.bfloat16)
    read_proj = projected[:, N:].astype(jnp.bfloat16)
    step_size = jax.nn.softplus(jnp.dot(normed, step_weight, preferred_element_type=jnp.float32) + biases)
    padded = jnp.concatenate([jnp.zeros((CONV - 1, D), jnp.float32), normed.astype(jnp.float32)], axis=0)
    conv_sum = conv_taps[0] * padded[0:TOKENS]
    for tap_id in range(1, CONV):
        conv_sum = conv_sum + conv_taps[tap_id] * padded[tap_id:tap_id + TOKENS]
    inner_act = jax.nn.silu(conv_sum).astype(jnp.bfloat16).reshape(TOKENS, H, P_SIZE)
    log_decay = -step_size * decay_rates
    group_count = TOKENS // GROUP
    lower_mask = (jnp.arange(GROUP)[:, None] >= jnp.arange(GROUP)[None, :]).astype(jnp.float32)

    def advance(state_now, pieces):
        inner_k, write_k, read_k, step_k, decay_k, stream_k = pieces
        cumulative = jnp.dot(lower_mask, decay_k, precision=highest)
        scores = jnp.dot(read_k, write_k.T, preferred_element_type=jnp.float32)
        cumul_heads = cumulative.T
        spread = cumul_heads[:, :, None] - cumul_heads[:, None, :]
        damping = jnp.exp(jnp.where(lower_mask[None] > 0, spread, -1e+30))
        mixing = (scores[None] * damping * step_k.T[:, None, :]).astype(jnp.bfloat16)
        within = jnp.einsum('hts,shp->thp', mixing.astype(jnp.float32), inner_k.astype(jnp.float32), precision=highest)
        carried_in = jnp.exp(cumulative)[:, :, None] * jnp.einsum('tn,hpn->thp', read_k.astype(jnp.float32), state_now, precision=highest)
        closing = cumulative[GROUP - 1]
        weights = jnp.exp(closing[None, :] - cumulative) * step_k
        weighted = (inner_k.astype(jnp.float32) * weights[:, :, None]).astype(jnp.bfloat16)
        fresh_state = jnp.einsum('shp,sn->hpn', weighted.astype(jnp.float32), write_k.astype(jnp.float32), precision=highest)
        new_state = jnp.exp(closing)[:, None, None] * state_now + fresh_state
        output = within + carried_in + skip_row[None, :, None] * inner_k.astype(jnp.float32)
        meansq = lax.optimization_barrier(jnp.mean(output * output, axis=-1, keepdims=True))
        normed_out = (output * lax.rsqrt(meansq + epsilon)).reshape(GROUP, D)
        mixed_rows = (stream_k.astype(jnp.float32) + normed_out * out_row).astype(jnp.bfloat16)
        return (new_state, mixed_rows)
    pieces = (inner_act.reshape(group_count, GROUP, H, P_SIZE), write_proj.reshape(group_count, GROUP, N), read_proj.reshape(group_count, GROUP, N), step_size.reshape(group_count, GROUP, H), log_decay.reshape(group_count, GROUP, H), stream.reshape(group_count, GROUP, D))
    final_state, mixed_rows = lax.scan(advance, jnp.zeros((H, P_SIZE, N), jnp.float32), pieces)
    return mixed_rows.reshape(TOKENS, D)

def reference(incoming, norm_gain, proj_state, proj_step, conv_weight, decay_rate, step_bias, skip_gain, out_gain):
    results = []
    for section in range(N_PIPE):
        results.append(run_layer(incoming[section], norm_gain[section], proj_state[section], proj_step[section], conv_weight[section], decay_rate[section], step_bias[section], skip_gain[section], out_gain[section]))
    return jnp.stack([results[(section - 1) % N_PIPE] for section in range(N_PIPE)], axis=0)
```

```python
import functools

import jax
import jax.numpy as jnp
from jax import lax
from jax.experimental import pallas as pl
from jax.experimental.pallas import tpu as pltpu
from jax.sharding import PartitionSpec as P

MESH = pl.DeviceIdType.MESH
F32 = jnp.float32
BF16 = jnp.bfloat16

ROWS = 256
STATE = 128
HEADS = 128
HEAD = 64
CONV = 4
HALO = 8
TILE = 512
CHIPS = 16
LOG2E = 1.4426950408889634
epsilon = 1e-05
VMEM_LIMIT = 56 * 1024 * 1024

HEADS_HOME = 64
HEADS_AWAY = HEADS - HEADS_HOME


def dot(a, b):
    return jnp.dot(a, b, preferred_element_type=F32)


def two_parts(x):
    high = x.astype(BF16)
    low = (x - high.astype(F32)).astype(BF16)
    return jnp.concatenate([high, low], axis=-1)


def spreader(first_head, width):
    head = lax.broadcasted_iota(jnp.int32, (HEADS, width), 0)
    feature = lax.broadcasted_iota(jnp.int32, (HEADS, width), 1)
    one = (head == first_head + feature // HEAD).astype(F32).astype(BF16)
    return jnp.concatenate([one, one], axis=0)


def project_kernel(x_ref, ws_ref, wt_ref, gain_ref, bias_ref, write_ref, read_ref, step_ref, scale_ref, acc):
    at = pl.program_id(0)
    width = ws_ref.shape[0]

    @pl.when(at == 0)
    def _():
        total = jnp.zeros((ROWS, 128), F32)
        for i in range(x_ref.shape[1] // 512):
            part = x_ref[:, i * 512 : (i + 1) * 512].astype(F32)
            part = part * part
            total = total + (part[:, :128] + part[:, 128:256]) + (part[:, 256:384] + part[:, 384:])
        meansq = jnp.sum(total, axis=-1, keepdims=True) * (1.0 / x_ref.shape[1])
        scale_ref[...] = jnp.broadcast_to(lax.rsqrt(meansq + epsilon), (ROWS, 128))
        acc[...] = jnp.zeros_like(acc)

    columns = pl.ds(pl.multiple_of(at * width, width), width)
    scale = scale_ref[:, :1]
    normed = (x_ref[:, columns].astype(F32) * scale * gain_ref[...]).astype(BF16)
    acc[:, : 2 * STATE] += dot(normed, ws_ref[...])
    acc[:, 2 * STATE :] += dot(normed, wt_ref[...])

    @pl.when(at == pl.num_programs(0) - 1)
    def _():
        write_ref[...] = acc[:, :STATE].astype(BF16)
        read_ref[...] = acc[:, STATE : 2 * STATE].astype(BF16)
        step_ref[...] = jax.nn.softplus(acc[:, 2 * STATE :] + bias_ref[...])


def project(x, proj_state, proj_step, gain, bias):
    features = x.shape[1]
    width = 1024
    return pl.pallas_call(
        project_kernel,
        grid=(features // width,),
        in_specs=[
            pl.BlockSpec((ROWS, features), lambda i: (0, 0)),
            pl.BlockSpec((width, 2 * STATE), lambda i: (i, 0)),
            pl.BlockSpec((width, HEADS), lambda i: (i, 0)),
            pl.BlockSpec((1, width), lambda i: (0, i)),
            pl.BlockSpec((1, HEADS), lambda i: (0, 0)),
        ],
        out_specs=[
            pl.BlockSpec((ROWS, STATE), lambda i: (0, 0)),
            pl.BlockSpec((ROWS, STATE), lambda i: (0, 0)),
            pl.BlockSpec((ROWS, HEADS), lambda i: (0, 0)),
            pl.BlockSpec((ROWS, 128), lambda i: (0, 0)),
        ],
        out_shape=[
            jax.ShapeDtypeStruct((ROWS, STATE), BF16),
            jax.ShapeDtypeStruct((ROWS, STATE), BF16),
            jax.ShapeDtypeStruct((ROWS, HEADS), F32),
            jax.ShapeDtypeStruct((ROWS, 128), F32),
        ],
        scratch_shapes=[pltpu.VMEM((ROWS, 3 * STATE), F32)],
        compiler_params=pltpu.CompilerParams(
            dimension_semantics=("arbitrary",), vmem_limit_bytes=VMEM_LIMIT
        ),
        cost_estimate=pl.CostEstimate(
            flops=2 * ROWS * features * 3 * STATE, bytes_accessed=12 << 20, transcendentals=0
        ),
        name="project",
    )(x, proj_state, proj_step, gain, bias)


def decay_kernel(step_ref, rate_ref, cum_ref, closing_ref, weight_ref, enter_ref, step2_ref):
    step = step_ref[...]
    log_decay = -step * rate_ref[...]
    row = lax.broadcasted_iota(jnp.int32, (ROWS, ROWS), 0)
    column = lax.broadcasted_iota(jnp.int32, (ROWS, ROWS), 1)
    lower = (row >= column).astype(F32).astype(BF16)
    first = log_decay.astype(BF16)
    rest = log_decay - first.astype(F32)
    second = rest.astype(BF16)
    third = (rest - second.astype(F32)).astype(BF16)
    cumulative = dot(lower, third) + dot(lower, second) + dot(lower, first)
    closing = cumulative[ROWS - 1 :, :]
    cum_ref[...] = (cumulative * LOG2E).T
    closing_ref[...] = jnp.broadcast_to(closing, (8, HEADS))
    weight_ref[...] = two_parts(jnp.exp(closing - cumulative) * step)
    enter_ref[...] = two_parts(jnp.exp(cumulative))
    step2_ref[...] = two_parts(step)


def decays(step, rate):
    pair = jax.ShapeDtypeStruct((ROWS, 2 * HEADS), BF16)
    return pl.pallas_call(
        decay_kernel,
        out_shape=[
            jax.ShapeDtypeStruct((HEADS, ROWS), F32),
            jax.ShapeDtypeStruct((8, HEADS), F32),
            pair,
            pair,
            pair,
        ],
        compiler_params=pltpu.CompilerParams(vmem_limit_bytes=VMEM_LIMIT),
        cost_estimate=pl.CostEstimate(flops=1 << 26, bytes_accessed=1 << 20, transcendentals=1 << 17),
        name="decays",
    )(step, rate)


def fresh_kernel(first, x_ref, halo_ref, vec_ref, scale_ref, weight_ref, write_ref, inner_ref, fresh_ref, padded):
    at = pl.program_id(0)
    normed = (x_ref[...].astype(F32) * scale_ref[:, :1] * vec_ref[4:5, :]).astype(BF16)
    padded[HALO:, :] = normed.astype(F32)
    padded[:HALO, :] = halo_ref[...].astype(F32)
    conv = vec_ref[0:1, :] * padded[HALO - 3 : HALO - 3 + ROWS, :]
    for tap in range(1, CONV):
        conv = conv + vec_ref[tap : tap + 1, :] * padded[HALO - 3 + tap : HALO - 3 + tap + ROWS, :]
    inner = (conv * jax.nn.sigmoid(conv)).astype(BF16)
    inner_ref[...] = inner
    spread = spreader(first + at * (TILE // HEAD), TILE)
    weighted = (inner.astype(F32) * dot(weight_ref[...], spread)).astype(BF16)
    fresh_ref[...] = lax.dot_general(
        write_ref[...], weighted, (((0,), (0,)), ((), ())), preferred_element_type=F32
    ).astype(BF16)


def fresh_states(first, x, halo, vec, scale, weight, write):
    heads = vec.shape[1] // HEAD
    features = heads * HEAD
    return pl.pallas_call(
        functools.partial(fresh_kernel, first),
        grid=(features // TILE,),
        in_specs=[
            pl.BlockSpec((ROWS, TILE), lambda i: (0, i)),
            pl.BlockSpec((HALO, TILE), lambda i: (0, i)),
            pl.BlockSpec((vec.shape[0], TILE), lambda i: (0, i)),
            pl.BlockSpec((ROWS, 128), lambda i: (0, 0)),
            pl.BlockSpec((ROWS, 2 * HEADS), lambda i: (0, 0)),
            pl.BlockSpec((ROWS, STATE), lambda i: (0, 0)),
        ],
        out_specs=[
            pl.BlockSpec((ROWS, TILE), lambda i: (0, i)),
            pl.BlockSpec((STATE, TILE), lambda i: (0, i)),
        ],
        out_shape=[
            jax.ShapeDtypeStruct((ROWS, features), BF16),
            jax.ShapeDtypeStruct((STATE, features), BF16),
        ],
        scratch_shapes=[pltpu.VMEM((ROWS + HALO, TILE), F32)],
        compiler_params=pltpu.CompilerParams(
            dimension_semantics=("arbitrary",), vmem_limit_bytes=VMEM_LIMIT
        ),
        cost_estimate=pl.CostEstimate(
            flops=40 * ROWS * features, bytes_accessed=10 * ROWS * features, transcendentals=ROWS * features
        ),
        name="fresh",
    )(x, halo, vec, scale, weight, write)


def prefix_kernel(
    first,
    fresh_ref,
    closing_ref,
    out_ref,
    peer,
    peer_closing,
    total,
    total_closing,
    got,
    got_closing,
    before,
    entering,
    theirs,
    landed,
    pair_send,
    pair_recv,
    send1,
    recv1,
    send2,
    recv2,
    send3,
    recv3,
):
    features = fresh_ref.shape[1]
    half, quarter = features // 2, features // 4
    heads = features // HEAD
    me = lax.axis_index("ctx")
    core = lax.rem(me, 2)
    chip = me // 2
    partner = chip * 2 + (1 - core)

    def device(index):
        return {"ctx": index}

    def place(of):
        return (
            pl.ds(pl.multiple_of(lax.rem(of, 8) * 16, 16), 16),
            pl.ds(pl.multiple_of((of // 8) * quarter, 128), quarter),
        )

    barrier = pltpu.get_barrier_semaphore()
    pl.semaphore_signal(barrier, inc=1, device_id=device(partner), device_id_type=MESH)

    def greet(d, carry):
        other = lax.rem(chip + d, CHIPS) * 2 + core
        pl.semaphore_signal(barrier, inc=1, device_id=device(other), device_id_type=MESH)
        return carry

    lax.fori_loop(1, CHIPS, greet, 0)
    pl.semaphore_wait(barrier, CHIPS)

    mine_columns = pl.ds(pl.multiple_of(core * half, 128), half)
    other_columns = pl.ds(pl.multiple_of((1 - core) * half, 128), half)

    to_pair = pltpu.make_async_remote_copy(
        fresh_ref.at[:, other_columns], peer, pair_send.at[0], pair_recv.at[0], device(partner), MESH
    )
    to_pair_closing = pltpu.make_async_remote_copy(
        closing_ref, peer_closing, pair_send.at[1], pair_recv.at[1], device(partner), MESH
    )
    to_pair.start()
    to_pair_closing.start()
    to_pair.wait()
    to_pair_closing.wait()
    is_first = core == 0
    own = fresh_ref[:, mine_columns].astype(F32)
    other = peer[...].astype(F32)
    state0 = jnp.where(is_first, own, other)
    state1 = jnp.where(is_first, other, own)
    closing0 = jnp.where(is_first, closing_ref[...], peer_closing[...])
    closing1 = jnp.where(is_first, peer_closing[...], closing_ref[...])
    spread = spreader(first + core * (heads // 2), half)
    decay0 = dot(two_parts(jnp.exp(closing0)), spread)[0:1, :]
    decay1 = dot(two_parts(jnp.exp(closing1)), spread)[0:1, :]
    total[...] = (decay1 * state0 + state1).astype(BF16)
    total_closing[...] = closing0 + closing1

    def out1(d):
        to = lax.rem(chip + d, CHIPS)
        rows, columns = place(to)
        return pltpu.make_async_remote_copy(
            total.at[rows, columns], got.at[chip], send1.at[to], recv1.at[chip], device(to * 2 + core), MESH
        )

    def out2(d):
        to = lax.rem(chip + d, CHIPS)
        return pltpu.make_async_remote_copy(
            total_closing, got_closing.at[chip], send2.at[to], recv2.at[chip], device(to * 2 + core), MESH
        )

    def in1(d):
        of = lax.rem(chip + d, CHIPS)
        rows, columns = place(of)
        return pltpu.make_async_remote_copy(
            total.at[rows, columns], got.at[of], send1.at[of], recv1.at[of], device(of * 2 + core), MESH
        )

    def in2(d):
        of = lax.rem(chip + d, CHIPS)
        return pltpu.make_async_remote_copy(
            total_closing, got_closing.at[of], send2.at[of], recv2.at[of], device(of * 2 + core), MESH
        )

    def start12(d, carry):
        out2(d).start()
        out1(d).start()
        return carry

    def wait12(d, carry):
        in2(d).wait_recv()
        in1(d).wait_recv()
        out2(d).wait_send()
        out1(d).wait_send()
        return carry

    lax.fori_loop(1, CHIPS, start12, 0)
    rows, columns = place(chip)
    got[chip] = total[rows, columns]
    got_closing[chip] = total_closing[...]
    lax.fori_loop(1, CHIPS, wait12, 0)

    spread = spreader(first + core * (heads // 2) + (chip // 8) * (heads // 4), quarter)
    decays_all = dot(two_parts(jnp.exp(got_closing[:, 0, :])), spread)
    state = jnp.zeros((16, quarter), F32)
    for k in range(CHIPS):
        before[k] = state.astype(BF16)
        if k < CHIPS - 1:
            state = decays_all[k : k + 1, :] * state + got[k].astype(F32)

    def out3(d):
        to = lax.rem(chip + d, CHIPS)
        rows, columns = place(chip)
        return pltpu.make_async_remote_copy(
            before.at[to], entering.at[rows, columns], send3.at[to], recv3.at[chip], device(to * 2 + core), MESH
        )

    def in3(d):
        of = lax.rem(chip + d, CHIPS)
        rows, columns = place(of)
        return pltpu.make_async_remote_copy(
            before.at[of], entering.at[rows, columns], send3.at[of], recv3.at[of], device(of * 2 + core), MESH
        )

    def start3(d, carry):
        out3(d).start()
        return carry

    def wait3(d, carry):
        in3(d).wait_recv()
        out3(d).wait_send()
        return carry

    lax.fori_loop(1, CHIPS, start3, 0)
    entering[rows, columns] = before[chip]
    lax.fori_loop(1, CHIPS, wait3, 0)

    for_first = entering[...]
    for_second = (decay0 * for_first.astype(F32) + state0).astype(BF16)
    theirs[...] = jnp.where(is_first, for_second, for_first)
    back = pltpu.make_async_remote_copy(
        theirs, landed, pair_send.at[2], pair_recv.at[2], device(partner), MESH
    )
    back.start()
    out_ref[:, mine_columns] = jnp.where(is_first, for_first, for_second)
    back.wait()
    out_ref[:, other_columns] = landed[...]


def prefix(first, fresh, closing, collective_id):
    features = fresh.shape[1]
    half, quarter = features // 2, features // 4
    dma = pltpu.SemaphoreType.DMA
    return pl.pallas_call(
        functools.partial(prefix_kernel, first),
        out_shape=jax.ShapeDtypeStruct((STATE, features), BF16),
        in_specs=[pl.BlockSpec(memory_space=pltpu.VMEM)] * 2,
        out_specs=pl.BlockSpec(memory_space=pltpu.VMEM),
        scratch_shapes=[
            pltpu.VMEM((STATE, half), BF16),
            pltpu.VMEM((8, HEADS), F32),
            pltpu.VMEM((STATE, half), BF16),
            pltpu.VMEM((8, HEADS), F32),
            pltpu.VMEM((CHIPS, 16, quarter), BF16),
            pltpu.VMEM((CHIPS, 8, HEADS), F32),
            pltpu.VMEM((CHIPS, 16, quarter), BF16),
            pltpu.VMEM((STATE, half), BF16),
            pltpu.VMEM((STATE, half), BF16),
            pltpu.VMEM((STATE, half), BF16),
            dma((3,)),
            dma((3,)),
            dma((CHIPS,)),
            dma((CHIPS,)),
            dma((CHIPS,)),
            dma((CHIPS,)),
            dma((CHIPS,)),
            dma((CHIPS,)),
        ],
        compiler_params=pltpu.CompilerParams(
            collective_id=collective_id, has_side_effects=True, vmem_limit_bytes=VMEM_LIMIT
        ),
        cost_estimate=pl.CostEstimate(
            flops=STATE * features * 1000, bytes_accessed=STATE * features * 50, transcendentals=0
        ),
        name="prefix",
    )(fresh, closing)


def output_kernel(
    first,
    x_ref,
    inner_ref,
    state_ref,
    vec_ref,
    skip_ref,
    write_ref,
    read_ref,
    cum_ref,
    enter_ref,
    step2_ref,
    out_ref,
    scores,
):
    at = pl.program_id(0)

    @pl.when(at == 0)
    def _():
        row = lax.broadcasted_iota(jnp.int32, (ROWS, ROWS), 0)
        column = lax.broadcasted_iota(jnp.int32, (ROWS, ROWS), 1)
        product = lax.dot_general(
            read_ref[...], write_ref[...], (((1,), (1,)), ((), ())), preferred_element_type=F32
        )
        scores[...] = jnp.where(row >= column, product, 0.0)

    spread = spreader(first + at * (TILE // HEAD), TILE)
    inner = inner_ref[...].astype(F32)
    stepped = (inner * dot(step2_ref[...], spread)).astype(BF16)
    cum = cum_ref[...]
    cum_columns = cum.T
    top, bottom = scores[:128, :128], scores[128:, :]
    lane = lax.broadcasted_iota(jnp.int32, (ROWS, 128), 1)
    pieces = []
    for pair in range(TILE // 128):
        values = stepped[:, pair * 128 : (pair + 1) * 128]
        upper = lower = None
        for side in range(2):
            h = pair * 2 + side
            column = cum_columns[:, h : h + 1]
            row = cum[h : h + 1, :]
            own = jnp.where((lane >= HEAD) == (side == 1), values, jnp.zeros_like(values))
            mix0 = (jnp.exp2(jnp.minimum(column[:128] - row[:, :128], 0.0)) * top).astype(BF16)
            mix1 = (jnp.exp2(jnp.minimum(column[128:] - row, 0.0)) * bottom).astype(BF16)
            up, low = dot(mix0, own[:128]), dot(mix1, own)
            upper = up if upper is None else upper + up
            lower = low if lower is None else lower + low
        pieces.append(jnp.concatenate([upper, lower], axis=0))
    within = jnp.concatenate(pieces, axis=1)
    carried = dot(read_ref[...], state_ref[...]) * dot(enter_ref[...], spread)
    skip = dot(two_parts(jnp.broadcast_to(skip_ref[...], (8, HEADS))), spread)[0:1, :]
    output = within + carried + skip * inner
    square = (output * output).astype(BF16)
    a = lax.broadcasted_iota(jnp.int32, (256, 256), 0) // HEAD
    b = lax.broadcasted_iota(jnp.int32, (256, 256), 1) // HEAD
    group = (a == b).astype(F32).astype(BF16)
    sums = jnp.concatenate(
        [dot(square[:, i * 256 : (i + 1) * 256], group) for i in range(TILE // 256)], axis=1
    )
    normed = output * lax.rsqrt(sums * (1.0 / HEAD) + epsilon)
    out_ref[...] = (x_ref[...].astype(F32) + normed * vec_ref[5:6, :]).astype(BF16)


def outputs(first, x, inner, state, vec, skip, write, read, cum, enter, step2, place=0, width=None):
    features = inner.shape[1]
    width = features if width is None else width
    base = first * HEAD // TILE
    whole = lambda i: (0, 0)
    return pl.pallas_call(
        functools.partial(output_kernel, first),
        grid=(features // TILE,),
        in_specs=[
            pl.BlockSpec((ROWS, TILE), lambda i: (0, i)),
            pl.BlockSpec((ROWS, TILE), lambda i: (0, i)),
            pl.BlockSpec((STATE, TILE), lambda i: (0, i)),
            pl.BlockSpec((vec.shape[0], TILE), lambda i: (0, i)),
            pl.BlockSpec((1, HEADS), whole),
            pl.BlockSpec((ROWS, STATE), whole),
            pl.BlockSpec((ROWS, STATE), whole),
            pl.BlockSpec((TILE // HEAD, ROWS), lambda i: (base + i, 0)),
            pl.BlockSpec((ROWS, 2 * HEADS), whole),
            pl.BlockSpec((ROWS, 2 * HEADS), whole),
        ],
        out_specs=pl.BlockSpec((ROWS, TILE), lambda i: (0, place + i)),
        out_shape=jax.ShapeDtypeStruct((ROWS, width), BF16),
        scratch_shapes=[pltpu.VMEM((ROWS, ROWS), F32)],
        compiler_params=pltpu.CompilerParams(
            dimension_semantics=("arbitrary",), vmem_limit_bytes=VMEM_LIMIT
        ),
        cost_estimate=pl.CostEstimate(
            flops=1000 * ROWS * features, bytes_accessed=10 * ROWS * features, transcendentals=ROWS * features
        ),
        name="output",
    )(x, inner, state, vec, skip, write, read, cum, enter, step2)


def onward(array):
    peers = lax.axis_size("pipe")
    return lax.ppermute(array, "pipe", [(i, (i + 1) % peers) for i in range(peers)])


def normalize(values_in, gain_row):
    values = values_in.astype(F32)
    meansq = jnp.mean(values * values, axis=-1, keepdims=True)
    return (values * lax.rsqrt(meansq + epsilon) * gain_row).astype(BF16)


def shards(
    incoming, norm_gain, proj_state, proj_step, conv_weight, decay_rate, step_bias, skip_gain, out_gain
):
    x = incoming[0]
    features = x.shape[1]
    home = HEADS_HOME * HEAD
    tokens_peers = lax.axis_size("ctx")

    x_away = onward(x[:, home:])
    vec = jnp.concatenate([conv_weight[0], norm_gain, out_gain], axis=0)
    vec_away = onward(vec[:, home:])
    small_away = onward(jnp.concatenate([decay_rate, skip_gain], axis=0))

    edge = lax.ppermute(x[ROWS - HALO :], "ctx", [(i, i + 1) for i in range(tokens_peers - 1)])
    write, read, step, scale = project(x, proj_state[0], proj_step[0], norm_gain, step_bias)
    halo = normalize(edge, norm_gain[0])
    halo_away = onward(halo[:, home:])
    maps_away = onward(jnp.concatenate([write, read], axis=1))
    step_away = onward(jnp.concatenate([step, scale], axis=1))

    cum, closing, weight, enter, step2 = decays(step, decay_rate)
    inner, fresh = fresh_states(0, x, halo, vec[:, :home], scale, weight, write)
    state = prefix(0, fresh, closing, 0)
    rows = outputs(0, x, inner, state, vec, skip_gain, write, read, cum, enter, step2)
    rows_in = onward(rows)

    write, read = maps_away[:, :STATE], maps_away[:, STATE:]
    step, scale = step_away[:, :HEADS], step_away[:, HEADS:]
    cum, closing, weight, enter, step2 = decays(step, small_away[0:1])
    inner, fresh = fresh_states(HEADS_HOME, x_away, halo_away, vec_away, scale, weight, write)
    state = prefix(HEADS_HOME, fresh, closing, 1)
    passed = outputs(
        HEADS_HOME, x_away, inner, state, vec_away, small_away[1:2], write, read, cum, enter, step2,
        place=home // TILE, width=features,
    )
    passed = lax.dynamic_update_slice(passed, rows_in, (0, 0))
    return passed[None]


def solution(mesh):
    return jax.shard_map(
        shards,
        mesh=mesh,
        in_specs=(
            P("pipe", "ctx", None),
            P("pipe", None),
            P("pipe", None, None),
            P("pipe", None, None),
            P("pipe", None, None),
            P("pipe", None),
            P("pipe", None),
            P("pipe", None),
            P("pipe", None),
        ),
        out_specs=P("pipe", "ctx", None),
        check_vma=False,
    )
```

```python
import functools

import jax
import jax.numpy as jnp
from jax import lax
from jax.experimental import pallas as pl
from jax.experimental.pallas import tpu as pltpu
from jax.sharding import PartitionSpec as P

MESH = pl.DeviceIdType.MESH
F32 = jnp.float32
BF16 = jnp.bfloat16

ROWS = 256
STATE = 128
HEADS = 128
HEAD = 64
CONV = 4
HALO = 8
TILE = 512
STEP_ROWS = ROWS + 8
CHIPS = 16
LOG2E = 1.4426950408889634
epsilon = 1e-05
VMEM_LIMIT = 56 * 1024 * 1024

HEADS_HOME = 64
HEADS_EARLY = 16
HEADS_AWAY = HEADS - HEADS_HOME


def dot(a, b):
    return jnp.dot(a, b, preferred_element_type=F32)


def three_parts(x):
    first = x.astype(BF16)
    rest = x - first.astype(F32)
    second = rest.astype(BF16)
    return first, second, (rest - second.astype(F32)).astype(BF16)


def spreader(rows, width):
    head = lax.broadcasted_iota(jnp.int32, (2 * rows, width), 0) % rows
    feature = lax.broadcasted_iota(jnp.int32, (2 * rows, width), 1) // HEAD
    return (head == feature).astype(F32).astype(BF16)


def spread_heads(values, width):
    high = values.astype(BF16).astype(F32)
    both = jnp.concatenate([high, values - high], axis=0).astype(BF16)
    return lax.dot_general(
        both, spreader(values.shape[0], width), (((0,), (0,)), ((), ())), preferred_element_type=F32
    )


def project_kernel(x_ref, ws_ref, wt_ref, gain_ref, bias_ref, rate_ref, skip_ref, maps_ref, step_ref, scale, acc):
    at = pl.program_id(0)
    width = ws_ref.shape[0]

    @pl.when(at == 0)
    def _():
        total = jnp.zeros((ROWS, 128), F32)
        for i in range(x_ref.shape[1] // 512):
            part = x_ref[:, i * 512 : (i + 1) * 512].astype(F32)
            part = part * part
            total = total + (part[:, :128] + part[:, 128:256]) + (part[:, 256:384] + part[:, 384:])
        meansq = jnp.sum(total, axis=-1, keepdims=True) * (1.0 / x_ref.shape[1])
        scale[...] = jnp.broadcast_to(lax.rsqrt(meansq + epsilon), (ROWS, 128))
        acc[...] = jnp.zeros_like(acc)

    columns = pl.ds(pl.multiple_of(at * width, width), width)
    normed = (x_ref[:, columns].astype(F32) * scale[:, :1] * gain_ref[...]).astype(BF16)
    acc[:, : 2 * STATE] += dot(normed, ws_ref[...])
    acc[:, 2 * STATE :] += dot(normed, wt_ref[...])

    @pl.when(at == pl.num_programs(0) - 1)
    def _():
        maps_ref[...] = acc[:, : 2 * STATE].astype(BF16)
        step_ref[:ROWS, :] = jax.nn.softplus(acc[:, 2 * STATE :] + bias_ref[...])
        flat = scale[...].T
        step_ref[ROWS : ROWS + 8, :] = jnp.concatenate(
            [flat[:1, :128], flat[:1, 128:], rate_ref[...], skip_ref[...], jnp.zeros((4, HEADS), F32)], axis=0
        )


def project(x, proj_state, proj_step, gain, bias, rate, skip):
    features = x.shape[1]
    width = 1024
    whole = lambda i: (0, 0)
    return pl.pallas_call(
        project_kernel,
        grid=(features // width,),
        in_specs=[
            pl.BlockSpec((ROWS, features), whole),
            pl.BlockSpec((width, 2 * STATE), lambda i: (i, 0)),
            pl.BlockSpec((width, HEADS), lambda i: (i, 0)),
            pl.BlockSpec((1, width), lambda i: (0, i)),
            pl.BlockSpec((1, HEADS), whole),
            pl.BlockSpec((1, HEADS), whole),
            pl.BlockSpec((1, HEADS), whole),
        ],
        out_specs=[pl.BlockSpec((ROWS, 2 * STATE), whole), pl.BlockSpec((STEP_ROWS, HEADS), whole)],
        out_shape=[
            jax.ShapeDtypeStruct((ROWS, 2 * STATE), BF16),
            jax.ShapeDtypeStruct((STEP_ROWS, HEADS), F32),
        ],
        scratch_shapes=[pltpu.VMEM((ROWS, 128), F32), pltpu.VMEM((ROWS, 3 * STATE), F32)],
        compiler_params=pltpu.CompilerParams(
            dimension_semantics=("arbitrary",), vmem_limit_bytes=VMEM_LIMIT
        ),
        cost_estimate=pl.CostEstimate(
            flops=ROWS * features, bytes_accessed=ROWS * features, transcendentals=0
        ),
        name="project",
    )(x, proj_state, proj_step, gain, bias, rate, skip)


def group_kernel(
    first,
    pieces,
    *refs,
):
    x_refs, refs = refs[: len(pieces)], refs[len(pieces) :]
    group_body(first, pieces, x_refs, *refs)


def group_body(
    first,
    pieces,
    x_refs,
    halo_ref,
    vec_ref,
    maps_ref,
    step_ref,
    out_ref,
    x_ref,
    x_sems,
    cum_heads,
    weight_heads,
    enter_heads,
    step_heads,
    skip_heads,
    closing,
    scale,
    scores,
    write_flat,
    inner_ref,
    within_ref,
    fresh,
    peer,
    peer_closing,
    total,
    total_closing,
    got,
    got_closing,
    before,
    entering,
    mine,
    theirs,
    landed,
    pair_send,
    pair_recv,
    send1,
    recv1,
    send2,
    recv2,
    send3,
    recv3,
):
    features = x_ref.shape[1]
    half, quarter = features // 2, features // 4
    heads = features // HEAD
    tiles = features // TILE
    in_tile = TILE // HEAD
    me = lax.axis_index("ctx")
    core = lax.rem(me, 2)
    chip = me // 2
    partner = chip * 2 + (1 - core)

    def device(index):
        return {"ctx": index}

    def tile_columns(i):
        return pl.ds(pl.multiple_of(i * TILE, TILE), TILE)

    def tile_heads(i):
        return pl.ds(pl.multiple_of(first + i * in_tile, in_tile), in_tile)

    def place(of):
        return (
            pl.ds(pl.multiple_of(lax.rem(of, 8) * 16, 16), 16),
            pl.ds(pl.multiple_of((of // 8) * quarter, 128), quarter),
        )

    barrier = pltpu.get_barrier_semaphore()
    pl.semaphore_signal(barrier, inc=1, device_id=device(partner), device_id_type=MESH)

    def greet(d, carry):
        other = lax.rem(chip + d, CHIPS) * 2 + core
        pl.semaphore_signal(barrier, inc=1, device_id=device(other), device_id_type=MESH)
        return carry

    lax.fori_loop(1, CHIPS, greet, 0)

    loads = []
    for k, width in enumerate(pieces):
        start = sum(pieces[:k])
        load = pltpu.make_async_copy(
            x_refs[k].at[:, :width], x_ref.at[:, start : start + width], x_sems.at[k]
        )
        load.start()
        loads.append(load)

    step = step_ref[:ROWS, :]
    extra = step_ref[ROWS:, :]
    log_decay = -step * extra[2:3, :]
    row = lax.broadcasted_iota(jnp.int32, (ROWS, ROWS), 0)
    column = lax.broadcasted_iota(jnp.int32, (ROWS, ROWS), 1)
    lower = (row >= column).astype(F32).astype(BF16)
    part1, part2, part3 = three_parts(log_decay)
    cumulative = dot(lower, part3) + dot(lower, part2) + dot(lower, part1)
    last = cumulative[ROWS - 1 :, :]
    cum_heads[...] = (cumulative * LOG2E).T
    weight_heads[...] = (jnp.exp(last - cumulative) * step).T
    enter_heads[...] = jnp.exp(cumulative).T
    step_heads[...] = step.T
    closing[...] = jnp.broadcast_to(last, (8, HEADS))
    extra_columns = extra.T
    skip_heads[...] = jnp.broadcast_to(extra_columns[:, 3:4], (HEADS, 128))
    scale[...] = jnp.broadcast_to(
        jnp.concatenate([extra_columns[:, 0:1], extra_columns[:, 1:2]], axis=0), (ROWS, 128)
    )
    write_flat[...] = maps_ref[:, :STATE].astype(F32).T.astype(BF16)
    product = dot(maps_ref[:, STATE:], write_flat[...])
    scores[...] = jnp.where(row >= column, product, 0.0)

    for load in loads:
        load.wait()

    def fresh_tile(i):
        columns = tile_columns(i)
        normed = (x_ref[:, columns].astype(F32) * scale[:, :1] * vec_ref[4:5, columns]).astype(BF16)
        normed = jnp.concatenate([halo_ref[:, columns].astype(F32), normed.astype(F32)], axis=0)
        shifted = pltpu.roll(normed, 1, 0)
        early = vec_ref[1:2, columns] * normed + vec_ref[0:1, columns] * shifted
        conv = vec_ref[3:4, columns] * normed[HALO:] + vec_ref[2:3, columns] * shifted[HALO:]
        conv = conv + pltpu.roll(early, 2, 0)[HALO:]
        conv = conv * 0.5
        inner = (conv + conv * jnp.tanh(conv)).astype(BF16)
        inner_ref[:, columns] = inner
        spread = spread_heads(weight_heads[tile_heads(i), :], TILE)
        weighted = (inner.astype(F32) * spread).astype(BF16)
        fresh[:, columns] = dot(write_flat[...], weighted).astype(BF16)

    def within_tile(i):
        columns = tile_columns(i)
        inner = inner_ref[:, columns].astype(F32)
        stepped = (inner * spread_heads(step_heads[tile_heads(i), :], TILE)).astype(BF16)
        cum = cum_heads[tile_heads(i), :]
        cum_columns = cum.T
        top, bottom = scores[:128, :128], scores[128:, :]
        lane = lax.broadcasted_iota(jnp.int32, (ROWS, 128), 1)
        for pair in range(TILE // 128):
            values = stepped[:, pair * 128 : (pair + 1) * 128]
            upper = lower = None
            for side in range(2):
                h = pair * 2 + side
                column = cum_columns[:, h : h + 1]
                row = cum[h : h + 1, :]
                own = jnp.where((lane >= HEAD) == (side == 1), values, jnp.zeros_like(values))
                mix0 = (jnp.exp2(jnp.minimum(column[:128] - row[:, :128], 0.0)) * top).astype(BF16)
                mix1 = (jnp.exp2(jnp.minimum(column[128:] - row, 0.0)) * bottom).astype(BF16)
                up, low = dot(mix0, own[:128]), dot(mix1, own)
                upper = up if upper is None else upper + up
                lower = low if lower is None else lower + low
            at = pl.ds(pl.multiple_of(i * TILE + pair * 128, 128), 128)
            within_ref[:128, at] = upper
            within_ref[128:, at] = lower

    def finish_tile(i, state):
        columns = tile_columns(i)
        inner = inner_ref[:, columns].astype(F32)
        carried = dot(maps_ref[:, STATE:], state) * spread_heads(enter_heads[tile_heads(i), :], TILE)
        skip = spread_heads(skip_heads[tile_heads(i), :8], TILE)[0:1, :]
        output = within_ref[:, columns] + carried + skip * inner
        square = (output * output).astype(BF16)
        a = lax.broadcasted_iota(jnp.int32, (256, 256), 0) // HEAD
        b = lax.broadcasted_iota(jnp.int32, (256, 256), 1) // HEAD
        same = (a == b).astype(F32).astype(BF16)
        sums = jnp.concatenate(
            [dot(square[:, k * 256 : (k + 1) * 256], same) for k in range(TILE // 256)], axis=1
        )
        normed = output * lax.rsqrt(sums * (1.0 / HEAD) + epsilon)
        out_ref[:, columns] = (x_ref[:, columns].astype(F32) + normed * vec_ref[5:6, columns]).astype(BF16)

    def run(body, start, stop):
        def one(i, carry):
            body(i)
            return carry

        lax.fori_loop(start, stop, one, 0)

    mine_columns = pl.ds(pl.multiple_of(core * half, 128), half)
    other_columns = pl.ds(pl.multiple_of((1 - core) * half, 128), half)
    mine_tile, other_tile = core * (tiles // 2), (1 - core) * (tiles // 2)

    run(lambda j: fresh_tile(other_tile + j), 0, tiles // 2)
    pl.semaphore_wait(barrier, CHIPS)
    to_pair = pltpu.make_async_remote_copy(
        fresh.at[:, other_columns], peer, pair_send.at[0], pair_recv.at[0], device(partner), MESH
    )
    to_pair_closing = pltpu.make_async_remote_copy(
        closing, peer_closing, pair_send.at[1], pair_recv.at[1], device(partner), MESH
    )
    to_pair.start()
    to_pair_closing.start()
    run(lambda j: fresh_tile(mine_tile + j), 0, tiles // 2)
    to_pair.wait()
    to_pair_closing.wait()

    is_first = core == 0
    own = fresh[:, mine_columns].astype(F32)
    other = peer[...].astype(F32)
    state0 = jnp.where(is_first, own, other)
    state1 = jnp.where(is_first, other, own)
    closing0 = jnp.where(is_first, closing[...], peer_closing[...])
    closing1 = jnp.where(is_first, peer_closing[...], closing[...])

    def decay_of(log_decays, first_head, width):
        values = jnp.exp(log_decays)
        high = values.astype(BF16)
        both = jnp.concatenate([high, (values - high.astype(F32)).astype(BF16)], axis=1)
        head = lax.broadcasted_iota(jnp.int32, (2 * HEADS, width), 0) % HEADS
        feature = lax.broadcasted_iota(jnp.int32, (2 * HEADS, width), 1) // HEAD
        return dot(both, (head == first_head + feature).astype(F32).astype(BF16))

    both = decay_of(jnp.concatenate([closing0, closing1], axis=0), first + core * (heads // 2), half)
    decay0, decay1 = both[0:1, :], both[8:9, :]
    total[...] = (decay1 * state0 + state1).astype(BF16)
    total_closing[...] = closing0 + closing1

    def state_copy(source, target, to):
        rows, columns = place(to)
        return pltpu.make_async_remote_copy(
            total.at[rows, columns], got.at[target], send1.at[to], recv1.at[source], device(to * 2 + core), MESH
        )

    def closing_copy(source, target, to):
        return pltpu.make_async_remote_copy(
            total_closing, got_closing.at[target], send2.at[to], recv2.at[source], device(to * 2 + core), MESH
        )

    def back_copy(source, to):
        rows, columns = place(source)
        return pltpu.make_async_remote_copy(
            before.at[to], entering.at[rows, columns], send3.at[to], recv3.at[source], device(to * 2 + core), MESH
        )

    def start12(d):
        to = lax.rem(chip + d, CHIPS)
        closing_copy(chip, chip, to).start()
        state_copy(chip, chip, to).start()

    def wait12(d):
        of = lax.rem(chip + d, CHIPS)
        closing_copy(of, of, of).wait_recv()
        state_copy(of, of, of).wait_recv()
        closing_copy(chip, chip, of).wait_send()
        state_copy(chip, chip, of).wait_send()

    run(start12, 1, CHIPS)
    rows, columns = place(chip)
    got[chip] = total[rows, columns]
    got_closing[chip] = total_closing[...]
    run(within_tile, 0, tiles // 2)
    run(wait12, 1, CHIPS)

    decays = decay_of(got_closing[:, 0, :], first + core * (heads // 2) + (chip // 8) * (heads // 4), quarter)
    state = jnp.zeros((16, quarter), F32)
    for k in range(CHIPS):
        before[k] = state.astype(BF16)
        if k < CHIPS - 1:
            state = decays[k : k + 1, :] * state + got[k].astype(F32)

    def start3(d):
        back_copy(chip, lax.rem(chip + d, CHIPS)).start()

    def wait3(d):
        of = lax.rem(chip + d, CHIPS)
        back_copy(of, of).wait_recv()
        back_copy(chip, of).wait_send()

    run(start3, 1, CHIPS)
    entering[rows, columns] = before[chip]
    run(within_tile, tiles // 2, tiles)
    run(wait3, 1, CHIPS)

    for_first = entering[...]
    for_second = (decay0 * for_first.astype(F32) + state0).astype(BF16)
    theirs[...] = jnp.where(is_first, for_second, for_first)
    back = pltpu.make_async_remote_copy(theirs, landed, pair_send.at[2], pair_recv.at[2], device(partner), MESH)
    back.start()
    mine[...] = jnp.where(is_first, for_first, for_second)
    run(lambda j: finish_tile(mine_tile + j, mine[:, tile_columns(j)]), 0, tiles // 2)
    back.wait()
    run(lambda j: finish_tile(other_tile + j, landed[:, tile_columns(j)]), 0, tiles // 2)


def group(first, pieces, xs, halo, vec, maps, step, collective_id):
    features = sum(pieces)
    half, quarter = features // 2, features // 4
    corner = lambda i: (0, 0)
    dma = pltpu.SemaphoreType.DMA
    vmem = pltpu.VMEM
    return pl.pallas_call(
        functools.partial(group_kernel, first, pieces),
        out_shape=jax.ShapeDtypeStruct((ROWS, features), BF16),
        grid=(1,),
        in_specs=[pl.BlockSpec(memory_space=pl.ANY)] * len(pieces)
        + [
            pl.BlockSpec((HALO, features), corner),
            pl.BlockSpec((vec.shape[0], features), corner),
            pl.BlockSpec((ROWS, 2 * STATE), corner),
            pl.BlockSpec((STEP_ROWS, HEADS), corner),
        ],
        out_specs=pl.BlockSpec((ROWS, features), corner),
        scratch_shapes=[
            vmem((ROWS, features), BF16),
            dma((len(pieces),)),
            vmem((HEADS, ROWS), F32),
            vmem((HEADS, ROWS), F32),
            vmem((HEADS, ROWS), F32),
            vmem((HEADS, ROWS), F32),
            vmem((HEADS, 128), F32),
            vmem((8, HEADS), F32),
            vmem((ROWS, 128), F32),
            vmem((ROWS, ROWS), F32),
            vmem((STATE, ROWS), BF16),
            vmem((ROWS, features), BF16),
            vmem((ROWS, features), F32),
            vmem((STATE, features), BF16),
            vmem((STATE, half), BF16),
            vmem((8, HEADS), F32),
            vmem((STATE, half), BF16),
            vmem((8, HEADS), F32),
            vmem((CHIPS, 16, quarter), BF16),
            vmem((CHIPS, 8, HEADS), F32),
            vmem((CHIPS, 16, quarter), BF16),
            vmem((STATE, half), BF16),
            vmem((STATE, half), BF16),
            vmem((STATE, half), BF16),
            vmem((STATE, half), BF16),
            dma((3,)),
            dma((3,)),
            dma((CHIPS,)),
            dma((CHIPS,)),
            dma((CHIPS,)),
            dma((CHIPS,)),
            dma((CHIPS,)),
            dma((CHIPS,)),
        ],
        compiler_params=pltpu.CompilerParams(
            collective_id=collective_id, has_side_effects=True, vmem_limit_bytes=VMEM_LIMIT
        ),
        cost_estimate=pl.CostEstimate(
            flops=ROWS * features, bytes_accessed=ROWS * features, transcendentals=0
        ),
        name="group",
    )(*xs, halo, vec, maps, step)


def widen_kernel(part_ref, out_ref):
    out_ref[...] = part_ref[...]


def widen(part, width):
    columns = part.shape[1]
    block = 1024
    skip = (width - columns) // block
    return pl.pallas_call(
        widen_kernel,
        grid=(columns // block,),
        in_specs=[pl.BlockSpec((ROWS, block), lambda i: (0, i))],
        out_specs=pl.BlockSpec((ROWS, block), lambda i: (0, skip + i)),
        out_shape=jax.ShapeDtypeStruct((ROWS, width), BF16),
        compiler_params=pltpu.CompilerParams(dimension_semantics=("arbitrary",)),
        cost_estimate=pl.CostEstimate(flops=1, bytes_accessed=ROWS * columns * 4, transcendentals=0),
        name="widen",
    )(part)


def onward(array):
    peers = lax.axis_size("pipe")
    return lax.ppermute(array, "pipe", [(i, (i + 1) % peers) for i in range(peers)])


def normalize(values_in, gain_row):
    values = values_in.astype(F32)
    meansq = jnp.mean(values * values, axis=-1, keepdims=True)
    return (values * lax.rsqrt(meansq + epsilon) * gain_row).astype(BF16)


def shards(
    incoming, norm_gain, proj_state, proj_step, conv_weight, decay_rate, step_bias, skip_gain, out_gain
):
    x = incoming[0]
    home, early = HEADS_HOME * HEAD, HEADS_EARLY * HEAD
    away = HEADS_AWAY * HEAD
    tokens_peers = lax.axis_size("ctx")

    x_early = onward(x[:, home : home + early])
    x_late = onward(x[:, home + early :])
    edge = lax.ppermute(x[ROWS - HALO :], "ctx", [(i, i + 1) for i in range(tokens_peers - 1)])
    vec = jnp.concatenate([conv_weight[0], norm_gain, out_gain], axis=0)
    vec_away = onward(vec[:, home:])
    maps, step = project(x, proj_state[0], proj_step[0], norm_gain, step_bias, decay_rate, skip_gain)
    maps, step, x_early = lax.optimization_barrier((maps, step, x_early))
    maps_away, step_away = onward(maps), onward(step)
    halo = normalize(edge, norm_gain[0])
    halo_away = onward(halo[:, home:])

    rows = group(0, (home,), (x,), halo, vec, maps, step, 0)
    rows, x_late, halo_away, vec_away, maps_away, step_away = lax.optimization_barrier(
        (rows, x_late, halo_away, vec_away, maps_away, step_away)
    )
    rows_in = onward(rows)

    rows_away = group(
        HEADS_HOME, (early, away - early), (x_early, x_late), halo_away, vec_away, maps_away, step_away, 1
    )
    passed = widen(rows_away, x.shape[1])
    return lax.dynamic_update_slice(passed, rows_in, (0, 0))[None]


def solution(mesh):
    return jax.shard_map(
        shards,
        mesh=mesh,
        in_specs=(
            P("pipe", "ctx", None),
            P("pipe", None),
            P("pipe", None, None),
            P("pipe", None, None),
            P("pipe", None, None),
            P("pipe", None),
            P("pipe", None),
            P("pipe", None),
            P("pipe", None),
        ),
        out_specs=P("pipe", "ctx", None),
        check_vma=False,
    )
```

```python
import functools

import jax
import jax.numpy as jnp
from jax import lax
from jax.experimental import pallas as pl
from jax.experimental.pallas import tpu as pltpu
from jax.sharding import PartitionSpec as P

MESH = pl.DeviceIdType.MESH
F32 = jnp.float32
BF16 = jnp.bfloat16

ROWS = 256
STATE = 128
HEADS = 128
HEAD = 64
CONV = 4
HALO = 8
TILE = 512
STEP_ROWS = ROWS + 8
CHIPS = 16
LOG2E = 1.4426950408889634
epsilon = 1e-05
VMEM_LIMIT = 56 * 1024 * 1024

HEADS_HOME = 64
HEADS_BACK = 12
HEADS_EARLY = 12
HEADS_ROUND = 12
HEADS_AWAY = HEADS - HEADS_HOME
HEADS_LATE = HEADS_AWAY - HEADS_EARLY - HEADS_ROUND


def dot(a, b):
    return jnp.dot(a, b, preferred_element_type=F32)


def three_parts(x):
    first = x.astype(BF16)
    rest = x - first.astype(F32)
    second = rest.astype(BF16)
    return first, second, (rest - second.astype(F32)).astype(BF16)


def spreader(rows, width):
    head = lax.broadcasted_iota(jnp.int32, (2 * rows, width), 0) % rows
    feature = lax.broadcasted_iota(jnp.int32, (2 * rows, width), 1) // HEAD
    return (head == feature).astype(F32).astype(BF16)


def spread_heads(values, width):
    high = values.astype(BF16).astype(F32)
    both = jnp.concatenate([high, values - high], axis=0).astype(BF16)
    return lax.dot_general(
        both, spreader(values.shape[0], width), (((0,), (0,)), ((), ())), preferred_element_type=F32
    )


def project_kernel(
    first,
    x_ref,
    ws_ref,
    wt_ref,
    gain_ref,
    conv_ref,
    out_gain_ref,
    bias_ref,
    rate_ref,
    skip_ref,
    maps_ref,
    step_ref,
    vec_ref,
    vec_away_ref,
    halo_ref,
    halo_away_ref,
    early_ref,
    late_ref,
    round_ref,
    scale,
    acc,
    edge,
    send,
    recv,
    late_sem,
):
    at = pl.program_id(0)
    width = ws_ref.shape[0]
    features = x_ref.shape[1]
    away = vec_away_ref.shape[1]
    me = lax.axis_index("ctx")
    peers = lax.axis_size("ctx")
    after, ahead = lax.rem(me + 1, peers), lax.rem(me + peers - 1, peers)
    edge_copy = pltpu.make_async_remote_copy(
        x_ref.at[ROWS - 16 :, :], edge, send.at[0], recv.at[0], {"ctx": after}, MESH
    )
    section = lax.axis_index("pipe")
    sections = lax.axis_size("pipe")
    behind, beyond = lax.rem(section + sections - 1, sections), lax.rem(section + 1, sections)
    second = first + early_ref.shape[1]
    third = second + late_ref.shape[1]
    early_copy = pltpu.make_async_remote_copy(
        x_ref.at[:, first:second], early_ref, send.at[1], recv.at[1], {"pipe": beyond}, MESH
    )
    late_copy = pltpu.make_async_copy(x_ref.at[:, second:third], late_ref, late_sem)
    round_copy = pltpu.make_async_remote_copy(
        x_ref.at[:, third:], round_ref, send.at[2], recv.at[2], {"pipe": behind}, MESH
    )

    @pl.when(at == 0)
    def _():
        barrier = pltpu.get_barrier_semaphore()
        for other in (after, ahead):
            pl.semaphore_signal(barrier, inc=1, device_id={"ctx": other}, device_id_type=MESH)
        for other in (behind, beyond):
            pl.semaphore_signal(barrier, inc=1, device_id={"pipe": other}, device_id_type=MESH)
        pl.semaphore_wait(barrier, 4)
        early_copy.start()
        round_copy.start()
        edge_copy.start()
        late_copy.start()
        total = jnp.zeros((ROWS, 128), F32)
        for i in range(features // 512):
            part = x_ref[:, i * 512 : (i + 1) * 512].astype(F32)
            part = part * part
            total = total + (part[:, :128] + part[:, 128:256]) + (part[:, 256:384] + part[:, 384:])
        meansq = jnp.sum(total, axis=-1, keepdims=True) * (1.0 / features)
        scale[...] = jnp.broadcast_to(lax.rsqrt(meansq + epsilon), (ROWS, 128))
        acc[...] = jnp.zeros_like(acc)

    columns = pl.ds(pl.multiple_of(at * width, width), width)
    normed = (x_ref[:, columns].astype(F32) * scale[:, :1] * gain_ref[:, columns]).astype(BF16)
    acc[:, : 2 * STATE] += dot(normed, ws_ref[...])
    acc[:, 2 * STATE :] += dot(normed, wt_ref[...])

    @pl.when(at == pl.num_programs(0) - 1)
    def _():
        maps_ref[...] = acc[:, : 2 * STATE].astype(BF16)
        step_ref[:ROWS, :] = jax.nn.softplus(acc[:, 2 * STATE :] + bias_ref[...])
        flat = scale[...].T
        step_ref[ROWS : ROWS + 8, :] = jnp.concatenate(
            [flat[:1, :128], flat[:1, 128:], rate_ref[...], skip_ref[...], jnp.zeros((4, HEADS), F32)], axis=0
        )
        vec_ref[:4, :] = conv_ref[...]
        vec_ref[4:5, :] = gain_ref[...]
        vec_ref[5:6, :] = out_gain_ref[...]
        vec_ref[6:8, :] = jnp.zeros((2, features), F32)
        vec_away_ref[...] = vec_ref[:, features - away :]
        edge_copy.wait()
        rows = edge[...].astype(F32)[16 - HALO :, :]
        meansq = jnp.sum(rows * rows, axis=-1, keepdims=True) * (1.0 / features)
        rows = rows * lax.rsqrt(meansq + epsilon) * gain_ref[...]
        rows = jnp.where(me == 0, jnp.zeros_like(rows), rows).astype(BF16)
        halo_ref[...] = rows
        halo_away_ref[...] = rows[:, features - away :]
        late_copy.wait()
        early_copy.wait()
        round_copy.wait()


def project(x, proj_state, proj_step, gain, conv, out_gain, bias, rate, skip, widths, collective_id):
    features = x.shape[1]
    away = sum(widths)
    width = 1024
    whole = lambda i: (0, 0)
    dma = pltpu.SemaphoreType.DMA
    row = pl.BlockSpec((1, features), whole)
    small = pl.BlockSpec((1, HEADS), whole)
    return pl.pallas_call(
        functools.partial(project_kernel, features - away),
        grid=(features // width,),
        in_specs=[
            pl.BlockSpec((ROWS, features), whole),
            pl.BlockSpec((width, 2 * STATE), lambda i: (i, 0)),
            pl.BlockSpec((width, HEADS), lambda i: (i, 0)),
            row,
            pl.BlockSpec((CONV, features), whole),
            row,
            small,
            small,
            small,
        ],
        out_specs=[
            pl.BlockSpec((ROWS, 2 * STATE), whole),
            pl.BlockSpec((STEP_ROWS, HEADS), whole),
            pl.BlockSpec((8, features), whole),
            pl.BlockSpec((8, away), whole),
            pl.BlockSpec((HALO, features), whole),
            pl.BlockSpec((HALO, away), whole),
        ]
        + [pl.BlockSpec(memory_space=pl.ANY)] * 3,
        out_shape=[
            jax.ShapeDtypeStruct((ROWS, 2 * STATE), BF16),
            jax.ShapeDtypeStruct((STEP_ROWS, HEADS), F32),
            jax.ShapeDtypeStruct((8, features), F32),
            jax.ShapeDtypeStruct((8, away), F32),
            jax.ShapeDtypeStruct((HALO, features), BF16),
            jax.ShapeDtypeStruct((HALO, away), BF16),
        ]
        + [jax.ShapeDtypeStruct((ROWS, columns), BF16) for columns in widths],
        scratch_shapes=[
            pltpu.VMEM((ROWS, 128), F32),
            pltpu.VMEM((ROWS, 3 * STATE), F32),
            pltpu.VMEM((16, features), BF16),
            dma((3,)),
            dma((3,)),
            dma,
        ],
        compiler_params=pltpu.CompilerParams(
            dimension_semantics=("arbitrary",),
            vmem_limit_bytes=VMEM_LIMIT,
            collective_id=collective_id,
            has_side_effects=True,
        ),
        cost_estimate=pl.CostEstimate(
            flops=2 * ROWS * features * 3 * STATE, bytes_accessed=36 << 20, transcendentals=0
        ),
        name="project",
    )(x, proj_state, proj_step, gain, conv, out_gain, bias, rate, skip)


def group_kernel(first, pieces, hops, outs, *refs):
    refs = list(refs)

    def take(n):
        taken = refs[:n]
        del refs[:n]
        return taken

    x_refs = take(len(pieces))
    shared = take(4)
    relay_in = take(1)[0]
    out_refs = take(len(outs))
    relay_out = take(1)[0]
    group_body(first, pieces, hops, outs, x_refs, *shared, relay_in, out_refs, relay_out, *refs)


def group_body(
    first,
    pieces,
    hops,
    outs,
    x_refs,
    halo_ref,
    vec_ref,
    maps_ref,
    step_ref,
    relay_in,
    out_refs,
    relay_out,
    relay_slots,
    relay_send,
    relay_recv,
    out_ref,
    out_sems,
    x_ref,
    x_sems,
    cum_heads,
    weight_heads,
    enter_heads,
    step_heads,
    skip_heads,
    closing,
    scale,
    scores,
    write_flat,
    inner_ref,
    within_ref,
    fresh,
    peer,
    peer_closing,
    total,
    total_closing,
    got,
    got_closing,
    before,
    entering,
    mine,
    theirs,
    landed,
    pair_send,
    pair_recv,
    send1,
    recv1,
    send2,
    recv2,
    send3,
    recv3,
):
    features = x_ref.shape[1]
    half, quarter = features // 2, features // 4
    heads = features // HEAD
    tiles = features // TILE
    in_tile = TILE // HEAD
    me = lax.axis_index("ctx")
    core = lax.rem(me, 2)
    chip = me // 2
    partner = chip * 2 + (1 - core)

    def device(index):
        return {"ctx": index}

    section = lax.axis_index("pipe")
    sections = lax.axis_size("pipe")
    behind, ahead = lax.rem(section + sections - 1, sections), lax.rem(section + 1, sections)

    def hop(k):
        source = relay_in if k == 0 else relay_slots.at[k - 1]
        return pltpu.make_async_remote_copy(
            source, relay_slots.at[k], relay_send.at[k], relay_recv.at[k], {"pipe": behind}, MESH
        )

    def pass_on(k):
        if k > 0:
            hop(k - 1).wait_recv()
        hop(k).start()

    def tile_columns(i):
        return pl.ds(pl.multiple_of(i * TILE, TILE), TILE)

    def tile_heads(i):
        return pl.ds(pl.multiple_of(first + i * in_tile, in_tile), in_tile)

    def place(of):
        return (
            pl.ds(pl.multiple_of(lax.rem(of, 8) * 16, 16), 16),
            pl.ds(pl.multiple_of((of // 8) * quarter, 128), quarter),
        )

    barrier = pltpu.get_barrier_semaphore()
    pl.semaphore_signal(barrier, inc=1, device_id=device(partner), device_id_type=MESH)

    def greet(d, carry):
        other = lax.rem(chip + d, CHIPS) * 2 + core
        pl.semaphore_signal(barrier, inc=1, device_id=device(other), device_id_type=MESH)
        return carry

    lax.fori_loop(1, CHIPS, greet, 0)
    for other in (behind, ahead):
        pl.semaphore_signal(barrier, inc=1, device_id={"pipe": other}, device_id_type=MESH)

    loads = []
    for k, width in enumerate(pieces):
        start = sum(pieces[:k])
        load = pltpu.make_async_copy(
            x_refs[k].at[:, :width], x_ref.at[:, start : start + width], x_sems.at[k]
        )
        load.start()
        loads.append(load)

    step = step_ref[:ROWS, :]
    extra = step_ref[ROWS:, :]
    log_decay = -step * extra[2:3, :]
    row = lax.broadcasted_iota(jnp.int32, (ROWS, ROWS), 0)
    column = lax.broadcasted_iota(jnp.int32, (ROWS, ROWS), 1)
    lower = (row >= column).astype(F32).astype(BF16)
    part1, part2, part3 = three_parts(log_decay)
    cumulative = dot(lower, part3) + dot(lower, part2) + dot(lower, part1)
    last = cumulative[ROWS - 1 :, :]
    cum_heads[...] = (cumulative * LOG2E).T
    weight_heads[...] = (jnp.exp(last - cumulative) * step).T
    enter_heads[...] = jnp.exp(cumulative).T
    step_heads[...] = step.T
    closing[...] = jnp.broadcast_to(last, (8, HEADS))
    extra_columns = extra.T
    skip_heads[...] = jnp.broadcast_to(extra_columns[:, 3:4], (HEADS, 128))
    scale[...] = jnp.broadcast_to(
        jnp.concatenate([extra_columns[:, 0:1], extra_columns[:, 1:2]], axis=0), (ROWS, 128)
    )
    write_flat[...] = maps_ref[:, :STATE].astype(F32).T.astype(BF16)
    product = dot(maps_ref[:, STATE:], write_flat[...])
    scores[...] = jnp.where(row >= column, product, 0.0)

    for load in loads:
        load.wait()
    pl.semaphore_wait(barrier, CHIPS + 2)
    pass_on(0)

    def fresh_tile(i):
        columns = tile_columns(i)
        normed = (x_ref[:, columns].astype(F32) * scale[:, :1] * vec_ref[4:5, columns]).astype(BF16)
        normed = jnp.concatenate([halo_ref[:, columns].astype(F32), normed.astype(F32)], axis=0)
        shifted = pltpu.roll(normed, 1, 0)
        early = vec_ref[1:2, columns] * normed + vec_ref[0:1, columns] * shifted
        conv = vec_ref[3:4, columns] * normed[HALO:] + vec_ref[2:3, columns] * shifted[HALO:]
        conv = conv + pltpu.roll(early, 2, 0)[HALO:]
        conv = conv * 0.5
        inner = (conv + conv * jnp.tanh(conv)).astype(BF16)
        inner_ref[:, columns] = inner
        spread = spread_heads(weight_heads[tile_heads(i), :], TILE)
        weighted = (inner.astype(F32) * spread).astype(BF16)
        fresh[:, columns] = dot(write_flat[...], weighted).astype(BF16)

    def within_tile(i):
        columns = tile_columns(i)
        inner = inner_ref[:, columns].astype(F32)
        stepped = (inner * spread_heads(step_heads[tile_heads(i), :], TILE)).astype(BF16)
        cum = cum_heads[tile_heads(i), :]
        cum_columns = cum.T
        top, bottom = scores[:128, :128], scores[128:, :]
        lane = lax.broadcasted_iota(jnp.int32, (ROWS, 128), 1)
        for pair in range(TILE // 128):
            values = stepped[:, pair * 128 : (pair + 1) * 128]
            upper = lower = None
            for side in range(2):
                h = pair * 2 + side
                column = cum_columns[:, h : h + 1]
                row = cum[h : h + 1, :]
                own = jnp.where((lane >= HEAD) == (side == 1), values, jnp.zeros_like(values))
                mix0 = (jnp.exp2(jnp.minimum(column[:128] - row[:, :128], 0.0)) * top).astype(BF16)
                mix1 = (jnp.exp2(jnp.minimum(column[128:] - row, 0.0)) * bottom).astype(BF16)
                up, low = dot(mix0, own[:128]), dot(mix1, own)
                upper = up if upper is None else upper + up
                lower = low if lower is None else lower + low
            at = pl.ds(pl.multiple_of(i * TILE + pair * 128, 128), 128)
            within_ref[:128, at] = upper
            within_ref[128:, at] = lower

    def finish_tile(i, state):
        columns = tile_columns(i)
        inner = inner_ref[:, columns].astype(F32)
        carried = dot(maps_ref[:, STATE:], state) * spread_heads(enter_heads[tile_heads(i), :], TILE)
        skip = spread_heads(skip_heads[tile_heads(i), :8], TILE)[0:1, :]
        output = within_ref[:, columns] + carried + skip * inner
        square = (output * output).astype(BF16)
        a = lax.broadcasted_iota(jnp.int32, (256, 256), 0) // HEAD
        b = lax.broadcasted_iota(jnp.int32, (256, 256), 1) // HEAD
        same = (a == b).astype(F32).astype(BF16)
        sums = jnp.concatenate(
            [dot(square[:, k * 256 : (k + 1) * 256], same) for k in range(TILE // 256)], axis=1
        )
        normed = output * lax.rsqrt(sums * (1.0 / HEAD) + epsilon)
        out_ref[:, columns] = (x_ref[:, columns].astype(F32) + normed * vec_ref[5:6, columns]).astype(BF16)

    def run(body, start, stop):
        def one(i, carry):
            body(i)
            return carry

        lax.fori_loop(start, stop, one, 0)

    mine_columns = pl.ds(pl.multiple_of(core * half, 128), half)
    other_columns = pl.ds(pl.multiple_of((1 - core) * half, 128), half)
    mine_tile, other_tile = core * (tiles // 2), (1 - core) * (tiles // 2)

    run(lambda j: fresh_tile(other_tile + j), 0, tiles // 2)
    to_pair = pltpu.make_async_remote_copy(
        fresh.at[:, other_columns], peer, pair_send.at[0], pair_recv.at[0], device(partner), MESH
    )
    to_pair_closing = pltpu.make_async_remote_copy(
        closing, peer_closing, pair_send.at[1], pair_recv.at[1], device(partner), MESH
    )
    to_pair.start()
    to_pair_closing.start()
    run(lambda j: fresh_tile(mine_tile + j), 0, tiles // 2)
    to_pair.wait()
    to_pair_closing.wait()

    is_first = core == 0
    own = fresh[:, mine_columns].astype(F32)
    other = peer[...].astype(F32)
    state0 = jnp.where(is_first, own, other)
    state1 = jnp.where(is_first, other, own)
    closing0 = jnp.where(is_first, closing[...], peer_closing[...])
    closing1 = jnp.where(is_first, peer_closing[...], closing[...])

    def decay_of(log_decays, first_head, width):
        values = jnp.exp(log_decays)
        high = values.astype(BF16)
        both = jnp.concatenate([high, (values - high.astype(F32)).astype(BF16)], axis=1)
        head = lax.broadcasted_iota(jnp.int32, (2 * HEADS, width), 0) % HEADS
        feature = lax.broadcasted_iota(jnp.int32, (2 * HEADS, width), 1) // HEAD
        return dot(both, (head == first_head + feature).astype(F32).astype(BF16))

    both = decay_of(jnp.concatenate([closing0, closing1], axis=0), first + core * (heads // 2), half)
    decay0, decay1 = both[0:1, :], both[8:9, :]
    total[...] = (decay1 * state0 + state1).astype(BF16)
    total_closing[...] = closing0 + closing1

    def state_copy(source, target, to):
        rows, columns = place(to)
        return pltpu.make_async_remote_copy(
            total.at[rows, columns], got.at[target], send1.at[to], recv1.at[source], device(to * 2 + core), MESH
        )

    def closing_copy(source, target, to):
        return pltpu.make_async_remote_copy(
            total_closing, got_closing.at[target], send2.at[to], recv2.at[source], device(to * 2 + core), MESH
        )

    def back_copy(source, to):
        rows, columns = place(source)
        return pltpu.make_async_remote_copy(
            before.at[to], entering.at[rows, columns], send3.at[to], recv3.at[source], device(to * 2 + core), MESH
        )

    def start12(d):
        to = lax.rem(chip + d, CHIPS)
        closing_copy(chip, chip, to).start()
        state_copy(chip, chip, to).start()

    def wait12(d):
        of = lax.rem(chip + d, CHIPS)
        closing_copy(of, of, of).wait_recv()
        state_copy(of, of, of).wait_recv()
        closing_copy(chip, chip, of).wait_send()
        state_copy(chip, chip, of).wait_send()

    run(start12, 1, CHIPS)
    rows, columns = place(chip)
    got[chip] = total[rows, columns]
    got_closing[chip] = total_closing[...]
    if hops == 3:
        pass_on(1)
    run(within_tile, 0, tiles // 2)
    if hops == 2:
        pass_on(1)
    run(wait12, 1, CHIPS)

    decays = decay_of(got_closing[:, 0, :], first + core * (heads // 2) + (chip // 8) * (heads // 4), quarter)
    state = jnp.zeros((16, quarter), F32)
    for k in range(CHIPS):
        before[k] = state.astype(BF16)
        if k < CHIPS - 1:
            state = decays[k : k + 1, :] * state + got[k].astype(F32)

    def start3(d):
        back_copy(chip, lax.rem(chip + d, CHIPS)).start()

    def wait3(d):
        of = lax.rem(chip + d, CHIPS)
        back_copy(of, of).wait_recv()
        back_copy(chip, of).wait_send()

    run(start3, 1, CHIPS)
    entering[rows, columns] = before[chip]
    if hops == 3:
        pass_on(2)
    run(within_tile, tiles // 2, tiles)
    run(wait3, 1, CHIPS)

    for_first = entering[...]
    for_second = (decay0 * for_first.astype(F32) + state0).astype(BF16)
    theirs[...] = jnp.where(is_first, for_second, for_first)
    back = pltpu.make_async_remote_copy(theirs, landed, pair_send.at[2], pair_recv.at[2], device(partner), MESH)
    back.start()
    mine[...] = jnp.where(is_first, for_first, for_second)
    run(lambda j: finish_tile(mine_tile + j, mine[:, tile_columns(j)]), 0, tiles // 2)
    back.wait()
    run(lambda j: finish_tile(other_tile + j, landed[:, tile_columns(j)]), 0, tiles // 2)
    stores = []
    for k, width in enumerate(outs):
        start = sum(outs[:k])
        store = pltpu.make_async_copy(out_ref.at[:, start : start + width], out_refs[k], out_sems.at[k])
        store.start()
        stores.append(store)
    hop(hops - 1).wait_recv()
    last = pltpu.make_async_copy(relay_slots.at[hops - 1], relay_out, out_sems.at[len(outs)])
    last.start()
    for k in range(hops):
        hop(k).wait_send()
    for store in stores + [last]:
        store.wait()


def group(first, pieces, xs, halo, vec, maps, step, relay, hops, outs, collective_id):
    features = sum(pieces)
    half, quarter = features // 2, features // 4
    corner = lambda i: (0, 0)
    dma = pltpu.SemaphoreType.DMA
    vmem = pltpu.VMEM
    return pl.pallas_call(
        functools.partial(group_kernel, first, pieces, hops, outs),
        out_shape=[jax.ShapeDtypeStruct((ROWS, columns), BF16) for columns in outs]
        + [jax.ShapeDtypeStruct(relay.shape, BF16)],
        grid=(1,),
        in_specs=[pl.BlockSpec(memory_space=pl.ANY)] * len(pieces)
        + [
            pl.BlockSpec((HALO, features), corner),
            pl.BlockSpec((vec.shape[0], features), corner),
            pl.BlockSpec((ROWS, 2 * STATE), corner),
            pl.BlockSpec((STEP_ROWS, HEADS), corner),
            pl.BlockSpec(memory_space=pl.ANY),
        ],
        out_specs=[pl.BlockSpec(memory_space=pl.ANY)] * (len(outs) + 1),
        scratch_shapes=[
            vmem((hops,) + relay.shape, BF16),
            dma((hops,)),
            dma((hops,)),
            vmem((ROWS, features), BF16),
            dma((len(outs) + 1,)),
            vmem((ROWS, features), BF16),
            dma((len(pieces),)),
            vmem((HEADS, ROWS), F32),
            vmem((HEADS, ROWS), F32),
            vmem((HEADS, ROWS), F32),
            vmem((HEADS, ROWS), F32),
            vmem((HEADS, 128), F32),
            vmem((8, HEADS), F32),
            vmem((ROWS, 128), F32),
            vmem((ROWS, ROWS), F32),
            vmem((STATE, ROWS), BF16),
            vmem((ROWS, features), BF16),
            vmem((ROWS, features), F32),
            vmem((STATE, features), BF16),
            vmem((STATE, half), BF16),
            vmem((8, HEADS), F32),
            vmem((STATE, half), BF16),
            vmem((8, HEADS), F32),
            vmem((CHIPS, 16, quarter), BF16),
            vmem((CHIPS, 8, HEADS), F32),
            vmem((CHIPS, 16, quarter), BF16),
            vmem((STATE, half), BF16),
            vmem((STATE, half), BF16),
            vmem((STATE, half), BF16),
            vmem((STATE, half), BF16),
            dma((3,)),
            dma((3,)),
            dma((CHIPS,)),
            dma((CHIPS,)),
            dma((CHIPS,)),
            dma((CHIPS,)),
            dma((CHIPS,)),
            dma((CHIPS,)),
        ],
        compiler_params=pltpu.CompilerParams(
            collective_id=collective_id, has_side_effects=True, vmem_limit_bytes=VMEM_LIMIT
        ),
        cost_estimate=pl.CostEstimate(
            flops=ROWS * features, bytes_accessed=ROWS * features, transcendentals=0
        ),
        name="group",
    )(*xs, halo, vec, maps, step, relay)


def widen_kernel(*refs):
    parts, out, sems = refs[:-2], refs[-2], refs[-1]
    start = out.shape[1] - sum(part.shape[1] for part in parts)
    copies = []
    for k, part in enumerate(parts):
        copies.append(pltpu.make_async_copy(part, out.at[:, start : start + part.shape[1]], sems.at[k]))
        start += part.shape[1]
    for copy in copies:
        copy.start()
    for copy in copies:
        copy.wait()


def widen(parts, width):
    return pl.pallas_call(
        widen_kernel,
        in_specs=[pl.BlockSpec(memory_space=pltpu.VMEM)] * len(parts),
        out_specs=pl.BlockSpec(memory_space=pl.ANY),
        out_shape=jax.ShapeDtypeStruct((ROWS, width), BF16),
        scratch_shapes=[pltpu.SemaphoreType.DMA((len(parts),))],
        cost_estimate=pl.CostEstimate(flops=1, bytes_accessed=ROWS * width * 2, transcendentals=0),
        name="widen",
    )(*parts)


def moved(array, by):
    peers = lax.axis_size("pipe")
    return lax.ppermute(array, "pipe", [(i, (i + by) % peers) for i in range(peers)])


def shards(
    incoming, norm_gain, proj_state, proj_step, conv_weight, decay_rate, step_bias, skip_gain, out_gain
):
    x = incoming[0]
    features = x.shape[1]
    home, back, away = HEADS_HOME * HEAD, HEADS_BACK * HEAD, HEADS_AWAY * HEAD
    early, late, round_ = HEADS_EARLY * HEAD, HEADS_LATE * HEAD, HEADS_ROUND * HEAD

    maps, step, vec, vec_away, halo, halo_away, x_early, x_late, x_round = project(
        x, proj_state[0], proj_step[0], norm_gain, conv_weight[0], out_gain, step_bias, decay_rate, skip_gain,
        (early, late, round_), 2,
    )
    x_late, vec_away, halo_away = moved(x_late, 1), moved(vec_away, 1), moved(halo_away, 1)
    maps_away, step_away = moved(maps, 1), moved(step, 1)

    rows, rows_back, x_round = group(
        0, (home,), (x,), halo, vec, maps, step, x_round, 2, (home - back, back), 0
    )
    rows, x_late, halo_away, vec_away, maps_away, step_away = lax.optimization_barrier(
        (rows, x_late, halo_away, vec_away, maps_away, step_away)
    )
    rows_in = moved(rows, 1)

    rows_away, rows_back = group(
        HEADS_HOME, (early, late, round_), (x_early, x_late, x_round), halo_away, vec_away, maps_away, step_away,
        rows_back, 3, (away,), 1,
    )
    passed = widen((rows_back, rows_away), features)
    return lax.dynamic_update_slice(passed, rows_in, (0, 0))[None]


def solution(mesh):
    return jax.shard_map(
        shards,
        mesh=mesh,
        in_specs=(
            P("pipe", "ctx", None),
            P("pipe", None),
            P("pipe", None, None),
            P("pipe", None, None),
            P("pipe", None, None),
            P("pipe", None),
            P("pipe", None),
            P("pipe", None),
            P("pipe", None),
        ),
        out_specs=P("pipe", "ctx", None),
        check_vma=False,
    )
```

```python
import functools

import jax
import jax.numpy as jnp
from jax import lax
from jax.experimental import pallas as pl
from jax.experimental.pallas import tpu as pltpu
from jax.sharding import PartitionSpec as P

MESH = pl.DeviceIdType.MESH
F32 = jnp.float32
BF16 = jnp.bfloat16

ROWS = 256
STATE = 128
HEADS = 128
HEAD = 64
CONV = 4
HALO = 8
TILE = 512
CHUNK = 2048
CHIPS = 16
BATCHES = 2
LOG2E = 1.4426950408889634
epsilon = 1e-05
VMEM_LIMIT = 56 * 1024 * 1024

HEADS_HOME = 64
HEADS_BACK = 12
HEADS_EARLY = 12
HEADS_ROUND = 12
HEADS_AWAY = HEADS - HEADS_HOME
HEADS_LATE = HEADS_AWAY - HEADS_EARLY - HEADS_ROUND


def dot(a, b):
    return jnp.dot(a, b, preferred_element_type=F32)


def three_parts(x):
    first = x.astype(BF16)
    rest = x - first.astype(F32)
    second = rest.astype(BF16)
    return first, second, (rest - second.astype(F32)).astype(BF16)


def spreader(rows, width):
    head = lax.broadcasted_iota(jnp.int32, (2 * rows, width), 0) % rows
    feature = lax.broadcasted_iota(jnp.int32, (2 * rows, width), 1) // HEAD
    return (head == feature).astype(F32).astype(BF16)


def spread_heads(values, width):
    high = values.astype(BF16).astype(F32)
    both = jnp.concatenate([high, values - high], axis=0).astype(BF16)
    return lax.dot_general(
        both, spreader(values.shape[0], width), (((0,), (0,)), ((), ())), preferred_element_type=F32
    )


def project_kernel(
    first,
    x_ref,
    ws_ref,
    wt_ref,
    gain_ref,
    conv_ref,
    out_gain_ref,
    bias_ref,
    rate_ref,
    skip_ref,
    maps_ref,
    step_ref,
    step_away_ref,
    vec_ref,
    halo_ref,
    halo_away_ref,
    vec_away_ref,
    early_ref,
    late_ref,
    round_ref,
    x,
    ws,
    wt,
    edge,
    x_sems,
    w_sems,
    send,
    recv,
    late_sem,
):
    features = x.shape[1]
    away = vec_away_ref.shape[1]
    chunks = features // CHUNK
    me = lax.axis_index("ctx")
    peers = lax.axis_size("ctx")
    after, ahead = lax.rem(me + 1, peers), lax.rem(me + peers - 1, peers)
    section = lax.axis_index("pipe")
    sections = lax.axis_size("pipe")
    behind, beyond = lax.rem(section + sections - 1, sections), lax.rem(section + 1, sections)

    barrier = pltpu.get_barrier_semaphore()
    for other in (after, ahead):
        pl.semaphore_signal(barrier, inc=1, device_id={"ctx": other}, device_id_type=MESH)
    for other in (behind, beyond):
        pl.semaphore_signal(barrier, inc=1, device_id={"pipe": other}, device_id_type=MESH)

    def part(k):
        return slice(k * CHUNK, (k + 1) * CHUNK)

    x_loads = [pltpu.make_async_copy(x_ref.at[:, part(k)], x.at[:, part(k)], x_sems.at[k]) for k in range(chunks)]
    w_loads = [
        (
            pltpu.make_async_copy(ws_ref.at[part(k), :], ws.at[part(k), :], w_sems.at[2 * k]),
            pltpu.make_async_copy(wt_ref.at[part(k), :], wt.at[part(k), :], w_sems.at[2 * k + 1]),
        )
        for k in range(chunks)
    ]
    second = first + early_ref.shape[1]
    third = second + late_ref.shape[1]
    early_copy = pltpu.make_async_remote_copy(
        x_ref.at[:, first:second], early_ref, send.at[0], recv.at[0], {"pipe": beyond}, MESH
    )
    round_copy = pltpu.make_async_remote_copy(
        x_ref.at[:, third:], round_ref, send.at[1], recv.at[1], {"pipe": behind}, MESH
    )
    edge_copy = pltpu.make_async_remote_copy(
        x_ref.at[ROWS - 16 :, :], edge, send.at[2], recv.at[2], {"ctx": after}, MESH
    )
    vec_copy = pltpu.make_async_remote_copy(
        vec_ref.at[:, first:], vec_away_ref, send.at[3], recv.at[3], {"pipe": beyond}, MESH
    )
    late_copy = pltpu.make_async_copy(x.at[:, second:third], late_ref, late_sem)

    for load in x_loads:
        load.start()
    for pair in w_loads:
        for load in pair:
            load.start()
    pl.semaphore_wait(barrier, 4)
    early_copy.start()
    round_copy.start()
    edge_copy.start()

    vec_ref[:4, :] = conv_ref[...]
    vec_ref[4:5, :] = gain_ref[...]
    vec_ref[5:6, :] = out_gain_ref[...]
    vec_ref[6:8, :] = jnp.zeros((2, features), F32)
    vec_copy.start()

    total = jnp.zeros((ROWS, 128), F32)
    for k in range(chunks):
        x_loads[k].wait()
        for i in range(k * CHUNK, (k + 1) * CHUNK, 512):
            square = x[:, i : i + 512].astype(F32)
            square = square * square
            total = total + (square[:, :128] + square[:, 128:256]) + (square[:, 256:384] + square[:, 384:])
    late_copy.start()
    scale = lax.rsqrt(jnp.sum(total, axis=-1, keepdims=True) * (1.0 / features) + epsilon)

    maps = jnp.zeros((ROWS, 2 * STATE), F32)
    step = jnp.zeros((ROWS, HEADS), F32)
    for k in range(chunks):
        for load in w_loads[k]:
            load.wait()
        normed = (x[:, part(k)].astype(F32) * scale * gain_ref[:, part(k)]).astype(BF16)
        maps = maps + dot(normed, ws[part(k), :])
        step = step + dot(normed, wt[part(k), :])
    maps_ref[...] = maps.astype(BF16)
    step = jax.nn.softplus(step + bias_ref[...]).T
    flat = jnp.broadcast_to(scale, (ROWS, 128)).T[:1, :]
    home = step_ref.shape[0] - 8
    for ref, start, stop in ((step_ref, 0, home), (step_away_ref, home, HEADS)):
        ref[: stop - start, :] = step[start:stop, :]
        pad = jnp.zeros((1, ROWS - (stop - start)), F32)
        rate = jnp.concatenate([rate_ref[:, start:stop], pad], axis=1)
        skip = jnp.concatenate([skip_ref[:, start:stop], pad], axis=1)
        ref[stop - start :, :] = jnp.concatenate([flat, rate, skip, jnp.zeros((5, ROWS), F32)], axis=0)

    edge_copy.wait()
    rows = edge[...].astype(F32)[16 - HALO :, :]
    meansq = jnp.sum(rows * rows, axis=-1, keepdims=True) * (1.0 / features)
    rows = rows * lax.rsqrt(meansq + epsilon) * gain_ref[...]
    rows = jnp.where(me == 0, jnp.zeros_like(rows), rows).astype(BF16)
    halo_ref[...] = rows
    halo_away_ref[...] = rows[:, features - away :]
    late_copy.wait()
    vec_copy.wait()
    early_copy.wait()
    round_copy.wait()


def project(x, proj_state, proj_step, gain, conv, out_gain, bias, rate, skip, widths, collective_id):
    features = x.shape[1]
    away = sum(widths)
    chunks = features // CHUNK
    any_ = pl.BlockSpec(memory_space=pl.ANY)
    vmem = pl.BlockSpec(memory_space=pltpu.VMEM)
    dma = pltpu.SemaphoreType.DMA
    return pl.pallas_call(
        functools.partial(project_kernel, features - away),
        in_specs=[any_] * 3 + [vmem] * 6,
        out_specs=[vmem] * 6 + [any_] * 4,
        out_shape=[
            jax.ShapeDtypeStruct((ROWS, 2 * STATE), BF16),
            jax.ShapeDtypeStruct((HEADS - away // HEAD + 8, ROWS), F32),
            jax.ShapeDtypeStruct((away // HEAD + 8, ROWS), F32),
            jax.ShapeDtypeStruct((8, features), F32),
            jax.ShapeDtypeStruct((HALO, features), BF16),
            jax.ShapeDtypeStruct((HALO, away), BF16),
            jax.ShapeDtypeStruct((8, away), F32),
        ]
        + [jax.ShapeDtypeStruct((ROWS, columns), BF16) for columns in widths],
        scratch_shapes=[
            pltpu.VMEM(x.shape, BF16),
            pltpu.VMEM(proj_state.shape, BF16),
            pltpu.VMEM(proj_step.shape, BF16),
            pltpu.VMEM((16, features), BF16),
            dma((chunks,)),
            dma((2 * chunks,)),
            dma((4,)),
            dma((4,)),
            dma,
        ],
        compiler_params=pltpu.CompilerParams(
            vmem_limit_bytes=VMEM_LIMIT, collective_id=collective_id, has_side_effects=True
        ),
        cost_estimate=pl.CostEstimate(
            flops=2 * ROWS * features * 3 * STATE, bytes_accessed=36 << 20, transcendentals=0
        ),
        name="project",
    )(x, proj_state, proj_step, gain, conv, out_gain, bias, rate, skip)


def group_kernel(pieces, hops, outs, *refs):
    refs = list(refs)

    def take(n):
        taken = refs[:n]
        del refs[:n]
        return taken

    x_refs = take(len(pieces))
    shared = take(4)
    relay_in = take(1)[0]
    out_refs = take(len(outs))
    relay_out = take(1)[0]
    group_body(pieces, hops, outs, x_refs, *shared, relay_in, out_refs, relay_out, *refs)


def group_body(
    pieces,
    hops,
    outs,
    x_refs,
    halo_ref,
    vec_ref,
    maps_ref,
    step_ref,
    relay_in,
    out_refs,
    relay_out,
    relay_slots,
    relay_send,
    relay_recv,
    out_ref,
    out_sems,
    x_ref,
    x_sems,
    cum_heads,
    weight_heads,
    enter_heads,
    skip_heads,
    pair_heads,
    chip_heads,
    closing,
    scale,
    scores,
    write_flat,
    inner_ref,
    within_ref,
    fresh,
    peer,
    peer_closing,
    total,
    total_closing,
    got,
    got_closing,
    before,
    entering,
    mine,
    theirs,
    landed,
    pair_send,
    pair_recv,
    send1,
    recv1,
    send2,
    recv2,
    send3,
    recv3,
):
    features = x_ref.shape[1]
    heads = features // HEAD
    batch = features // BATCHES
    half, quarter = batch // 2, batch // 4
    batch_tiles = batch // TILE
    half_tiles = batch_tiles // 2
    in_tile = TILE // HEAD
    me = lax.axis_index("ctx")
    core = lax.rem(me, 2)
    chip = me // 2
    partner = chip * 2 + (1 - core)

    def device(index):
        return {"ctx": index}

    section = lax.axis_index("pipe")
    sections = lax.axis_size("pipe")
    behind, ahead = lax.rem(section + sections - 1, sections), lax.rem(section + 1, sections)

    def hop(k):
        source = relay_in if k == 0 else relay_slots.at[k - 1]
        return pltpu.make_async_remote_copy(
            source, relay_slots.at[k], relay_send.at[k], relay_recv.at[k], {"pipe": behind}, MESH
        )

    def pass_on(k):
        if k > 0:
            hop(k - 1).wait_recv()
        hop(k).start()

    def tile_columns(i):
        return pl.ds(pl.multiple_of(i * TILE, TILE), TILE)

    def tile_heads(i):
        return pl.ds(pl.multiple_of(i * in_tile, in_tile), in_tile)

    barrier = pltpu.get_barrier_semaphore()
    pl.semaphore_signal(barrier, inc=1, device_id=device(partner), device_id_type=MESH)

    def greet(d, carry):
        other = lax.rem(chip + d, CHIPS) * 2 + core
        pl.semaphore_signal(barrier, inc=1, device_id=device(other), device_id_type=MESH)
        return carry

    lax.fori_loop(1, CHIPS, greet, 0)
    for other in (behind, ahead):
        pl.semaphore_signal(barrier, inc=1, device_id={"pipe": other}, device_id_type=MESH)

    loads = []
    for k, width in enumerate(pieces):
        start = sum(pieces[:k])
        load = pltpu.make_async_copy(
            x_refs[k].at[:, :width], x_ref.at[:, start : start + width], x_sems.at[k]
        )
        load.start()
        loads.append(load)

    step = step_ref[:heads, :]
    extra = step_ref[heads:, :].T
    log_decay = -step * extra[:heads, 1:2]
    row = lax.broadcasted_iota(jnp.int32, (ROWS, ROWS), 0)
    column = lax.broadcasted_iota(jnp.int32, (ROWS, ROWS), 1)
    upper = (row <= column).astype(F32).astype(BF16)
    part1, part2, part3 = three_parts(log_decay)
    cumulative = dot(part3, upper) + dot(part2, upper) + dot(part1, upper)
    last = cumulative[:, ROWS - 1 :]
    cum_heads[...] = cumulative * LOG2E
    weight_heads[...] = jnp.exp(last - cumulative) * step
    enter_heads[...] = jnp.exp(cumulative)
    closing[...] = jnp.concatenate(
        [jnp.broadcast_to(last, (heads, 128)), jnp.zeros((HEADS - heads, 128), F32)], axis=0
    ).T[:8, :]
    skip_heads[...] = jnp.broadcast_to(extra[:heads, 2:3], (heads, 128))
    scale[...] = jnp.broadcast_to(extra[:, 0:1], (ROWS, 128))
    write_flat[...] = maps_ref[:, :STATE].astype(F32).T.astype(BF16)

    for load in loads:
        load.wait()

    def fresh_tile(i):
        columns = tile_columns(i)
        normed = (x_ref[:, columns].astype(F32) * scale[:, :1] * vec_ref[4:5, columns]).astype(BF16)
        normed = jnp.concatenate([halo_ref[:, columns].astype(F32), normed.astype(F32)], axis=0)
        shifted = pltpu.roll(normed, 1, 0)
        early = vec_ref[1:2, columns] * normed + vec_ref[0:1, columns] * shifted
        conv = vec_ref[3:4, columns] * normed[HALO:] + vec_ref[2:3, columns] * shifted[HALO:]
        conv = conv + pltpu.roll(early, 2, 0)[HALO:]
        conv = conv * 0.5
        inner = (conv + conv * jnp.tanh(conv)).astype(BF16)
        inner_ref[:, columns] = inner
        spread = spread_heads(weight_heads[tile_heads(i), :], TILE)
        weighted = (inner.astype(F32) * spread).astype(BF16)
        fresh[:, columns] = dot(write_flat[...], weighted).astype(BF16)

    def within_tile(i):
        columns = tile_columns(i)
        inner = inner_ref[:, columns].astype(F32)
        stepped = (inner * spread_heads(step_ref[tile_heads(i), :], TILE)).astype(BF16)
        cum = cum_heads[tile_heads(i), :]
        cum_columns = cum.T
        top, bottom = scores[:128, :128], scores[128:, :]
        lane = lax.broadcasted_iota(jnp.int32, (ROWS, 128), 1)
        for pair in range(TILE // 128):
            values = stepped[:, pair * 128 : (pair + 1) * 128]
            upper = lower = None
            for side in range(2):
                h = pair * 2 + side
                column = cum_columns[:, h : h + 1]
                row = cum[h : h + 1, :]
                own = jnp.where((lane >= HEAD) == (side == 1), values, jnp.zeros_like(values))
                mix0 = (jnp.exp2(jnp.minimum(column[:128] - row[:, :128], 0.0)) * top).astype(BF16)
                mix1 = (jnp.exp2(jnp.minimum(column[128:] - row, 0.0)) * bottom).astype(BF16)
                up, low = dot(mix0, own[:128]), dot(mix1, own)
                upper = up if upper is None else upper + up
                lower = low if lower is None else lower + low
            at = pl.ds(pl.multiple_of(i * TILE + pair * 128, 128), 128)
            within_ref[:128, at] = upper
            within_ref[128:, at] = lower

    def finish_tile(i, state):
        columns = tile_columns(i)
        inner = inner_ref[:, columns].astype(F32)
        carried = dot(maps_ref[:, STATE:], state) * spread_heads(enter_heads[tile_heads(i), :], TILE)
        skip = spread_heads(skip_heads[tile_heads(i), :8], TILE)[0:1, :]
        output = within_ref[:, columns] + carried + skip * inner
        square = (output * output).astype(BF16)
        a = lax.broadcasted_iota(jnp.int32, (256, 256), 0) // HEAD
        b = lax.broadcasted_iota(jnp.int32, (256, 256), 1) // HEAD
        same = (a == b).astype(F32).astype(BF16)
        sums = jnp.concatenate(
            [dot(square[:, k * 256 : (k + 1) * 256], same) for k in range(TILE // 256)], axis=1
        )
        normed = output * lax.rsqrt(sums * (1.0 / HEAD) + epsilon)
        out_ref[:, columns] = (x_ref[:, columns].astype(F32) + normed * vec_ref[5:6, columns]).astype(BF16)

    def run(body, start, stop):
        def one(i, carry):
            body(i)
            return carry

        lax.fori_loop(start, stop, one, 0)

    is_first = core == 0

    def columns_of(b, which, width):
        return pl.ds(pl.multiple_of(b * batch + which * width, 128), width)

    def half_tile(b, which, j):
        return b * batch_tiles + which * half_tiles + j

    def place(of):
        return (
            pl.ds(pl.multiple_of(lax.rem(of, 8) * 16, 16), 16),
            pl.ds(pl.multiple_of((of // 8) * quarter, 128), quarter),
        )

    def pair_copy(b):
        return pltpu.make_async_remote_copy(
            fresh.at[:, columns_of(b, 1 - core, half)], peer.at[b], pair_send.at[b], pair_recv.at[b], device(partner), MESH
        )

    def back_pair_copy(b):
        return pltpu.make_async_remote_copy(
            theirs.at[b], landed.at[b], pair_send.at[BATCHES + b], pair_recv.at[BATCHES + b], device(partner), MESH
        )

    closing_pair_copy = pltpu.make_async_remote_copy(
        closing, peer_closing, pair_send.at[2 * BATCHES], pair_recv.at[2 * BATCHES], device(partner), MESH
    )

    def own_states(b):
        own = fresh[:, columns_of(b, core, half)].astype(F32)
        other = peer[b].astype(F32)
        return jnp.where(is_first, own, other), jnp.where(is_first, other, own)

    def pair_decays(b):
        first = pl.multiple_of((b * batch + core * half) // HEAD, 8)
        return spread_heads(pair_heads[pl.ds(first, half // HEAD), :16], half)

    def combine(b):
        state0, state1 = own_states(b)
        total[b] = (pair_decays(b)[8:9, :] * state0 + state1).astype(BF16)

    def state_copy(b, to):
        rows, columns = place(to)
        return pltpu.make_async_remote_copy(
            total.at[b, rows, columns], got.at[b, chip], send1.at[b], recv1.at[b], device(to * 2 + core), MESH
        )

    def closing_copy(to):
        return pltpu.make_async_remote_copy(
            total_closing, got_closing.at[chip], send2, recv2, device(to * 2 + core), MESH
        )

    def back_copy(b, to):
        rows, columns = place(chip)
        return pltpu.make_async_remote_copy(
            before.at[b, to], entering.at[b, rows, columns], send3.at[b], recv3.at[b], device(to * 2 + core), MESH
        )

    def send_states(b):
        def one(d):
            to = lax.rem(chip + d, CHIPS)
            if b == 0:
                closing_copy(to).start()
            state_copy(b, to).start()

        run(one, 1, CHIPS)
        rows, columns = place(chip)
        got[b, chip] = total[b, rows, columns]

    def all_of(ref, send, recv):
        pieces = ref.at[: CHIPS - 1]
        return pltpu.make_async_remote_copy(pieces, pieces, send, recv, device(partner), MESH)

    def scan_states(b):
        all_of(got.at[b], send1.at[b], recv1.at[b]).wait_recv()
        if b == 0:
            all_of(got_closing, send2, recv2).wait_recv()
            chip_heads[:, :CHIPS] = jnp.exp(got_closing[:, 0, :]).T
        first = pl.multiple_of((b * batch + core * half) // HEAD + (chip // 8) * (quarter // HEAD), 8)
        decays = spread_heads(chip_heads[pl.ds(first, quarter // HEAD), :CHIPS], quarter)
        state = jnp.zeros((16, quarter), F32)
        for k in range(CHIPS):
            before[b, k] = state.astype(BF16)
            if k < CHIPS - 1:
                state = decays[k : k + 1, :] * state + got[b, k].astype(F32)

    def send_back(b):
        run(lambda d: back_copy(b, lax.rem(chip + d, CHIPS)).start(), 1, CHIPS)
        rows, columns = place(chip)
        entering[b, rows, columns] = before[b, chip]

    def take_back(b):
        all_of(before.at[b], send3.at[b], recv3.at[b]).wait_recv()
        for_first = entering[b]
        for_second = (pair_decays(b)[0:1, :] * for_first.astype(F32) + own_states(b)[0]).astype(BF16)
        theirs[b] = jnp.where(is_first, for_second, for_first)
        back_pair_copy(b).start()
        mine[b] = jnp.where(is_first, for_first, for_second)

    def finish_half(b, which, states):
        run(lambda j: finish_tile(half_tile(b, which, j), states[b, :, tile_columns(j)]), 0, half_tiles)

    def fresh_half(b, which):
        run(lambda j: fresh_tile(half_tile(b, which, j)), 0, half_tiles)

    cuts = sorted({0, batch, *(sum(outs[: k + 1]) for k in range(len(outs)))})
    stores = []
    for n, (start, stop) in enumerate(zip(cuts, cuts[1:])):
        k = sum(sum(outs[: i + 1]) <= start for i in range(len(outs)))
        at = start - sum(outs[:k])
        stores.append(
            pltpu.make_async_copy(
                out_ref.at[:, start:stop], out_refs[k].at[:, at : at + stop - start], out_sems.at[n]
            )
        )

    fresh_half(0, 1 - core)
    pl.semaphore_wait(barrier, CHIPS + 2)
    pair_copy(0).start()
    pass_on(0)
    closing_pair_copy.start()
    fresh_half(0, core)
    fresh_half(1, 1 - core)
    pair_copy(1).start()
    closing_pair_copy.wait()
    closing0 = jnp.where(is_first, closing[...], peer_closing[...])
    closing1 = jnp.where(is_first, peer_closing[...], closing[...])
    pair_heads[:, :16] = jnp.exp(jnp.concatenate([closing0, closing1], axis=0)).T
    total_closing[...] = closing0 + closing1
    got_closing[chip] = total_closing[...]
    pair_copy(0).wait()
    combine(0)
    send_states(0)
    fresh_half(1, core)
    pair_copy(1).wait()
    combine(1)
    send_states(1)
    if hops == 3:
        pass_on(1)
    scores[...] = jnp.where(row >= column, dot(maps_ref[:, STATE:], write_flat[...]), 0.0)
    run(within_tile, 0, batch_tiles)
    scan_states(0)
    send_back(0)
    if hops == 2:
        pass_on(1)
    run(within_tile, batch_tiles, batch_tiles + half_tiles)
    scan_states(1)
    send_back(1)
    if hops == 3:
        pass_on(2)
    run(within_tile, batch_tiles + half_tiles, 2 * batch_tiles)
    take_back(0)
    finish_half(0, core, mine)
    back_pair_copy(0).wait()
    finish_half(0, 1 - core, landed)
    stores[0].start()
    take_back(1)
    finish_half(1, core, mine)
    back_pair_copy(1).wait()
    finish_half(1, 1 - core, landed)
    for store in stores[1:]:
        store.start()
    all_of(got_closing, send2, recv2).wait_send()
    for b in range(BATCHES):
        all_of(got.at[b], send1.at[b], recv1.at[b]).wait_send()
        all_of(before.at[b], send3.at[b], recv3.at[b]).wait_send()
    hop(hops - 1).wait_recv()
    last = pltpu.make_async_copy(relay_slots.at[hops - 1], relay_out, out_sems.at[len(outs) + 1])
    last.start()
    for k in range(hops):
        hop(k).wait_send()
    for store in stores + [last]:
        store.wait()


def group(pieces, xs, halo, vec, maps, step, relay, hops, outs, collective_id):
    features = sum(pieces)
    heads = features // HEAD
    half, quarter = features // BATCHES // 2, features // BATCHES // 4
    corner = lambda i: (0, 0)
    dma = pltpu.SemaphoreType.DMA
    vmem = pltpu.VMEM
    return pl.pallas_call(
        functools.partial(group_kernel, pieces, hops, outs),
        out_shape=[jax.ShapeDtypeStruct((ROWS, columns), BF16) for columns in outs]
        + [jax.ShapeDtypeStruct(array.shape, array.dtype) for array in (relay,)],
        grid=(1,),
        in_specs=[pl.BlockSpec(memory_space=pl.ANY)] * len(pieces)
        + [
            pl.BlockSpec((HALO, features), corner),
            pl.BlockSpec((vec.shape[0], features), corner),
            pl.BlockSpec((ROWS, 2 * STATE), corner),
            pl.BlockSpec((heads + 8, ROWS), corner),
        ]
        + [pl.BlockSpec(memory_space=pl.ANY)] ,
        out_specs=[pl.BlockSpec(memory_space=pl.ANY)] * (len(outs) + 1),
        scratch_shapes=[
            vmem((hops,) + relay.shape, BF16),
            dma((hops,)),
            dma((hops,)),
            vmem((ROWS, features), BF16),
            dma((len(outs) + 2,)),
            vmem((ROWS, features), BF16),
            dma((len(pieces),)),
            vmem((heads, ROWS), F32),
            vmem((heads, ROWS), F32),
            vmem((heads, ROWS), F32),
            vmem((heads, 128), F32),
            vmem((HEADS, 128), F32),
            vmem((HEADS, 128), F32),
            vmem((8, HEADS), F32),
            vmem((ROWS, 128), F32),
            vmem((ROWS, ROWS), F32),
            vmem((STATE, ROWS), BF16),
            vmem((ROWS, features), BF16),
            vmem((ROWS, features), F32),
            vmem((STATE, features), BF16),
            vmem((BATCHES, STATE, half), BF16),
            vmem((8, HEADS), F32),
            vmem((BATCHES, STATE, half), BF16),
            vmem((8, HEADS), F32),
            vmem((BATCHES, CHIPS, 16, quarter), BF16),
            vmem((CHIPS, 8, HEADS), F32),
            vmem((BATCHES, CHIPS, 16, quarter), BF16),
            vmem((BATCHES, STATE, half), BF16),
            vmem((BATCHES, STATE, half), BF16),
            vmem((BATCHES, STATE, half), BF16),
            vmem((BATCHES, STATE, half), BF16),
            dma((2 * BATCHES + 1,)),
            dma((2 * BATCHES + 1,)),
            dma((BATCHES,)),
            dma((BATCHES,)),
            dma,
            dma,
            dma((BATCHES,)),
            dma((BATCHES,)),
        ],
        compiler_params=pltpu.CompilerParams(
            collective_id=collective_id, has_side_effects=True, vmem_limit_bytes=VMEM_LIMIT
        ),
        cost_estimate=pl.CostEstimate(
            flops=ROWS * features, bytes_accessed=ROWS * features, transcendentals=0
        ),
        name="group",
    )(*xs, halo, vec, maps, step, relay)


def widen_kernel(blocks, *refs):
    parts, out, held, loads, stores = refs[:-4], refs[-4], refs[-3], refs[-2], refs[-1]
    start = out.shape[1] - sum(width for _, _, width in blocks)
    pairs = []
    at = 0
    for k, (part, begin, width) in enumerate(blocks):
        here = held.at[:, at : at + width]
        load = pltpu.make_async_copy(parts[part].at[:, begin : begin + width], here, loads.at[k])
        store = pltpu.make_async_copy(here, out.at[:, start + at : start + at + width], stores.at[k])
        pairs.append((load, store))
        at += width
    for load, _ in pairs:
        load.start()
    for load, store in pairs:
        load.wait()
        store.start()
    for _, store in pairs:
        store.wait()


def widen(parts, width):
    blocks = []
    for k, part in enumerate(parts):
        begin = 0
        while begin < part.shape[1]:
            size = min(1024, part.shape[1] - begin)
            blocks.append((k, begin, size))
            begin += size
    dma = pltpu.SemaphoreType.DMA((len(blocks),))
    return pl.pallas_call(
        functools.partial(widen_kernel, blocks),
        in_specs=[pl.BlockSpec(memory_space=pl.ANY)] * len(parts),
        out_specs=pl.BlockSpec(memory_space=pl.ANY),
        out_shape=jax.ShapeDtypeStruct((ROWS, width), BF16),
        scratch_shapes=[pltpu.VMEM((ROWS, sum(part.shape[1] for part in parts)), BF16), dma, dma],
        compiler_params=pltpu.CompilerParams(vmem_limit_bytes=VMEM_LIMIT),
        cost_estimate=pl.CostEstimate(flops=1, bytes_accessed=ROWS * width * 2, transcendentals=0),
        name="widen",
    )(*parts)


def moved(array, by):
    peers = lax.axis_size("pipe")
    return lax.ppermute(array, "pipe", [(i, (i + by) % peers) for i in range(peers)])


def shards(
    incoming, norm_gain, proj_state, proj_step, conv_weight, decay_rate, step_bias, skip_gain, out_gain
):
    x = incoming[0]
    features = x.shape[1]
    home, back, away = HEADS_HOME * HEAD, HEADS_BACK * HEAD, HEADS_AWAY * HEAD
    early, late, round_ = HEADS_EARLY * HEAD, HEADS_LATE * HEAD, HEADS_ROUND * HEAD

    maps, step, step_away, vec, halo, halo_away, vec_away, x_early, x_late, x_round = project(
        x, proj_state[0], proj_step[0], norm_gain, conv_weight[0], out_gain, step_bias, decay_rate, skip_gain,
        (early, late, round_), 2,
    )
    x_late, halo_away, step_away, maps_away = (moved(a, 1) for a in (x_late, halo_away, step_away, maps))

    rows, rows_back, x_round = group(
        (home,), (x,), halo, vec, maps, step, x_round, 2, (home - back, back), 0
    )
    rows, x_late, halo_away, step_away, maps_away = lax.optimization_barrier(
        (rows, x_late, halo_away, step_away, maps_away)
    )
    rows_in = moved(rows, 1)

    rows_away, rows_back = group(
        (early, late, round_), (x_early, x_late, x_round), halo_away, vec_away, maps_away, step_away,
        rows_back, 3, (away,), 1,
    )
    passed = widen((rows_back, rows_away), features)
    return lax.dynamic_update_slice(passed, rows_in, (0, 0))[None]


def solution(mesh):
    return jax.shard_map(
        shards,
        mesh=mesh,
        in_specs=(
            P("pipe", "ctx", None),
            P("pipe", None),
            P("pipe", None, None),
            P("pipe", None, None),
            P("pipe", None, None),
            P("pipe", None),
            P("pipe", None),
            P("pipe", None),
            P("pipe", None),
        ),
        out_specs=P("pipe", "ctx", None),
        check_vma=False,
    )
```

```python
import functools

import jax
import jax.numpy as jnp
from jax import lax
from jax.experimental import pallas as pl
from jax.experimental.pallas import tpu as pltpu
from jax.sharding import PartitionSpec as P

MESH = pl.DeviceIdType.MESH
F32 = jnp.float32
BF16 = jnp.bfloat16

ROWS = 256
STATE = 128
HEADS = 128
HEAD = 64
CONV = 4
HALO = 8
TILE = 512
CHUNK = 2048
CHIPS = 16
BATCHES = 2
LOG2E = 1.4426950408889634
epsilon = 1e-05
VMEM_LIMIT = 56 * 1024 * 1024

HEADS_HOME = 64
HEADS_BACK = 12
HEADS_EARLY = 12
HEADS_ROUND = 14
HEADS_AWAY = HEADS - HEADS_HOME
HEADS_LATE = HEADS_AWAY - HEADS_EARLY - HEADS_ROUND


def dot(a, b):
    return jnp.dot(a, b, preferred_element_type=F32)


def three_parts(x):
    first = x.astype(BF16)
    rest = x - first.astype(F32)
    second = rest.astype(BF16)
    return first, second, (rest - second.astype(F32)).astype(BF16)


def spreader(rows, width):
    head = lax.broadcasted_iota(jnp.int32, (2 * rows, width), 0) % rows
    feature = lax.broadcasted_iota(jnp.int32, (2 * rows, width), 1) // HEAD
    return (head == feature).astype(F32).astype(BF16)


def spread_heads(values, width):
    high = values.astype(BF16).astype(F32)
    both = jnp.concatenate([high, values - high], axis=0).astype(BF16)
    return lax.dot_general(
        both, spreader(values.shape[0], width), (((0,), (0,)), ((), ())), preferred_element_type=F32
    )


def project_kernel(
    first,
    x_ref,
    ws_ref,
    wt_ref,
    gain_ref,
    conv_ref,
    out_gain_ref,
    bias_ref,
    rate_ref,
    skip_ref,
    maps_ref,
    maps_away_ref,
    step_ref,
    step_away_ref,
    vec_ref,
    vec_away_ref,
    early_ref,
    late_ref,
    round_ref,
    x,
    ws,
    wt,
    edge,
    x_sems,
    w_sems,
    send,
    recv,
    late_sem,
):
    features = x.shape[1]
    away = vec_away_ref.shape[1]
    chunks = features // CHUNK
    me = lax.axis_index("ctx")
    peers = lax.axis_size("ctx")
    after, ahead = lax.rem(me + 1, peers), lax.rem(me + peers - 1, peers)
    section = lax.axis_index("pipe")
    sections = lax.axis_size("pipe")
    behind, beyond = lax.rem(section + sections - 1, sections), lax.rem(section + 1, sections)

    barrier = pltpu.get_barrier_semaphore()
    for other in (after, ahead):
        pl.semaphore_signal(barrier, inc=1, device_id={"ctx": other}, device_id_type=MESH)
    for other in (behind, beyond):
        pl.semaphore_signal(barrier, inc=1, device_id={"pipe": other}, device_id_type=MESH)

    def part(k):
        return slice(k * CHUNK, (k + 1) * CHUNK)

    x_loads = [pltpu.make_async_copy(x_ref.at[:, part(k)], x.at[:, part(k)], x_sems.at[k]) for k in range(chunks)]
    w_loads = [
        (
            pltpu.make_async_copy(ws_ref.at[part(k), :], ws.at[part(k), :], w_sems.at[2 * k]),
            pltpu.make_async_copy(wt_ref.at[part(k), :], wt.at[part(k), :], w_sems.at[2 * k + 1]),
        )
        for k in range(chunks)
    ]
    second = first + early_ref.shape[1]
    third = second + late_ref.shape[1]
    early_copy = pltpu.make_async_remote_copy(
        x_ref.at[:, first:second], early_ref, send.at[0], recv.at[0], {"pipe": beyond}, MESH
    )
    round_copy = pltpu.make_async_remote_copy(
        x_ref.at[:, third:], round_ref, send.at[1], recv.at[1], {"pipe": behind}, MESH
    )
    edge_copy = pltpu.make_async_remote_copy(
        x_ref.at[ROWS - 16 :, :], edge, send.at[2], recv.at[2], {"ctx": after}, MESH
    )
    core = lax.rem(me, 2)
    half = away // 2
    mine = pl.ds(pl.multiple_of(core * half, 128), half)
    vec_copy = pltpu.make_async_remote_copy(
        vec_ref.at[:, pl.ds(pl.multiple_of(first + core * half, 128), half)],
        vec_away_ref.at[:, mine],
        send.at[3],
        recv.at[3],
        {"pipe": beyond},
        MESH,
    )
    vec_pair_copy = pltpu.make_async_remote_copy(
        vec_away_ref.at[:, mine],
        vec_away_ref.at[:, mine],
        send.at[4],
        recv.at[4],
        {"ctx": me + 1 - 2 * core},
        MESH,
    )
    late_copy = pltpu.make_async_copy(x.at[:, second:third], late_ref, late_sem)

    vec_ref[:4, :] = conv_ref[...]
    vec_ref[4:5, :] = gain_ref[...]
    vec_ref[5:6, :] = out_gain_ref[...]
    vec_ref[6:8, :] = jnp.zeros((2, features), F32)
    for load in x_loads:
        load.start()
    for pair in w_loads:
        for load in pair:
            load.start()
    pl.semaphore_wait(barrier, 4)
    vec_copy.start()
    early_copy.start()
    round_copy.start()
    edge_copy.start()

    total = jnp.zeros((ROWS, 128), F32)
    for k in range(chunks):
        x_loads[k].wait()
        for i in range(k * CHUNK, (k + 1) * CHUNK, 512):
            square = x[:, i : i + 512].astype(F32)
            square = square * square
            total = total + (square[:, :128] + square[:, 128:256]) + (square[:, 256:384] + square[:, 384:])
    late_copy.start()
    scale = lax.rsqrt(jnp.sum(total, axis=-1, keepdims=True) * (1.0 / features) + epsilon)

    vec_copy.wait()
    vec_pair_copy.start()

    maps = jnp.zeros((ROWS, 2 * STATE), F32)
    step = jnp.zeros((ROWS, HEADS), F32)
    for k in range(chunks):
        for load in w_loads[k]:
            load.wait()
        normed = (x[:, part(k)].astype(F32) * scale * gain_ref[:, part(k)]).astype(BF16)
        maps = maps + dot(normed, ws[part(k), :])
        step = step + dot(normed, wt[part(k), :])
    for ref in (maps_ref, maps_away_ref):
        ref[:, : 2 * STATE] = maps.astype(BF16)
    step = jax.nn.softplus(step + bias_ref[...]).T
    flat = jnp.broadcast_to(scale, (ROWS, 128)).T[:1, :]
    home = step_ref.shape[0] - 8
    for ref, start, stop in ((step_ref, 0, home), (step_away_ref, home, HEADS)):
        ref[: stop - start, :] = step[start:stop, :]
        pad = jnp.zeros((1, ROWS - (stop - start)), F32)
        rate = jnp.concatenate([rate_ref[:, start:stop], pad], axis=1)
        skip = jnp.concatenate([skip_ref[:, start:stop], pad], axis=1)
        ref[stop - start :, :] = jnp.concatenate([flat, rate, skip, jnp.zeros((5, ROWS), F32)], axis=0)

    edge_copy.wait()
    rows = edge[...].astype(F32)[16 - HALO :, :]
    meansq = jnp.sum(rows * rows, axis=-1, keepdims=True) * (1.0 / features)
    rows = rows * lax.rsqrt(meansq + epsilon) * gain_ref[...]
    rows = jnp.where(me == 0, jnp.zeros_like(rows), rows)
    for ref, start in ((maps_ref, 0), (maps_away_ref, features - away)):
        ref[:, 2 * STATE :] = jnp.concatenate(
            [rows[:, start + i * 128 : start + (i + 1) * 128] for i in range(ROWS // HALO)], axis=0
        ).astype(BF16)
    late_copy.wait()
    vec_pair_copy.wait()
    early_copy.wait()
    round_copy.wait()


def project(x, proj_state, proj_step, gain, conv, out_gain, bias, rate, skip, widths, collective_id):
    features = x.shape[1]
    away = sum(widths)
    chunks = features // CHUNK
    any_ = pl.BlockSpec(memory_space=pl.ANY)
    vmem = pl.BlockSpec(memory_space=pltpu.VMEM)
    dma = pltpu.SemaphoreType.DMA
    return pl.pallas_call(
        functools.partial(project_kernel, features - away),
        in_specs=[any_] * 3 + [vmem] * 6,
        out_specs=[vmem] * 5 + [any_] * 4,
        out_shape=[
            jax.ShapeDtypeStruct((ROWS, 2 * STATE + 128), BF16),
            jax.ShapeDtypeStruct((ROWS, 2 * STATE + 128), BF16),
            jax.ShapeDtypeStruct((HEADS - away // HEAD + 8, ROWS), F32),
            jax.ShapeDtypeStruct((away // HEAD + 8, ROWS), F32),
            jax.ShapeDtypeStruct((8, features), F32),
            jax.ShapeDtypeStruct((8, away), F32),
        ]
        + [jax.ShapeDtypeStruct((ROWS, columns), BF16) for columns in widths],
        scratch_shapes=[
            pltpu.VMEM(x.shape, BF16),
            pltpu.VMEM(proj_state.shape, BF16),
            pltpu.VMEM(proj_step.shape, BF16),
            pltpu.VMEM((16, features), BF16),
            dma((chunks,)),
            dma((2 * chunks,)),
            dma((5,)),
            dma((5,)),
            dma,
        ],
        compiler_params=pltpu.CompilerParams(
            vmem_limit_bytes=VMEM_LIMIT, collective_id=collective_id, has_side_effects=True
        ),
        cost_estimate=pl.CostEstimate(
            flops=2 * ROWS * features * 3 * STATE, bytes_accessed=36 << 20, transcendentals=0
        ),
        name="project",
    )(x, proj_state, proj_step, gain, conv, out_gain, bias, rate, skip)


def group_kernel(pieces, hops, outs, *refs):
    refs = list(refs)

    def take(n):
        taken = refs[:n]
        del refs[:n]
        return taken

    x_refs = take(len(pieces))
    shared = take(3)
    relay_in = take(1)[0]
    out_refs = take(len(outs))
    relay_out = take(1)[0]
    group_body(pieces, hops, outs, x_refs, *shared, relay_in, out_refs, relay_out, *refs)


def group_body(
    pieces,
    hops,
    outs,
    x_refs,
    vec_ref,
    maps_ref,
    step_ref,
    relay_in,
    out_refs,
    relay_out,
    relay_slots,
    relay_send,
    relay_recv,
    out_ref,
    out_sems,
    x_ref,
    x_sems,
    cum_heads,
    weight_heads,
    enter_heads,
    skip_heads,
    pair_heads,
    chip_heads,
    closing,
    scale,
    scores,
    write_flat,
    inner_ref,
    within_ref,
    fresh,
    peer,
    peer_closing,
    total,
    total_closing,
    got,
    got_closing,
    before,
    entering,
    mine,
    theirs,
    landed,
    pair_send,
    pair_recv,
    send1,
    recv1,
    send2,
    recv2,
    send3,
    recv3,
):
    features = x_ref.shape[1]
    heads = features // HEAD
    batch = features // BATCHES
    half, quarter = batch // 2, batch // 4
    batch_tiles = batch // TILE
    half_tiles = batch_tiles // 2
    in_tile = TILE // HEAD
    me = lax.axis_index("ctx")
    core = lax.rem(me, 2)
    chip = me // 2
    partner = chip * 2 + (1 - core)

    def device(index):
        return {"ctx": index}

    section = lax.axis_index("pipe")
    sections = lax.axis_size("pipe")
    behind, ahead = lax.rem(section + sections - 1, sections), lax.rem(section + 1, sections)

    def hop(k):
        source = relay_in if k == 0 else relay_slots.at[k - 1]
        return pltpu.make_async_remote_copy(
            source, relay_slots.at[k], relay_send.at[k], relay_recv.at[k], {"pipe": behind}, MESH
        )

    def pass_on(k):
        if k > 0:
            hop(k - 1).wait_recv()
        hop(k).start()

    def tile_columns(i):
        return pl.ds(pl.multiple_of(i * TILE, TILE), TILE)

    def tile_heads(i):
        return pl.ds(pl.multiple_of(i * in_tile, in_tile), in_tile)

    barrier = pltpu.get_barrier_semaphore()
    pl.semaphore_signal(barrier, inc=1, device_id=device(partner), device_id_type=MESH)

    def greet(d, carry):
        other = lax.rem(chip + d, CHIPS) * 2 + core
        pl.semaphore_signal(barrier, inc=1, device_id=device(other), device_id_type=MESH)
        return carry

    lax.fori_loop(1, CHIPS, greet, 0)
    for other in (behind, ahead):
        pl.semaphore_signal(barrier, inc=1, device_id={"pipe": other}, device_id_type=MESH)

    loads = []
    for k, width in enumerate(pieces):
        start = sum(pieces[:k])
        load = pltpu.make_async_copy(
            x_refs[k].at[:, :width], x_ref.at[:, start : start + width], x_sems.at[k]
        )
        load.start()
        loads.append(load)

    step = step_ref[:heads, :]
    extra = step_ref[heads:, :].T
    log_decay = -step * extra[:heads, 1:2]
    row = lax.broadcasted_iota(jnp.int32, (ROWS, ROWS), 0)
    column = lax.broadcasted_iota(jnp.int32, (ROWS, ROWS), 1)
    upper = (row <= column).astype(F32).astype(BF16)
    part1, part2, part3 = three_parts(log_decay)
    cumulative = dot(part3, upper) + dot(part2, upper) + dot(part1, upper)
    last = cumulative[:, ROWS - 1 :]
    cum_heads[...] = cumulative * LOG2E
    weight_heads[...] = jnp.exp(last - cumulative) * step
    enter_heads[...] = jnp.exp(cumulative)
    closing[...] = jnp.concatenate(
        [jnp.broadcast_to(last, (heads, 128)), jnp.zeros((HEADS - heads, 128), F32)], axis=0
    ).T[:8, :]
    skip_heads[...] = jnp.broadcast_to(extra[:heads, 2:3], (heads, 128))
    scale[...] = jnp.broadcast_to(extra[:, 0:1], (ROWS, 128))
    write_flat[...] = maps_ref[:, :STATE].astype(F32).T.astype(BF16)

    for load in loads:
        load.wait()

    def fresh_tile(i):
        columns = tile_columns(i)
        normed = (x_ref[:, columns].astype(F32) * scale[:, :1] * vec_ref[4:5, columns]).astype(BF16)
        parts = TILE // 128
        halo = maps_ref[pl.ds(pl.multiple_of(i * HALO * parts, HALO * parts), HALO * parts), 2 * STATE :].astype(F32)
        halo = jnp.concatenate([halo[k * HALO : (k + 1) * HALO] for k in range(parts)], axis=1)
        normed = jnp.concatenate([halo, normed.astype(F32)], axis=0)
        shifted = pltpu.roll(normed, 1, 0)
        early = vec_ref[1:2, columns] * normed + vec_ref[0:1, columns] * shifted
        conv = vec_ref[3:4, columns] * normed[HALO:] + vec_ref[2:3, columns] * shifted[HALO:]
        conv = conv + pltpu.roll(early, 2, 0)[HALO:]
        conv = conv * 0.5
        inner = (conv + conv * jnp.tanh(conv)).astype(BF16)
        inner_ref[:, columns] = inner
        spread = spread_heads(weight_heads[tile_heads(i), :], TILE)
        weighted = (inner.astype(F32) * spread).astype(BF16)
        fresh[:, columns] = dot(write_flat[...], weighted).astype(BF16)

    def within_tile(i):
        columns = tile_columns(i)
        inner = inner_ref[:, columns].astype(F32)
        stepped = (inner * spread_heads(step_ref[tile_heads(i), :], TILE)).astype(BF16)
        cum = cum_heads[tile_heads(i), :]
        cum_columns = cum.T
        top, bottom = scores[:128, :128], scores[128:, :]
        lane = lax.broadcasted_iota(jnp.int32, (ROWS, 128), 1)
        for pair in range(TILE // 128):
            values = stepped[:, pair * 128 : (pair + 1) * 128]
            upper = lower = None
            for side in range(2):
                h = pair * 2 + side
                column = cum_columns[:, h : h + 1]
                row = cum[h : h + 1, :]
                own = jnp.where((lane >= HEAD) == (side == 1), values, jnp.zeros_like(values))
                mix0 = (jnp.exp2(jnp.minimum(column[:128] - row[:, :128], 0.0)) * top).astype(BF16)
                mix1 = (jnp.exp2(jnp.minimum(column[128:] - row, 0.0)) * bottom).astype(BF16)
                up, low = dot(mix0, own[:128]), dot(mix1, own)
                upper = up if upper is None else upper + up
                lower = low if lower is None else lower + low
            at = pl.ds(pl.multiple_of(i * TILE + pair * 128, 128), 128)
            within_ref[:128, at] = upper
            within_ref[128:, at] = lower

    def finish_tile(i, state):
        columns = tile_columns(i)
        inner = inner_ref[:, columns].astype(F32)
        carried = dot(maps_ref[:, STATE : 2 * STATE], state) * spread_heads(enter_heads[tile_heads(i), :], TILE)
        skip = spread_heads(skip_heads[tile_heads(i), :8], TILE)[0:1, :]
        output = within_ref[:, columns] + carried + skip * inner
        square = (output * output).astype(BF16)
        a = lax.broadcasted_iota(jnp.int32, (256, 256), 0) // HEAD
        b = lax.broadcasted_iota(jnp.int32, (256, 256), 1) // HEAD
        same = (a == b).astype(F32).astype(BF16)
        sums = jnp.concatenate(
            [dot(square[:, k * 256 : (k + 1) * 256], same) for k in range(TILE // 256)], axis=1
        )
        normed = output * lax.rsqrt(sums * (1.0 / HEAD) + epsilon)
        out_ref[:, columns] = (x_ref[:, columns].astype(F32) + normed * vec_ref[5:6, columns]).astype(BF16)

    def run(body, start, stop):
        def one(i, carry):
            body(i)
            return carry

        lax.fori_loop(start, stop, one, 0)

    is_first = core == 0

    def columns_of(b, which, width):
        return pl.ds(pl.multiple_of(b * batch + which * width, 128), width)

    def half_tile(b, which, j):
        return b * batch_tiles + which * half_tiles + j

    def place(of):
        return (
            pl.ds(pl.multiple_of(lax.rem(of, 8) * 16, 16), 16),
            pl.ds(pl.multiple_of((of // 8) * quarter, 128), quarter),
        )

    def pair_copy(b):
        return pltpu.make_async_remote_copy(
            fresh.at[:, columns_of(b, 1 - core, half)], peer.at[b], pair_send.at[b], pair_recv.at[b], device(partner), MESH
        )

    def back_pair_copy(b):
        return pltpu.make_async_remote_copy(
            theirs.at[b], landed.at[b], pair_send.at[BATCHES + b], pair_recv.at[BATCHES + b], device(partner), MESH
        )

    closing_pair_copy = pltpu.make_async_remote_copy(
        closing, peer_closing, pair_send.at[2 * BATCHES], pair_recv.at[2 * BATCHES], device(partner), MESH
    )

    def own_states(b):
        own = fresh[:, columns_of(b, core, half)].astype(F32)
        other = peer[b].astype(F32)
        return jnp.where(is_first, own, other), jnp.where(is_first, other, own)

    def pair_decays(b):
        first = pl.multiple_of((b * batch + core * half) // HEAD, 8)
        return spread_heads(pair_heads[pl.ds(first, half // HEAD), :16], half)

    def combine(b):
        state0, state1 = own_states(b)
        total[b] = (pair_decays(b)[8:9, :] * state0 + state1).astype(BF16)

    def state_copy(b, to):
        rows, columns = place(to)
        return pltpu.make_async_remote_copy(
            total.at[b, rows, columns], got.at[b, chip], send1.at[b], recv1.at[b], device(to * 2 + core), MESH
        )

    def closing_copy(to):
        return pltpu.make_async_remote_copy(
            total_closing, got_closing.at[chip], send2, recv2, device(to * 2 + core), MESH
        )

    def back_copy(b, to):
        rows, columns = place(chip)
        return pltpu.make_async_remote_copy(
            before.at[b, to], entering.at[b, rows, columns], send3.at[b], recv3.at[b], device(to * 2 + core), MESH
        )

    def send_states(b):
        def one(d):
            to = lax.rem(chip + d, CHIPS)
            if b == 0:
                closing_copy(to).start()
            state_copy(b, to).start()

        for d in range(1, CHIPS):
            one(d)
        rows, columns = place(chip)
        got[b, chip] = total[b, rows, columns]

    def all_of(ref, send, recv):
        pieces = ref.at[: CHIPS - 1]
        return pltpu.make_async_remote_copy(pieces, pieces, send, recv, device(partner), MESH)

    def scan_states(b):
        all_of(got.at[b], send1.at[b], recv1.at[b]).wait_recv()
        if b == 0:
            all_of(got_closing, send2, recv2).wait_recv()
            chip_heads[:, :CHIPS] = jnp.exp(got_closing[:, 0, :]).T
        first = pl.multiple_of((b * batch + core * half) // HEAD + (chip // 8) * (quarter // HEAD), 8)
        decays = spread_heads(chip_heads[pl.ds(first, quarter // HEAD), :CHIPS], quarter)
        state = jnp.zeros((16, quarter), F32)
        for k in range(CHIPS):
            before[b, k] = state.astype(BF16)
            if k < CHIPS - 1:
                state = decays[k : k + 1, :] * state + got[b, k].astype(F32)

    def send_back(b):
        for d in range(1, CHIPS):
            back_copy(b, lax.rem(chip + d, CHIPS)).start()
        rows, columns = place(chip)
        entering[b, rows, columns] = before[b, chip]

    def take_back(b):
        all_of(before.at[b], send3.at[b], recv3.at[b]).wait_recv()
        for_first = entering[b]
        for_second = (pair_decays(b)[0:1, :] * for_first.astype(F32) + own_states(b)[0]).astype(BF16)
        theirs[b] = jnp.where(is_first, for_second, for_first)
        back_pair_copy(b).start()
        mine[b] = jnp.where(is_first, for_first, for_second)

    def finish_half(b, which, states):
        run(lambda j: finish_tile(half_tile(b, which, j), states[b, :, tile_columns(j)]), 0, half_tiles)

    def fresh_half(b, which):
        run(lambda j: fresh_tile(half_tile(b, which, j)), 0, half_tiles)

    cuts = sorted({0, batch, *(sum(outs[: k + 1]) for k in range(len(outs)))})
    stores = []
    for n, (start, stop) in enumerate(zip(cuts, cuts[1:])):
        k = sum(sum(outs[: i + 1]) <= start for i in range(len(outs)))
        at = start - sum(outs[:k])
        stores.append(
            pltpu.make_async_copy(
                out_ref.at[:, start:stop], out_refs[k].at[:, at : at + stop - start], out_sems.at[n]
            )
        )

    fresh_half(0, 1 - core)
    pl.semaphore_wait(barrier, CHIPS + 2)
    pair_copy(0).start()
    pass_on(0)
    closing_pair_copy.start()
    fresh_half(0, core)
    fresh_half(1, 1 - core)
    pair_copy(1).start()
    closing_pair_copy.wait()
    closing0 = jnp.where(is_first, closing[...], peer_closing[...])
    closing1 = jnp.where(is_first, peer_closing[...], closing[...])
    pair_heads[:, :16] = jnp.exp(jnp.concatenate([closing0, closing1], axis=0)).T
    total_closing[...] = closing0 + closing1
    got_closing[chip] = total_closing[...]
    pair_copy(0).wait()
    combine(0)
    send_states(0)
    fresh_half(1, core)
    pair_copy(1).wait()
    combine(1)
    send_states(1)
    if hops == 3:
        pass_on(1)
    scores[...] = jnp.where(row >= column, dot(maps_ref[:, STATE : 2 * STATE], write_flat[...]), 0.0)
    run(within_tile, 0, batch_tiles)
    scan_states(0)
    send_back(0)
    if hops == 2:
        pass_on(1)
    run(within_tile, batch_tiles, batch_tiles + half_tiles)
    scan_states(1)
    send_back(1)
    if hops == 3:
        pass_on(2)
    run(within_tile, batch_tiles + half_tiles, 2 * batch_tiles)
    take_back(0)
    finish_half(0, core, mine)
    back_pair_copy(0).wait()
    finish_half(0, 1 - core, landed)
    stores[0].start()
    take_back(1)
    finish_half(1, core, mine)
    back_pair_copy(1).wait()
    finish_half(1, 1 - core, landed)
    for store in stores[1:]:
        store.start()
    all_of(got_closing, send2, recv2).wait_send()
    for b in range(BATCHES):
        all_of(got.at[b], send1.at[b], recv1.at[b]).wait_send()
        all_of(before.at[b], send3.at[b], recv3.at[b]).wait_send()
    hop(hops - 1).wait_recv()
    last = pltpu.make_async_copy(relay_slots.at[hops - 1], relay_out, out_sems.at[len(outs) + 1])
    last.start()
    for k in range(hops):
        hop(k).wait_send()
    for store in stores + [last]:
        store.wait()


def group(pieces, xs, vec, maps, step, relay, hops, outs, collective_id):
    features = sum(pieces)
    heads = features // HEAD
    half, quarter = features // BATCHES // 2, features // BATCHES // 4
    corner = lambda i: (0, 0)
    dma = pltpu.SemaphoreType.DMA
    vmem = pltpu.VMEM
    return pl.pallas_call(
        functools.partial(group_kernel, pieces, hops, outs),
        out_shape=[jax.ShapeDtypeStruct((ROWS, columns), BF16) for columns in outs]
        + [jax.ShapeDtypeStruct(array.shape, array.dtype) for array in (relay,)],
        grid=(1,),
        in_specs=[pl.BlockSpec(memory_space=pl.ANY)] * len(pieces)
        + [
            pl.BlockSpec((vec.shape[0], features), corner),
            pl.BlockSpec(maps.shape, corner),
            pl.BlockSpec((heads + 8, ROWS), corner),
        ]
        + [pl.BlockSpec(memory_space=pl.ANY)] ,
        out_specs=[pl.BlockSpec(memory_space=pl.ANY)] * (len(outs) + 1),
        scratch_shapes=[
            vmem((hops,) + relay.shape, BF16),
            dma((hops,)),
            dma((hops,)),
            vmem((ROWS, features), BF16),
            dma((len(outs) + 2,)),
            vmem((ROWS, features), BF16),
            dma((len(pieces),)),
            vmem((heads, ROWS), F32),
            vmem((heads, ROWS), F32),
            vmem((heads, ROWS), F32),
            vmem((heads, 128), F32),
            vmem((HEADS, 128), F32),
            vmem((HEADS, 128), F32),
            vmem((8, HEADS), F32),
            vmem((ROWS, 128), F32),
            vmem((ROWS, ROWS), F32),
            vmem((STATE, ROWS), BF16),
            vmem((ROWS, features), BF16),
            vmem((ROWS, features), F32),
            vmem((STATE, features), BF16),
            vmem((BATCHES, STATE, half), BF16),
            vmem((8, HEADS), F32),
            vmem((BATCHES, STATE, half), BF16),
            vmem((8, HEADS), F32),
            vmem((BATCHES, CHIPS, 16, quarter), BF16),
            vmem((CHIPS, 8, HEADS), F32),
            vmem((BATCHES, CHIPS, 16, quarter), BF16),
            vmem((BATCHES, STATE, half), BF16),
            vmem((BATCHES, STATE, half), BF16),
            vmem((BATCHES, STATE, half), BF16),
            vmem((BATCHES, STATE, half), BF16),
            dma((2 * BATCHES + 1,)),
            dma((2 * BATCHES + 1,)),
            dma((BATCHES,)),
            dma((BATCHES,)),
            dma,
            dma,
            dma((BATCHES,)),
            dma((BATCHES,)),
        ],
        compiler_params=pltpu.CompilerParams(
            collective_id=collective_id, has_side_effects=True, vmem_limit_bytes=VMEM_LIMIT
        ),
        cost_estimate=pl.CostEstimate(
            flops=ROWS * features, bytes_accessed=ROWS * features, transcendentals=0
        ),
        name="group",
    )(*xs, vec, maps, step, relay)


def widen_kernel(blocks, *refs):
    parts, out, held, loads, stores = refs[:-4], refs[-4], refs[-3], refs[-2], refs[-1]
    start = out.shape[1] - sum(width for _, _, width in blocks)
    pairs = []
    at = 0
    for k, (part, begin, width) in enumerate(blocks):
        here = held.at[:, at : at + width]
        load = pltpu.make_async_copy(parts[part].at[:, begin : begin + width], here, loads.at[k])
        store = pltpu.make_async_copy(here, out.at[:, start + at : start + at + width], stores.at[k])
        pairs.append((load, store))
        at += width
    for load, _ in pairs:
        load.start()
    for load, store in pairs:
        load.wait()
        store.start()
    for _, store in pairs:
        store.wait()


def widen(parts, width):
    blocks = []
    for k, part in enumerate(parts):
        begin = 0
        while begin < part.shape[1]:
            size = min(1024, part.shape[1] - begin)
            blocks.append((k, begin, size))
            begin += size
    dma = pltpu.SemaphoreType.DMA((len(blocks),))
    return pl.pallas_call(
        functools.partial(widen_kernel, blocks),
        in_specs=[pl.BlockSpec(memory_space=pl.ANY)] * len(parts),
        out_specs=pl.BlockSpec(memory_space=pl.ANY),
        out_shape=jax.ShapeDtypeStruct((ROWS, width), BF16),
        scratch_shapes=[pltpu.VMEM((ROWS, sum(part.shape[1] for part in parts)), BF16), dma, dma],
        compiler_params=pltpu.CompilerParams(vmem_limit_bytes=VMEM_LIMIT),
        cost_estimate=pl.CostEstimate(flops=1, bytes_accessed=ROWS * width * 2, transcendentals=0),
        name="widen",
    )(*parts)


def moved(array, by):
    peers = lax.axis_size("pipe")
    return lax.ppermute(array, "pipe", [(i, (i + by) % peers) for i in range(peers)])


def shards(
    incoming, norm_gain, proj_state, proj_step, conv_weight, decay_rate, step_bias, skip_gain, out_gain
):
    x = incoming[0]
    features = x.shape[1]
    home, back, away = HEADS_HOME * HEAD, HEADS_BACK * HEAD, HEADS_AWAY * HEAD
    early, late, round_ = HEADS_EARLY * HEAD, HEADS_LATE * HEAD, HEADS_ROUND * HEAD

    maps, maps_away, step, step_away, vec, vec_away, x_early, x_late, x_round = project(
        x, proj_state[0], proj_step[0], norm_gain, conv_weight[0], out_gain, step_bias, decay_rate, skip_gain,
        (early, late, round_), 2,
    )
    x_late, step_away, maps_away = (moved(a, 1) for a in (x_late, step_away, maps_away))

    rows, rows_back, x_round = group(
        (home,), (x,), vec, maps, step, x_round, 2, (home - back, back), 0
    )
    rows, x_late, step_away, maps_away = lax.optimization_barrier((rows, x_late, step_away, maps_away))
    rows_in = moved(rows, 1)

    rows_away, rows_back = group(
        (early, late, round_), (x_early, x_late, x_round), vec_away, maps_away, step_away,
        rows_back, 3, (away,), 1,
    )
    passed = widen((rows_back, rows_away), features)
    return lax.dynamic_update_slice(passed, rows_in, (0, 0))[None]


def solution(mesh):
    return jax.shard_map(
        shards,
        mesh=mesh,
        in_specs=(
            P("pipe", "ctx", None),
            P("pipe", None),
            P("pipe", None, None),
            P("pipe", None, None),
            P("pipe", None, None),
            P("pipe", None),
            P("pipe", None),
            P("pipe", None),
            P("pipe", None),
        ),
        out_specs=P("pipe", "ctx", None),
        check_vma=False,
    )
```

```python
import functools

import jax
import jax.numpy as jnp
from jax import lax
from jax.experimental import pallas as pl
from jax.experimental.pallas import tpu as pltpu
from jax.sharding import PartitionSpec as P

MESH = pl.DeviceIdType.MESH
F32 = jnp.float32
BF16 = jnp.bfloat16

ROWS = 256
STATE = 128
HEADS = 128
HEAD = 64
CONV = 4
HALO = 8
TILE = 512
CHUNK = 2048
CHIPS = 16
BATCHES = 2
LOG2E = 1.4426950408889634
epsilon = 1e-05
VMEM_LIMIT = 56 * 1024 * 1024

HEADS_HOME = 64
HEADS_BACK = 12
HEADS_ROUND = 16
HEADS_AWAY = HEADS - HEADS_HOME
HEADS_AHEAD = HEADS_AWAY - HEADS_ROUND


def dot(a, b):
    return jnp.dot(a, b, preferred_element_type=F32)


def three_parts(x):
    first = x.astype(BF16)
    rest = x - first.astype(F32)
    second = rest.astype(BF16)
    return first, second, (rest - second.astype(F32)).astype(BF16)


def spreader(rows, width):
    head = lax.broadcasted_iota(jnp.int32, (2 * rows, width), 0) % rows
    feature = lax.broadcasted_iota(jnp.int32, (2 * rows, width), 1) // HEAD
    return (head == feature).astype(F32).astype(BF16)


def spread_heads(values, width):
    high = values.astype(BF16).astype(F32)
    both = jnp.concatenate([high, values - high], axis=0).astype(BF16)
    return lax.dot_general(
        both, spreader(values.shape[0], width), (((0,), (0,)), ((), ())), preferred_element_type=F32
    )


def project_kernel(
    x_ref,
    ws_ref,
    wt_ref,
    gain_ref,
    conv_ref,
    out_gain_ref,
    bias_ref,
    rate_ref,
    skip_ref,
    maps_ref,
    maps_away_ref,
    step_ref,
    step_away_ref,
    vec_ref,
    vec_away_ref,
    x,
    ws,
    wt,
    edge,
    x_sems,
    w_sems,
    edge_send,
    edge_recv,
):
    features = x.shape[1]
    away = vec_away_ref.shape[1]
    chunks = features // CHUNK
    me = lax.axis_index("ctx")
    peers = lax.axis_size("ctx")
    after, ahead = lax.rem(me + 1, peers), lax.rem(me + peers - 1, peers)

    barrier = pltpu.get_barrier_semaphore()
    for other in (after, ahead):
        pl.semaphore_signal(barrier, inc=1, device_id={"ctx": other}, device_id_type=MESH)

    def part(k):
        return slice(k * CHUNK, (k + 1) * CHUNK)

    x_loads = [pltpu.make_async_copy(x_ref.at[:, part(k)], x.at[:, part(k)], x_sems.at[k]) for k in range(chunks)]
    w_loads = [
        (
            pltpu.make_async_copy(ws_ref.at[part(k), :], ws.at[part(k), :], w_sems.at[2 * k]),
            pltpu.make_async_copy(wt_ref.at[part(k), :], wt.at[part(k), :], w_sems.at[2 * k + 1]),
        )
        for k in range(chunks)
    ]
    edge_copy = pltpu.make_async_remote_copy(
        x_ref.at[ROWS - 16 :, :], edge, edge_send, edge_recv, {"ctx": after}, MESH
    )

    vec_ref[:4, :] = conv_ref[...]
    vec_ref[4:5, :] = gain_ref[...]
    vec_ref[5:6, :] = out_gain_ref[...]
    vec_ref[6:8, :] = jnp.zeros((2, features), F32)
    vec_away_ref[...] = vec_ref[:, features - away :]
    for load in x_loads:
        load.start()
    for pair in w_loads:
        for load in pair:
            load.start()
    pl.semaphore_wait(barrier, 2)
    edge_copy.start()

    total = jnp.zeros((ROWS, 128), F32)
    for k in range(chunks):
        x_loads[k].wait()
        for i in range(k * CHUNK, (k + 1) * CHUNK, 512):
            square = x[:, i : i + 512].astype(F32)
            square = square * square
            total = total + (square[:, :128] + square[:, 128:256]) + (square[:, 256:384] + square[:, 384:])
    scale = lax.rsqrt(jnp.sum(total, axis=-1, keepdims=True) * (1.0 / features) + epsilon)

    maps = jnp.zeros((ROWS, 2 * STATE), F32)
    step = jnp.zeros((ROWS, HEADS), F32)
    for k in range(chunks):
        for load in w_loads[k]:
            load.wait()
        normed = (x[:, part(k)].astype(F32) * scale * gain_ref[:, part(k)]).astype(BF16)
        maps = maps + dot(normed, ws[part(k), :])
        step = step + dot(normed, wt[part(k), :])
    for ref in (maps_ref, maps_away_ref):
        ref[:, : 2 * STATE] = maps.astype(BF16)
    step = jax.nn.softplus(step + bias_ref[...]).T
    flat = jnp.broadcast_to(scale, (ROWS, 128)).T[:1, :]
    home = step_ref.shape[0] - 8
    for ref, start, stop in ((step_ref, 0, home), (step_away_ref, home, HEADS)):
        ref[: stop - start, :] = step[start:stop, :]
        pad = jnp.zeros((1, ROWS - (stop - start)), F32)
        rate = jnp.concatenate([rate_ref[:, start:stop], pad], axis=1)
        skip = jnp.concatenate([skip_ref[:, start:stop], pad], axis=1)
        ref[stop - start :, :] = jnp.concatenate([flat, rate, skip, jnp.zeros((5, ROWS), F32)], axis=0)

    edge_copy.wait()
    rows = edge[...].astype(F32)[16 - HALO :, :]
    meansq = jnp.sum(rows * rows, axis=-1, keepdims=True) * (1.0 / features)
    rows = rows * lax.rsqrt(meansq + epsilon) * gain_ref[...]
    rows = jnp.where(me == 0, jnp.zeros_like(rows), rows)
    for ref, start in ((maps_ref, 0), (maps_away_ref, features - away)):
        ref[:, 2 * STATE :] = jnp.concatenate(
            [rows[:, start + i * 128 : start + (i + 1) * 128] for i in range(ROWS // HALO)], axis=0
        ).astype(BF16)


def project(x, proj_state, proj_step, gain, conv, out_gain, bias, rate, skip, away, collective_id):
    features = x.shape[1]
    chunks = features // CHUNK
    any_ = pl.BlockSpec(memory_space=pl.ANY)
    vmem = pl.BlockSpec(memory_space=pltpu.VMEM)
    dma = pltpu.SemaphoreType.DMA
    return pl.pallas_call(
        project_kernel,
        in_specs=[any_] * 3 + [vmem] * 6,
        out_specs=[vmem] * 6,
        out_shape=[
            jax.ShapeDtypeStruct((ROWS, 2 * STATE + 128), BF16),
            jax.ShapeDtypeStruct((ROWS, 2 * STATE + 128), BF16),
            jax.ShapeDtypeStruct((HEADS - away // HEAD + 8, ROWS), F32),
            jax.ShapeDtypeStruct((away // HEAD + 8, ROWS), F32),
            jax.ShapeDtypeStruct((8, features), F32),
            jax.ShapeDtypeStruct((8, away), F32),
        ],
        scratch_shapes=[
            pltpu.VMEM(x.shape, BF16),
            pltpu.VMEM(proj_state.shape, BF16),
            pltpu.VMEM(proj_step.shape, BF16),
            pltpu.VMEM((16, features), BF16),
            dma((chunks,)),
            dma((2 * chunks,)),
            dma,
            dma,
        ],
        compiler_params=pltpu.CompilerParams(
            vmem_limit_bytes=VMEM_LIMIT, collective_id=collective_id, has_side_effects=True
        ),
        cost_estimate=pl.CostEstimate(
            flops=2 * ROWS * features * 3 * STATE, bytes_accessed=36 << 20, transcendentals=0
        ),
        name="project",
    )(x, proj_state, proj_step, gain, conv, out_gain, bias, rate, skip)


def group_kernel(pieces, hops, outs, *refs):
    refs = list(refs)

    def take(n):
        taken = refs[:n]
        del refs[:n]
        return taken

    x_refs = take(len(pieces))
    shared = take(3)
    relay_in = take(1)[0]
    out_refs = take(len(outs))
    relay_out = take(1)[0]
    group_body(pieces, hops, outs, x_refs, *shared, relay_in, out_refs, relay_out, *refs)


def group_body(
    pieces,
    hops,
    outs,
    x_refs,
    vec_ref,
    maps_ref,
    step_ref,
    relay_in,
    out_refs,
    relay_out,
    relay_slots,
    relay_send,
    relay_recv,
    out_ref,
    out_sems,
    x_ref,
    x_sems,
    cum_heads,
    weight_heads,
    enter_heads,
    skip_heads,
    pair_heads,
    chip_heads,
    closing,
    scale,
    scores,
    write_flat,
    inner_ref,
    within_ref,
    fresh,
    peer,
    peer_closing,
    total,
    total_closing,
    got,
    got_closing,
    before,
    entering,
    mine,
    theirs,
    landed,
    pair_send,
    pair_recv,
    send1,
    recv1,
    send2,
    recv2,
    send3,
    recv3,
):
    features = x_ref.shape[1]
    heads = features // HEAD
    batch = features // BATCHES
    half, quarter = batch // 2, batch // 4
    batch_tiles = batch // TILE
    half_tiles = batch_tiles // 2
    in_tile = TILE // HEAD
    me = lax.axis_index("ctx")
    core = lax.rem(me, 2)
    chip = me // 2
    partner = chip * 2 + (1 - core)

    def device(index):
        return {"ctx": index}

    section = lax.axis_index("pipe")
    sections = lax.axis_size("pipe")
    behind, ahead = lax.rem(section + sections - 1, sections), lax.rem(section + 1, sections)

    def hop(k):
        source = relay_in if k == 0 else relay_slots.at[k - 1]
        return pltpu.make_async_remote_copy(
            source, relay_slots.at[k], relay_send.at[k], relay_recv.at[k], {"pipe": behind}, MESH
        )

    def pass_on(k):
        if k > 0:
            hop(k - 1).wait_recv()
        hop(k).start()

    def tile_columns(i):
        return pl.ds(pl.multiple_of(i * TILE, TILE), TILE)

    def tile_heads(i):
        return pl.ds(pl.multiple_of(i * in_tile, in_tile), in_tile)

    barrier = pltpu.get_barrier_semaphore()
    pl.semaphore_signal(barrier, inc=1, device_id=device(partner), device_id_type=MESH)

    def greet(d, carry):
        other = lax.rem(chip + d, CHIPS) * 2 + core
        pl.semaphore_signal(barrier, inc=1, device_id=device(other), device_id_type=MESH)
        return carry

    lax.fori_loop(1, CHIPS, greet, 0)
    for other in (behind, ahead):
        pl.semaphore_signal(barrier, inc=1, device_id={"pipe": other}, device_id_type=MESH)

    loads = []
    for k, width in enumerate(pieces):
        start = sum(pieces[:k])
        load = pltpu.make_async_copy(
            x_refs[k].at[:, :width], x_ref.at[:, start : start + width], x_sems.at[k]
        )
        load.start()
        loads.append(load)

    step = step_ref[:heads, :]
    extra = step_ref[heads:, :].T
    log_decay = -step * extra[:heads, 1:2]
    row = lax.broadcasted_iota(jnp.int32, (ROWS, ROWS), 0)
    column = lax.broadcasted_iota(jnp.int32, (ROWS, ROWS), 1)
    upper = (row <= column).astype(F32).astype(BF16)
    part1, part2, part3 = three_parts(log_decay)
    cumulative = dot(part3, upper) + dot(part2, upper) + dot(part1, upper)
    last = cumulative[:, ROWS - 1 :]
    cum_heads[...] = cumulative * LOG2E
    weight_heads[...] = jnp.exp(last - cumulative) * step
    enter_heads[...] = jnp.exp(cumulative)
    closing[...] = jnp.concatenate(
        [jnp.broadcast_to(last, (heads, 128)), jnp.zeros((HEADS - heads, 128), F32)], axis=0
    ).T[:8, :]
    skip_heads[...] = jnp.broadcast_to(extra[:heads, 2:3], (heads, 128))
    scale[...] = jnp.broadcast_to(extra[:, 0:1], (ROWS, 128))
    write_flat[...] = maps_ref[:, :STATE].astype(F32).T.astype(BF16)

    for load in loads:
        load.wait()

    def fresh_tile(i):
        columns = tile_columns(i)
        normed = (x_ref[:, columns].astype(F32) * scale[:, :1] * vec_ref[4:5, columns]).astype(BF16)
        parts = TILE // 128
        halo = maps_ref[pl.ds(pl.multiple_of(i * HALO * parts, HALO * parts), HALO * parts), 2 * STATE :].astype(F32)
        halo = jnp.concatenate([halo[k * HALO : (k + 1) * HALO] for k in range(parts)], axis=1)
        normed = jnp.concatenate([halo, normed.astype(F32)], axis=0)
        shifted = pltpu.roll(normed, 1, 0)
        early = vec_ref[1:2, columns] * normed + vec_ref[0:1, columns] * shifted
        conv = vec_ref[3:4, columns] * normed[HALO:] + vec_ref[2:3, columns] * shifted[HALO:]
        conv = conv + pltpu.roll(early, 2, 0)[HALO:]
        conv = conv * 0.5
        inner = (conv + conv * jnp.tanh(conv)).astype(BF16)
        inner_ref[:, columns] = inner
        spread = spread_heads(weight_heads[tile_heads(i), :], TILE)
        weighted = (inner.astype(F32) * spread).astype(BF16)
        fresh[:, columns] = dot(write_flat[...], weighted).astype(BF16)

    def within_tile(i):
        columns = tile_columns(i)
        inner = inner_ref[:, columns].astype(F32)
        stepped = (inner * spread_heads(step_ref[tile_heads(i), :], TILE)).astype(BF16)
        cum = cum_heads[tile_heads(i), :]
        cum_columns = cum.T
        top, bottom = scores[:128, :128], scores[128:, :]
        lane = lax.broadcasted_iota(jnp.int32, (ROWS, 128), 1)
        for pair in range(TILE // 128):
            values = stepped[:, pair * 128 : (pair + 1) * 128]
            upper = lower = None
            for side in range(2):
                h = pair * 2 + side
                column = cum_columns[:, h : h + 1]
                row = cum[h : h + 1, :]
                own = jnp.where((lane >= HEAD) == (side == 1), values, jnp.zeros_like(values))
                mix0 = (jnp.exp2(jnp.minimum(column[:128] - row[:, :128], 0.0)) * top).astype(BF16)
                mix1 = (jnp.exp2(jnp.minimum(column[128:] - row, 0.0)) * bottom).astype(BF16)
                up, low = dot(mix0, own[:128]), dot(mix1, own)
                upper = up if upper is None else upper + up
                lower = low if lower is None else lower + low
            at = pl.ds(pl.multiple_of(i * TILE + pair * 128, 128), 128)
            within_ref[:128, at] = upper
            within_ref[128:, at] = lower

    def finish_tile(i, state):
        columns = tile_columns(i)
        inner = inner_ref[:, columns].astype(F32)
        carried = dot(maps_ref[:, STATE : 2 * STATE], state) * spread_heads(enter_heads[tile_heads(i), :], TILE)
        skip = spread_heads(skip_heads[tile_heads(i), :8], TILE)[0:1, :]
        output = within_ref[:, columns] + carried + skip * inner
        square = (output * output).astype(BF16)
        a = lax.broadcasted_iota(jnp.int32, (256, 256), 0) // HEAD
        b = lax.broadcasted_iota(jnp.int32, (256, 256), 1) // HEAD
        same = (a == b).astype(F32).astype(BF16)
        sums = jnp.concatenate(
            [dot(square[:, k * 256 : (k + 1) * 256], same) for k in range(TILE // 256)], axis=1
        )
        normed = output * lax.rsqrt(sums * (1.0 / HEAD) + epsilon)
        out_ref[:, columns] = (x_ref[:, columns].astype(F32) + normed * vec_ref[5:6, columns]).astype(BF16)

    def run(body, start, stop):
        def one(i, carry):
            body(i)
            return carry

        lax.fori_loop(start, stop, one, 0)

    is_first = core == 0

    def columns_of(b, which, width):
        return pl.ds(pl.multiple_of(b * batch + which * width, 128), width)

    def half_tile(b, which, j):
        return b * batch_tiles + which * half_tiles + j

    def place(of):
        return (
            pl.ds(pl.multiple_of(lax.rem(of, 8) * 16, 16), 16),
            pl.ds(pl.multiple_of((of // 8) * quarter, 128), quarter),
        )

    def pair_copy(b):
        return pltpu.make_async_remote_copy(
            fresh.at[:, columns_of(b, 1 - core, half)], peer.at[b], pair_send.at[b], pair_recv.at[b], device(partner), MESH
        )

    def back_pair_copy(b):
        return pltpu.make_async_remote_copy(
            theirs.at[b], landed.at[b], pair_send.at[BATCHES + b], pair_recv.at[BATCHES + b], device(partner), MESH
        )

    closing_pair_copy = pltpu.make_async_remote_copy(
        closing, peer_closing, pair_send.at[2 * BATCHES], pair_recv.at[2 * BATCHES], device(partner), MESH
    )

    def own_states(b):
        own = fresh[:, columns_of(b, core, half)].astype(F32)
        other = peer[b].astype(F32)
        return jnp.where(is_first, own, other), jnp.where(is_first, other, own)

    def pair_decays(b):
        first = pl.multiple_of((b * batch + core * half) // HEAD, 8)
        return spread_heads(pair_heads[pl.ds(first, half // HEAD), :16], half)

    def combine(b):
        state0, state1 = own_states(b)
        total[b] = (pair_decays(b)[8:9, :] * state0 + state1).astype(BF16)

    def state_copy(b, to):
        rows, columns = place(to)
        return pltpu.make_async_remote_copy(
            total.at[b, rows, columns], got.at[b, chip], send1.at[b], recv1.at[b], device(to * 2 + core), MESH
        )

    def closing_copy(to):
        return pltpu.make_async_remote_copy(
            total_closing, got_closing.at[chip], send2, recv2, device(to * 2 + core), MESH
        )

    def back_copy(b, to):
        rows, columns = place(chip)
        return pltpu.make_async_remote_copy(
            before.at[b, to], entering.at[b, rows, columns], send3.at[b], recv3.at[b], device(to * 2 + core), MESH
        )

    def send_states(b):
        def one(d):
            to = lax.rem(chip + d, CHIPS)
            if b == 0:
                closing_copy(to).start()
            state_copy(b, to).start()

        for d in range(1, CHIPS):
            one(d)
        rows, columns = place(chip)
        got[b, chip] = total[b, rows, columns]

    def all_of(ref, send, recv):
        pieces = ref.at[: CHIPS - 1]
        return pltpu.make_async_remote_copy(pieces, pieces, send, recv, device(partner), MESH)

    def scan_states(b):
        all_of(got.at[b], send1.at[b], recv1.at[b]).wait_recv()
        if b == 0:
            all_of(got_closing, send2, recv2).wait_recv()
            chip_heads[:, :CHIPS] = jnp.exp(got_closing[:, 0, :]).T
        first = pl.multiple_of((b * batch + core * half) // HEAD + (chip // 8) * (quarter // HEAD), 8)
        decays = spread_heads(chip_heads[pl.ds(first, quarter // HEAD), :CHIPS], quarter)
        state = jnp.zeros((16, quarter), F32)
        for k in range(CHIPS):
            before[b, k] = state.astype(BF16)
            if k < CHIPS - 1:
                state = decays[k : k + 1, :] * state + got[b, k].astype(F32)

    def send_back(b):
        for d in range(1, CHIPS):
            back_copy(b, lax.rem(chip + d, CHIPS)).start()
        rows, columns = place(chip)
        entering[b, rows, columns] = before[b, chip]

    def take_back(b):
        all_of(before.at[b], send3.at[b], recv3.at[b]).wait_recv()
        for_first = entering[b]
        for_second = (pair_decays(b)[0:1, :] * for_first.astype(F32) + own_states(b)[0]).astype(BF16)
        theirs[b] = jnp.where(is_first, for_second, for_first)
        back_pair_copy(b).start()
        mine[b] = jnp.where(is_first, for_first, for_second)

    def finish_half(b, which, states):
        run(lambda j: finish_tile(half_tile(b, which, j), states[b, :, tile_columns(j)]), 0, half_tiles)

    def fresh_half(b, which):
        run(lambda j: fresh_tile(half_tile(b, which, j)), 0, half_tiles)

    cuts = sorted({0, batch, *(sum(outs[: k + 1]) for k in range(len(outs)))})
    stores = []
    for n, (start, stop) in enumerate(zip(cuts, cuts[1:])):
        k = sum(sum(outs[: i + 1]) <= start for i in range(len(outs)))
        at = start - sum(outs[:k])
        stores.append(
            pltpu.make_async_copy(
                out_ref.at[:, start:stop], out_refs[k].at[:, at : at + stop - start], out_sems.at[n]
            )
        )

    fresh_half(0, 1 - core)
    pl.semaphore_wait(barrier, CHIPS + 2)
    pair_copy(0).start()
    pass_on(0)
    closing_pair_copy.start()
    fresh_half(0, core)
    fresh_half(1, 1 - core)
    pair_copy(1).start()
    closing_pair_copy.wait()
    closing0 = jnp.where(is_first, closing[...], peer_closing[...])
    closing1 = jnp.where(is_first, peer_closing[...], closing[...])
    pair_heads[:, :16] = jnp.exp(jnp.concatenate([closing0, closing1], axis=0)).T
    total_closing[...] = closing0 + closing1
    got_closing[chip] = total_closing[...]
    pair_copy(0).wait()
    combine(0)
    send_states(0)
    fresh_half(1, core)
    pair_copy(1).wait()
    combine(1)
    send_states(1)
    if hops == 3:
        pass_on(1)
    scores[...] = jnp.where(row >= column, dot(maps_ref[:, STATE : 2 * STATE], write_flat[...]), 0.0)
    run(within_tile, 0, batch_tiles)
    scan_states(0)
    send_back(0)
    if hops == 2:
        pass_on(1)
    run(within_tile, batch_tiles, batch_tiles + half_tiles)
    scan_states(1)
    send_back(1)
    run(within_tile, batch_tiles + half_tiles, 2 * batch_tiles)
    if hops == 3:
        pass_on(2)
    take_back(0)
    finish_half(0, core, mine)
    back_pair_copy(0).wait()
    finish_half(0, 1 - core, landed)
    stores[0].start()
    take_back(1)
    finish_half(1, core, mine)
    back_pair_copy(1).wait()
    finish_half(1, 1 - core, landed)
    for store in stores[1:]:
        store.start()
    all_of(got_closing, send2, recv2).wait_send()
    for b in range(BATCHES):
        all_of(got.at[b], send1.at[b], recv1.at[b]).wait_send()
        all_of(before.at[b], send3.at[b], recv3.at[b]).wait_send()
    hop(hops - 1).wait_recv()
    last = pltpu.make_async_copy(relay_slots.at[hops - 1], relay_out, out_sems.at[len(outs) + 1])
    last.start()
    for k in range(hops):
        hop(k).wait_send()
    for store in stores + [last]:
        store.wait()


def group(pieces, xs, vec, maps, step, relay, hops, outs, collective_id):
    features = sum(pieces)
    heads = features // HEAD
    half, quarter = features // BATCHES // 2, features // BATCHES // 4
    corner = lambda i: (0, 0)
    dma = pltpu.SemaphoreType.DMA
    vmem = pltpu.VMEM
    return pl.pallas_call(
        functools.partial(group_kernel, pieces, hops, outs),
        out_shape=[jax.ShapeDtypeStruct((ROWS, columns), BF16) for columns in outs]
        + [jax.ShapeDtypeStruct(array.shape, array.dtype) for array in (relay,)],
        grid=(1,),
        in_specs=[pl.BlockSpec(memory_space=pl.ANY)] * len(pieces)
        + [
            pl.BlockSpec((vec.shape[0], features), corner),
            pl.BlockSpec(maps.shape, corner),
            pl.BlockSpec((heads + 8, ROWS), corner),
        ]
        + [pl.BlockSpec(memory_space=pl.ANY)] ,
        out_specs=[pl.BlockSpec(memory_space=pl.ANY)] * (len(outs) + 1),
        scratch_shapes=[
            vmem((hops,) + relay.shape, BF16),
            dma((hops,)),
            dma((hops,)),
            vmem((ROWS, features), BF16),
            dma((len(outs) + 2,)),
            vmem((ROWS, features), BF16),
            dma((len(pieces),)),
            vmem((heads, ROWS), F32),
            vmem((heads, ROWS), F32),
            vmem((heads, ROWS), F32),
            vmem((heads, 128), F32),
            vmem((HEADS, 128), F32),
            vmem((HEADS, 128), F32),
            vmem((8, HEADS), F32),
            vmem((ROWS, 128), F32),
            vmem((ROWS, ROWS), F32),
            vmem((STATE, ROWS), BF16),
            vmem((ROWS, features), BF16),
            vmem((ROWS, features), F32),
            vmem((STATE, features), BF16),
            vmem((BATCHES, STATE, half), BF16),
            vmem((8, HEADS), F32),
            vmem((BATCHES, STATE, half), BF16),
            vmem((8, HEADS), F32),
            vmem((BATCHES, CHIPS, 16, quarter), BF16),
            vmem((CHIPS, 8, HEADS), F32),
            vmem((BATCHES, CHIPS, 16, quarter), BF16),
            vmem((BATCHES, STATE, half), BF16),
            vmem((BATCHES, STATE, half), BF16),
            vmem((BATCHES, STATE, half), BF16),
            vmem((BATCHES, STATE, half), BF16),
            dma((2 * BATCHES + 1,)),
            dma((2 * BATCHES + 1,)),
            dma((BATCHES,)),
            dma((BATCHES,)),
            dma,
            dma,
            dma((BATCHES,)),
            dma((BATCHES,)),
        ],
        compiler_params=pltpu.CompilerParams(
            collective_id=collective_id, has_side_effects=True, vmem_limit_bytes=VMEM_LIMIT
        ),
        cost_estimate=pl.CostEstimate(
            flops=ROWS * features, bytes_accessed=ROWS * features, transcendentals=0
        ),
        name="group",
    )(*xs, vec, maps, step, relay)


def widen_kernel(blocks, *refs):
    parts, out, held, loads, stores = refs[:-4], refs[-4], refs[-3], refs[-2], refs[-1]
    start = out.shape[1] - sum(width for _, _, width in blocks)
    pairs = []
    at = 0
    for k, (part, begin, width) in enumerate(blocks):
        here = held.at[:, at : at + width]
        load = pltpu.make_async_copy(parts[part].at[:, begin : begin + width], here, loads.at[k])
        store = pltpu.make_async_copy(here, out.at[:, start + at : start + at + width], stores.at[k])
        pairs.append((load, store))
        at += width
    for load, _ in pairs:
        load.start()
    for load, store in pairs:
        load.wait()
        store.start()
    for _, store in pairs:
        store.wait()


def widen(parts, width):
    blocks = []
    for k, part in enumerate(parts):
        begin = 0
        while begin < part.shape[1]:
            size = min(1024, part.shape[1] - begin)
            blocks.append((k, begin, size))
            begin += size
    dma = pltpu.SemaphoreType.DMA((len(blocks),))
    return pl.pallas_call(
        functools.partial(widen_kernel, blocks),
        in_specs=[pl.BlockSpec(memory_space=pl.ANY)] * len(parts),
        out_specs=pl.BlockSpec(memory_space=pl.ANY),
        out_shape=jax.ShapeDtypeStruct((ROWS, width), BF16),
        scratch_shapes=[pltpu.VMEM((ROWS, sum(part.shape[1] for part in parts)), BF16), dma, dma],
        compiler_params=pltpu.CompilerParams(vmem_limit_bytes=VMEM_LIMIT),
        cost_estimate=pl.CostEstimate(flops=1, bytes_accessed=ROWS * width * 2, transcendentals=0),
        name="widen",
    )(*parts)


def moved(array, by):
    peers = lax.axis_size("pipe")
    return lax.ppermute(array, "pipe", [(i, (i + by) % peers) for i in range(peers)])


def shards(
    incoming, norm_gain, proj_state, proj_step, conv_weight, decay_rate, step_bias, skip_gain, out_gain
):
    x = incoming[0]
    features = x.shape[1]
    home, back, away = HEADS_HOME * HEAD, HEADS_BACK * HEAD, HEADS_AWAY * HEAD
    ahead, round_ = HEADS_AHEAD * HEAD, HEADS_ROUND * HEAD

    x_ahead = moved(x[:, home : home + ahead], 1)
    x_round = moved(x[:, features - round_ :], -1)
    maps, maps_away, step, step_away, vec, vec_away = project(
        x, proj_state[0], proj_step[0], norm_gain, conv_weight[0], out_gain, step_bias, decay_rate, skip_gain,
        away, 2,
    )
    step_away, maps_away, vec_away = moved(step_away, 1), moved(maps_away, 1), moved(vec_away, 1)

    rows, rows_back, x_round = group(
        (home,), (x,), vec, maps, step, x_round, 2, (home - back, back), 0
    )
    rows, x_ahead, step_away, maps_away, vec_away = lax.optimization_barrier(
        (rows, x_ahead, step_away, maps_away, vec_away)
    )
    rows_in = moved(rows, 1)

    rows_away, rows_back = group(
        (ahead, round_), (x_ahead, x_round), vec_away, maps_away, step_away,
        rows_back, 3, (away,), 1,
    )
    passed = widen((rows_back, rows_away), features)
    return lax.dynamic_update_slice(passed, rows_in, (0, 0))[None]


def solution(mesh):
    return jax.shard_map(
        shards,
        mesh=mesh,
        in_specs=(
            P("pipe", "ctx", None),
            P("pipe", None),
            P("pipe", None, None),
            P("pipe", None, None),
            P("pipe", None, None),
            P("pipe", None),
            P("pipe", None),
            P("pipe", None),
            P("pipe", None),
        ),
        out_specs=P("pipe", "ctx", None),
        check_vma=False,
    )
```

```python
import functools

import jax
import jax.numpy as jnp
from jax import lax
from jax.experimental import pallas as pl
from jax.experimental.pallas import tpu as pltpu
from jax.sharding import PartitionSpec as P

MESH = pl.DeviceIdType.MESH
F32 = jnp.float32
BF16 = jnp.bfloat16

ROWS = 256
STATE = 128
HEADS = 128
HEAD = 64
CONV = 4
HALO = 8
TILE = 512
CHUNK = 2048
CHIPS = 16
BATCHES = 2
LOG2E = 1.4426950408889634
epsilon = 1e-05
VMEM_LIMIT = 56 * 1024 * 1024

HEADS_HOME = 64
HEADS_BACK = 12
HEADS_ROUND = 16
HEADS_AWAY = HEADS - HEADS_HOME
HEADS_AHEAD = HEADS_AWAY - HEADS_ROUND


def dot(a, b):
    return jnp.dot(a, b, preferred_element_type=F32)


def three_parts(x):
    first = x.astype(BF16)
    rest = x - first.astype(F32)
    second = rest.astype(BF16)
    return first, second, (rest - second.astype(F32)).astype(BF16)


def spreader(rows, width):
    head = lax.broadcasted_iota(jnp.int32, (2 * rows, width), 0) % rows
    feature = lax.broadcasted_iota(jnp.int32, (2 * rows, width), 1) // HEAD
    return (head == feature).astype(F32).astype(BF16)


def spread_heads(values, width):
    high = values.astype(BF16).astype(F32)
    both = jnp.concatenate([high, values - high], axis=0).astype(BF16)
    return lax.dot_general(
        both, spreader(values.shape[0], width), (((0,), (0,)), ((), ())), preferred_element_type=F32
    )


def project_kernel(
    x_ref,
    ws_ref,
    wt_ref,
    gain_ref,
    conv_ref,
    out_gain_ref,
    bias_ref,
    rate_ref,
    skip_ref,
    maps_ref,
    maps_away_ref,
    step_ref,
    step_away_ref,
    vec_ref,
    vec_away_ref,
    x,
    ws,
    wt,
    edge,
    x_sems,
    w_sems,
    edge_send,
    edge_recv,
):
    features = x.shape[1]
    away = vec_away_ref.shape[1]
    chunks = features // CHUNK
    me = lax.axis_index("ctx")
    peers = lax.axis_size("ctx")
    after, ahead = lax.rem(me + 1, peers), lax.rem(me + peers - 1, peers)

    barrier = pltpu.get_barrier_semaphore()
    for other in (after, ahead):
        pl.semaphore_signal(barrier, inc=1, device_id={"ctx": other}, device_id_type=MESH)

    def part(k):
        return slice(k * CHUNK, (k + 1) * CHUNK)

    x_loads = [pltpu.make_async_copy(x_ref.at[:, part(k)], x.at[:, part(k)], x_sems.at[k]) for k in range(chunks)]
    w_loads = [
        (
            pltpu.make_async_copy(ws_ref.at[part(k), :], ws.at[part(k), :], w_sems.at[2 * k]),
            pltpu.make_async_copy(wt_ref.at[part(k), :], wt.at[part(k), :], w_sems.at[2 * k + 1]),
        )
        for k in range(chunks)
    ]
    edge_copy = pltpu.make_async_remote_copy(
        x_ref.at[ROWS - 16 :, :], edge, edge_send, edge_recv, {"ctx": after}, MESH
    )

    vec_ref[:4, :] = conv_ref[...]
    vec_ref[4:5, :] = gain_ref[...]
    vec_ref[5:6, :] = out_gain_ref[...]
    vec_ref[6:8, :] = jnp.zeros((2, features), F32)
    vec_away_ref[...] = vec_ref[:, features - away :]
    for load in x_loads:
        load.start()
    for pair in w_loads:
        for load in pair:
            load.start()
    pl.semaphore_wait(barrier, 2)
    edge_copy.start()

    total = jnp.zeros((ROWS, 128), F32)
    for k in range(chunks):
        x_loads[k].wait()
        for i in range(k * CHUNK, (k + 1) * CHUNK, 512):
            square = x[:, i : i + 512].astype(F32)
            square = square * square
            total = total + (square[:, :128] + square[:, 128:256]) + (square[:, 256:384] + square[:, 384:])
    scale = lax.rsqrt(jnp.sum(total, axis=-1, keepdims=True) * (1.0 / features) + epsilon)

    maps = jnp.zeros((ROWS, 2 * STATE), F32)
    step = jnp.zeros((ROWS, HEADS), F32)
    for k in range(chunks):
        for load in w_loads[k]:
            load.wait()
        normed = (x[:, part(k)].astype(F32) * scale * gain_ref[:, part(k)]).astype(BF16)
        maps = maps + dot(normed, ws[part(k), :])
        step = step + dot(normed, wt[part(k), :])
    for ref in (maps_ref, maps_away_ref):
        ref[:, : 2 * STATE] = maps.astype(BF16)
    step = jax.nn.softplus(step + bias_ref[...]).T
    flat = jnp.broadcast_to(scale, (ROWS, 128)).T[:1, :]
    home = step_ref.shape[0] - 8
    for ref, start, stop in ((step_ref, 0, home), (step_away_ref, home, HEADS)):
        ref[: stop - start, :] = step[start:stop, :]
        pad = jnp.zeros((1, ROWS - (stop - start)), F32)
        rate = jnp.concatenate([rate_ref[:, start:stop], pad], axis=1)
        skip = jnp.concatenate([skip_ref[:, start:stop], pad], axis=1)
        ref[stop - start :, :] = jnp.concatenate([flat, rate, skip, jnp.zeros((5, ROWS), F32)], axis=0)

    edge_copy.wait()
    rows = edge[...].astype(F32)[16 - HALO :, :]
    meansq = jnp.sum(rows * rows, axis=-1, keepdims=True) * (1.0 / features)
    rows = rows * lax.rsqrt(meansq + epsilon) * gain_ref[...]
    rows = jnp.where(me == 0, jnp.zeros_like(rows), rows)
    for ref, start in ((maps_ref, 0), (maps_away_ref, features - away)):
        ref[:, 2 * STATE :] = jnp.concatenate(
            [rows[:, start + i * 128 : start + (i + 1) * 128] for i in range(ROWS // HALO)], axis=0
        ).astype(BF16)


def project(x, proj_state, proj_step, gain, conv, out_gain, bias, rate, skip, away, collective_id):
    features = x.shape[1]
    chunks = features // CHUNK
    any_ = pl.BlockSpec(memory_space=pl.ANY)
    vmem = pl.BlockSpec(memory_space=pltpu.VMEM)
    dma = pltpu.SemaphoreType.DMA
    return pl.pallas_call(
        project_kernel,
        in_specs=[any_] * 3 + [vmem] * 6,
        out_specs=[vmem] * 6,
        out_shape=[
            jax.ShapeDtypeStruct((ROWS, 2 * STATE + 128), BF16),
            jax.ShapeDtypeStruct((ROWS, 2 * STATE + 128), BF16),
            jax.ShapeDtypeStruct((HEADS - away // HEAD + 8, ROWS), F32),
            jax.ShapeDtypeStruct((away // HEAD + 8, ROWS), F32),
            jax.ShapeDtypeStruct((8, features), F32),
            jax.ShapeDtypeStruct((8, away), F32),
        ],
        scratch_shapes=[
            pltpu.VMEM(x.shape, BF16),
            pltpu.VMEM(proj_state.shape, BF16),
            pltpu.VMEM(proj_step.shape, BF16),
            pltpu.VMEM((16, features), BF16),
            dma((chunks,)),
            dma((2 * chunks,)),
            dma,
            dma,
        ],
        compiler_params=pltpu.CompilerParams(
            vmem_limit_bytes=VMEM_LIMIT, collective_id=collective_id, has_side_effects=True
        ),
        cost_estimate=pl.CostEstimate(
            flops=2 * ROWS * features * 3 * STATE, bytes_accessed=36 << 20, transcendentals=0
        ),
        name="project",
    )(x, proj_state, proj_step, gain, conv, out_gain, bias, rate, skip)


def group_kernel(pieces, hops, outs, *refs):
    refs = list(refs)

    def take(n):
        taken = refs[:n]
        del refs[:n]
        return taken

    x_refs = take(len(pieces))
    shared = take(3)
    relay_in = take(1)[0]
    out_refs = take(len(outs))
    relay_out = take(1)[0]
    group_body(pieces, hops, outs, x_refs, *shared, relay_in, out_refs, relay_out, *refs)


def group_body(
    pieces,
    hops,
    outs,
    x_refs,
    vec_ref,
    maps_ref,
    step_ref,
    relay_in,
    out_refs,
    relay_out,
    relay_slots,
    relay_send,
    relay_recv,
    out_ref,
    out_sems,
    x_ref,
    x_sems,
    cum_heads,
    weight_heads,
    enter_heads,
    skip_heads,
    pair_heads,
    chip_heads,
    closing,
    scale,
    scores,
    write_flat,
    inner_ref,
    within_ref,
    fresh,
    peer,
    peer_closing,
    total,
    total_closing,
    got,
    got_closing,
    before,
    entering,
    mine,
    theirs,
    landed,
    pair_send,
    pair_recv,
    send1,
    recv1,
    send2,
    recv2,
    send3,
    recv3,
):
    features = x_ref.shape[1]
    heads = features // HEAD
    batch = features // BATCHES
    half, quarter = batch // 2, batch // 4
    batch_tiles = batch // TILE
    half_tiles = batch_tiles // 2
    in_tile = TILE // HEAD
    me = lax.axis_index("ctx")
    core = lax.rem(me, 2)
    chip = me // 2
    partner = chip * 2 + (1 - core)

    def device(index):
        return {"ctx": index}

    section = lax.axis_index("pipe")
    sections = lax.axis_size("pipe")
    behind, ahead = lax.rem(section + sections - 1, sections), lax.rem(section + 1, sections)

    def hop(k):
        source = relay_in if k == 0 else relay_slots.at[k - 1]
        return pltpu.make_async_remote_copy(
            source, relay_slots.at[k], relay_send.at[k], relay_recv.at[k], {"pipe": behind}, MESH
        )

    def pass_on(k):
        if k > 0:
            hop(k - 1).wait_recv()
        hop(k).start()

    def tile_columns(i):
        return pl.ds(pl.multiple_of(i * TILE, TILE), TILE)

    def tile_heads(i):
        return pl.ds(pl.multiple_of(i * in_tile, in_tile), in_tile)

    barrier = pltpu.get_barrier_semaphore()
    pl.semaphore_signal(barrier, inc=1, device_id=device(partner), device_id_type=MESH)

    def greet(d, carry):
        other = lax.rem(chip + d, CHIPS) * 2 + core
        pl.semaphore_signal(barrier, inc=1, device_id=device(other), device_id_type=MESH)
        return carry

    lax.fori_loop(1, CHIPS, greet, 0)
    for other in (behind, ahead):
        pl.semaphore_signal(barrier, inc=1, device_id={"pipe": other}, device_id_type=MESH)

    loads = []
    for k, width in enumerate(pieces):
        start = sum(pieces[:k])
        load = pltpu.make_async_copy(
            x_refs[k].at[:, :width], x_ref.at[:, start : start + width], x_sems.at[k]
        )
        load.start()
        loads.append(load)

    step = step_ref[:heads, :]
    extra = step_ref[heads:, :].T
    log_decay = -step * extra[:heads, 1:2]
    row = lax.broadcasted_iota(jnp.int32, (ROWS, ROWS), 0)
    column = lax.broadcasted_iota(jnp.int32, (ROWS, ROWS), 1)
    upper = (row <= column).astype(F32).astype(BF16)
    part1, part2, part3 = three_parts(log_decay)
    cumulative = dot(part3, upper) + dot(part2, upper) + dot(part1, upper)
    last = cumulative[:, ROWS - 1 :]
    cum_heads[...] = cumulative * LOG2E
    weight_heads[...] = jnp.exp(last - cumulative) * step
    enter_heads[...] = jnp.exp(cumulative)
    closing[...] = jnp.concatenate(
        [jnp.broadcast_to(last, (heads, 128)), jnp.zeros((HEADS - heads, 128), F32)], axis=0
    ).T[:8, :]
    skip_heads[...] = jnp.broadcast_to(extra[:heads, 2:3], (heads, 128))
    scale[...] = jnp.broadcast_to(extra[:, 0:1], (ROWS, 128))
    write_flat[...] = maps_ref[:, :STATE].astype(F32).T.astype(BF16)

    for load in loads:
        load.wait()

    def fresh_tile(i):
        columns = tile_columns(i)
        normed = (x_ref[:, columns].astype(F32) * scale[:, :1] * vec_ref[4:5, columns]).astype(BF16)
        parts = TILE // 128
        halo = maps_ref[pl.ds(pl.multiple_of(i * HALO * parts, HALO * parts), HALO * parts), 2 * STATE :].astype(F32)
        halo = jnp.concatenate([halo[k * HALO : (k + 1) * HALO] for k in range(parts)], axis=1)
        normed = jnp.concatenate([halo, normed.astype(F32)], axis=0)
        shifted = pltpu.roll(normed, 1, 0)
        early = vec_ref[1:2, columns] * normed + vec_ref[0:1, columns] * shifted
        conv = vec_ref[3:4, columns] * normed[HALO:] + vec_ref[2:3, columns] * shifted[HALO:]
        conv = conv + pltpu.roll(early, 2, 0)[HALO:]
        conv = conv * 0.5
        inner = (conv + conv * jnp.tanh(conv)).astype(BF16)
        inner_ref[:, columns] = inner
        spread = spread_heads(weight_heads[tile_heads(i), :], TILE)
        weighted = (inner.astype(F32) * spread).astype(BF16)
        fresh[:, columns] = dot(write_flat[...], weighted).astype(BF16)

    def within_tile(i):
        columns = tile_columns(i)
        inner = inner_ref[:, columns].astype(F32)
        stepped = (inner * spread_heads(step_ref[tile_heads(i), :], TILE)).astype(BF16)
        cum = cum_heads[tile_heads(i), :]
        cum_columns = cum.T
        top, bottom = scores[:128, :128], scores[128:, :]
        lane = lax.broadcasted_iota(jnp.int32, (ROWS, 128), 1)
        for pair in range(TILE // 128):
            values = stepped[:, pair * 128 : (pair + 1) * 128]
            upper = lower = None
            for side in range(2):
                h = pair * 2 + side
                column = cum_columns[:, h : h + 1]
                row = cum[h : h + 1, :]
                own = jnp.where((lane >= HEAD) == (side == 1), values, jnp.zeros_like(values))
                mix0 = (jnp.exp2(jnp.minimum(column[:128] - row[:, :128], 0.0)) * top).astype(BF16)
                mix1 = (jnp.exp2(jnp.minimum(column[128:] - row, 0.0)) * bottom).astype(BF16)
                up, low = dot(mix0, own[:128]), dot(mix1, own)
                upper = up if upper is None else upper + up
                lower = low if lower is None else lower + low
            at = pl.ds(pl.multiple_of(i * TILE + pair * 128, 128), 128)
            within_ref[:128, at] = upper
            within_ref[128:, at] = lower

    def finish_tile(i, state):
        columns = tile_columns(i)
        inner = inner_ref[:, columns].astype(F32)
        carried = dot(maps_ref[:, STATE : 2 * STATE], state) * spread_heads(enter_heads[tile_heads(i), :], TILE)
        skip = spread_heads(skip_heads[tile_heads(i), :8], TILE)[0:1, :]
        output = within_ref[:, columns] + carried + skip * inner
        square = (output * output).astype(BF16)
        a = lax.broadcasted_iota(jnp.int32, (256, 256), 0) // HEAD
        b = lax.broadcasted_iota(jnp.int32, (256, 256), 1) // HEAD
        same = (a == b).astype(F32).astype(BF16)
        sums = jnp.concatenate(
            [dot(square[:, k * 256 : (k + 1) * 256], same) for k in range(TILE // 256)], axis=1
        )
        normed = output * lax.rsqrt(sums * (1.0 / HEAD) + epsilon)
        out_ref[:, columns] = (x_ref[:, columns].astype(F32) + normed * vec_ref[5:6, columns]).astype(BF16)

    def run(body, start, stop):
        def one(i, carry):
            body(i)
            return carry

        lax.fori_loop(start, stop, one, 0)

    is_first = core == 0

    def columns_of(b, which, width):
        return pl.ds(pl.multiple_of(b * batch + which * width, 128), width)

    def half_tile(b, which, j):
        return b * batch_tiles + which * half_tiles + j

    def place(of):
        return (
            pl.ds(pl.multiple_of(lax.rem(of, 8) * 16, 16), 16),
            pl.ds(pl.multiple_of((of // 8) * quarter, 128), quarter),
        )

    def pair_copy(b):
        return pltpu.make_async_remote_copy(
            fresh.at[:, columns_of(b, 1 - core, half)], peer.at[b], pair_send.at[b], pair_recv.at[b], device(partner), MESH
        )

    def back_pair_copy(b):
        return pltpu.make_async_remote_copy(
            theirs.at[b], landed.at[b], pair_send.at[BATCHES + b], pair_recv.at[BATCHES + b], device(partner), MESH
        )

    closing_pair_copy = pltpu.make_async_remote_copy(
        closing, peer_closing, pair_send.at[2 * BATCHES], pair_recv.at[2 * BATCHES], device(partner), MESH
    )

    def own_states(b):
        own = fresh[:, columns_of(b, core, half)].astype(F32)
        other = peer[b].astype(F32)
        return jnp.where(is_first, own, other), jnp.where(is_first, other, own)

    def pair_decays(b):
        first = pl.multiple_of((b * batch + core * half) // HEAD, 8)
        return spread_heads(pair_heads[pl.ds(first, half // HEAD), :16], half)

    def combine(b):
        state0, state1 = own_states(b)
        total[b] = (pair_decays(b)[8:9, :] * state0 + state1).astype(BF16)

    def state_copy(b, to):
        rows, columns = place(to)
        return pltpu.make_async_remote_copy(
            total.at[b, rows, columns], got.at[b, chip], send1.at[b], recv1.at[b], device(to * 2 + core), MESH
        )

    def closing_copy(to):
        return pltpu.make_async_remote_copy(
            total_closing, got_closing.at[chip], send2, recv2, device(to * 2 + core), MESH
        )

    def back_copy(b, to):
        rows, columns = place(chip)
        return pltpu.make_async_remote_copy(
            before.at[b, to], entering.at[b, rows, columns], send3.at[b], recv3.at[b], device(to * 2 + core), MESH
        )

    def send_states(b):
        def one(d):
            to = lax.rem(chip + d, CHIPS)
            if b == 0:
                closing_copy(to).start()
            state_copy(b, to).start()

        for d in range(1, CHIPS):
            one(d)
        rows, columns = place(chip)
        got[b, chip] = total[b, rows, columns]

    def all_of(ref, send, recv):
        pieces = ref.at[: CHIPS - 1]
        return pltpu.make_async_remote_copy(pieces, pieces, send, recv, device(partner), MESH)

    def scan_states(b):
        all_of(got.at[b], send1.at[b], recv1.at[b]).wait_recv()
        if b == 0:
            all_of(got_closing, send2, recv2).wait_recv()
            chip_heads[:, :CHIPS] = jnp.exp(got_closing[:, 0, :]).T
        first = pl.multiple_of((b * batch + core * half) // HEAD + (chip // 8) * (quarter // HEAD), 8)
        decays = spread_heads(chip_heads[pl.ds(first, quarter // HEAD), :CHIPS], quarter)
        state = jnp.zeros((16, quarter), F32)
        for k in range(CHIPS):
            before[b, k] = state.astype(BF16)
            if k < CHIPS - 1:
                state = decays[k : k + 1, :] * state + got[b, k].astype(F32)

    def send_back(b):
        for d in range(1, CHIPS):
            back_copy(b, lax.rem(chip + d, CHIPS)).start()
        rows, columns = place(chip)
        entering[b, rows, columns] = before[b, chip]

    def take_back(b):
        all_of(before.at[b], send3.at[b], recv3.at[b]).wait_recv()
        for_first = entering[b]
        for_second = (pair_decays(b)[0:1, :] * for_first.astype(F32) + own_states(b)[0]).astype(BF16)
        theirs[b] = jnp.where(is_first, for_second, for_first)
        back_pair_copy(b).start()
        mine[b] = jnp.where(is_first, for_first, for_second)

    def finish_half(b, which, states):
        run(lambda j: finish_tile(half_tile(b, which, j), states[b, :, tile_columns(j)]), 0, half_tiles)

    def fresh_half(b, which):
        run(lambda j: fresh_tile(half_tile(b, which, j)), 0, half_tiles)

    cuts = sorted({0, batch, *(sum(outs[: k + 1]) for k in range(len(outs)))})
    stores = []
    for n, (start, stop) in enumerate(zip(cuts, cuts[1:])):
        k = sum(sum(outs[: i + 1]) <= start for i in range(len(outs)))
        at = start - sum(outs[:k])
        stores.append(
            pltpu.make_async_copy(
                out_ref.at[:, start:stop], out_refs[k].at[:, at : at + stop - start], out_sems.at[n]
            )
        )

    fresh_half(0, 1 - core)
    pl.semaphore_wait(barrier, CHIPS + 2)
    pair_copy(0).start()
    pass_on(0)
    closing_pair_copy.start()
    fresh_half(0, core)
    fresh_half(1, 1 - core)
    pair_copy(1).start()
    closing_pair_copy.wait()
    closing0 = jnp.where(is_first, closing[...], peer_closing[...])
    closing1 = jnp.where(is_first, peer_closing[...], closing[...])
    pair_heads[:, :16] = jnp.exp(jnp.concatenate([closing0, closing1], axis=0)).T
    total_closing[...] = closing0 + closing1
    got_closing[chip] = total_closing[...]
    pair_copy(0).wait()
    combine(0)
    send_states(0)
    fresh_half(1, core)
    pair_copy(1).wait()
    combine(1)
    send_states(1)
    if hops == 3:
        pass_on(1)
    scores[...] = jnp.where(row >= column, dot(maps_ref[:, STATE : 2 * STATE], write_flat[...]), 0.0)
    run(within_tile, 0, batch_tiles)
    scan_states(0)
    send_back(0)
    if hops == 2:
        pass_on(1)
    run(within_tile, batch_tiles, batch_tiles + half_tiles)
    scan_states(1)
    send_back(1)
    run(within_tile, batch_tiles + half_tiles, 2 * batch_tiles)
    if hops == 3:
        pass_on(2)
    take_back(0)
    finish_half(0, core, mine)
    back_pair_copy(0).wait()
    finish_half(0, 1 - core, landed)
    stores[0].start()
    take_back(1)
    finish_half(1, core, mine)
    back_pair_copy(1).wait()
    finish_half(1, 1 - core, landed)
    for store in stores[1:]:
        store.start()
    all_of(got_closing, send2, recv2).wait_send()
    for b in range(BATCHES):
        all_of(got.at[b], send1.at[b], recv1.at[b]).wait_send()
        all_of(before.at[b], send3.at[b], recv3.at[b]).wait_send()
    hop(hops - 1).wait_recv()
    last = pltpu.make_async_copy(relay_slots.at[hops - 1], relay_out, out_sems.at[len(outs) + 1])
    last.start()
    for k in range(hops):
        hop(k).wait_send()
    for store in stores + [last]:
        store.wait()


def group(pieces, xs, vec, maps, step, relay, hops, outs, collective_id):
    features = sum(pieces)
    heads = features // HEAD
    half, quarter = features // BATCHES // 2, features // BATCHES // 4
    corner = lambda i: (0, 0)
    dma = pltpu.SemaphoreType.DMA
    vmem = pltpu.VMEM
    return pl.pallas_call(
        functools.partial(group_kernel, pieces, hops, outs),
        out_shape=[jax.ShapeDtypeStruct((ROWS, columns), BF16) for columns in outs]
        + [jax.ShapeDtypeStruct(array.shape, array.dtype) for array in (relay,)],
        grid=(1,),
        in_specs=[
            pl.BlockSpec(memory_space=vmem if x.shape[1] == columns else pl.ANY) for x, columns in zip(xs, pieces)
        ]
        + [
            pl.BlockSpec((vec.shape[0], features), corner),
            pl.BlockSpec(maps.shape, corner),
            pl.BlockSpec((heads + 8, ROWS), corner),
        ]
        + [pl.BlockSpec(memory_space=vmem if hops == 2 else pl.ANY)] ,
        out_specs=[pl.BlockSpec(memory_space=pl.ANY)] * (len(outs) + 1),
        scratch_shapes=[
            vmem((hops,) + relay.shape, BF16),
            dma((hops,)),
            dma((hops,)),
            vmem((ROWS, features), BF16),
            dma((len(outs) + 2,)),
            vmem((ROWS, features), BF16),
            dma((len(pieces),)),
            vmem((heads, ROWS), F32),
            vmem((heads, ROWS), F32),
            vmem((heads, ROWS), F32),
            vmem((heads, 128), F32),
            vmem((HEADS, 128), F32),
            vmem((HEADS, 128), F32),
            vmem((8, HEADS), F32),
            vmem((ROWS, 128), F32),
            vmem((ROWS, ROWS), F32),
            vmem((STATE, ROWS), BF16),
            vmem((ROWS, features), BF16),
            vmem((ROWS, features), F32),
            vmem((STATE, features), BF16),
            vmem((BATCHES, STATE, half), BF16),
            vmem((8, HEADS), F32),
            vmem((BATCHES, STATE, half), BF16),
            vmem((8, HEADS), F32),
            vmem((BATCHES, CHIPS, 16, quarter), BF16),
            vmem((CHIPS, 8, HEADS), F32),
            vmem((BATCHES, CHIPS, 16, quarter), BF16),
            vmem((BATCHES, STATE, half), BF16),
            vmem((BATCHES, STATE, half), BF16),
            vmem((BATCHES, STATE, half), BF16),
            vmem((BATCHES, STATE, half), BF16),
            dma((2 * BATCHES + 1,)),
            dma((2 * BATCHES + 1,)),
            dma((BATCHES,)),
            dma((BATCHES,)),
            dma,
            dma,
            dma((BATCHES,)),
            dma((BATCHES,)),
        ],
        compiler_params=pltpu.CompilerParams(
            collective_id=collective_id, has_side_effects=True, vmem_limit_bytes=VMEM_LIMIT
        ),
        cost_estimate=pl.CostEstimate(
            flops=ROWS * features, bytes_accessed=ROWS * features, transcendentals=0
        ),
        name="group",
    )(*xs, vec, maps, step, relay)


def widen_kernel(blocks, *refs):
    parts, out, held, loads, stores = refs[:-4], refs[-4], refs[-3], refs[-2], refs[-1]
    start = out.shape[1] - sum(width for _, _, width in blocks)
    pairs = []
    at = 0
    for k, (part, begin, width) in enumerate(blocks):
        here = held.at[:, at : at + width]
        load = pltpu.make_async_copy(parts[part].at[:, begin : begin + width], here, loads.at[k])
        store = pltpu.make_async_copy(here, out.at[:, start + at : start + at + width], stores.at[k])
        pairs.append((load, store))
        at += width
    for load, _ in pairs:
        load.start()
    for load, store in pairs:
        load.wait()
        store.start()
    for _, store in pairs:
        store.wait()


def widen(parts, width):
    blocks = []
    for k, part in enumerate(parts):
        begin = 0
        while begin < part.shape[1]:
            size = min(1024, part.shape[1] - begin)
            blocks.append((k, begin, size))
            begin += size
    dma = pltpu.SemaphoreType.DMA((len(blocks),))
    return pl.pallas_call(
        functools.partial(widen_kernel, blocks),
        in_specs=[pl.BlockSpec(memory_space=pl.ANY)] * len(parts),
        out_specs=pl.BlockSpec(memory_space=pl.ANY),
        out_shape=jax.ShapeDtypeStruct((ROWS, width), BF16),
        scratch_shapes=[pltpu.VMEM((ROWS, sum(part.shape[1] for part in parts)), BF16), dma, dma],
        compiler_params=pltpu.CompilerParams(vmem_limit_bytes=VMEM_LIMIT),
        cost_estimate=pl.CostEstimate(flops=1, bytes_accessed=ROWS * width * 2, transcendentals=0),
        name="widen",
    )(*parts)


def moved(array, by):
    peers = lax.axis_size("pipe")
    return lax.ppermute(array, "pipe", [(i, (i + by) % peers) for i in range(peers)])


def shards(
    incoming, norm_gain, proj_state, proj_step, conv_weight, decay_rate, step_bias, skip_gain, out_gain
):
    x = incoming[0]
    features = x.shape[1]
    home, back, away = HEADS_HOME * HEAD, HEADS_BACK * HEAD, HEADS_AWAY * HEAD
    ahead, round_ = HEADS_AHEAD * HEAD, HEADS_ROUND * HEAD

    x_ahead = moved(x[:, home : home + ahead], 1)
    x_round = moved(x[:, features - round_ :], -1)
    maps, maps_away, step, step_away, vec, vec_away = project(
        x, proj_state[0], proj_step[0], norm_gain, conv_weight[0], out_gain, step_bias, decay_rate, skip_gain,
        away, 2,
    )
    step_away, maps_away, vec_away = moved(step_away, 1), moved(maps_away, 1), moved(vec_away, 1)

    rows, rows_back, x_round = group(
        (home,), (x,), vec, maps, step, x_round, 2, (home - back, back), 0
    )
    rows, x_ahead, step_away, maps_away, vec_away = lax.optimization_barrier(
        (rows, x_ahead, step_away, maps_away, vec_away)
    )
    rows_in = moved(rows, 1)

    rows_away, rows_back = group(
        (ahead, round_), (x_ahead, x_round), vec_away, maps_away, step_away,
        rows_back, 3, (away,), 1,
    )
    passed = widen((rows_back, rows_away), features)
    return lax.dynamic_update_slice(passed, rows_in, (0, 0))[None]


def solution(mesh):
    return jax.shard_map(
        shards,
        mesh=mesh,
        in_specs=(
            P("pipe", "ctx", None),
            P("pipe", None),
            P("pipe", None, None),
            P("pipe", None, None),
            P("pipe", None, None),
            P("pipe", None),
            P("pipe", None),
            P("pipe", None),
            P("pipe", None),
        ),
        out_specs=P("pipe", "ctx", None),
        check_vma=False,
    )
```
